32 devices in a mesh: ctx: 16 (over z, x, core), tp: 2 (over y).
Axes of the slice: x: 2, y: 2, z: 4, core: 2. Of those that a mesh axis runs over, the one named last changes fastest.
Arguments:
- query_vectors: bfloat16 [2048, 3072], P(('ctx', 'tp')), may hold values from -20 to 20
- key_vectors: bfloat16 [2048, 3072], P(('ctx', 'tp')), may hold values from -20 to 20
- value_vectors: bfloat16 [2048, 3072], P(('ctx', 'tp')), may hold values from -6 to 6
- out_weight: bfloat16 [3072, 5120], P('tp'), may hold values from -0.109375 to 0.109375
Outputs:
- mixed: bfloat16 [2048, 5120], P(('ctx', 'tp'))
The draws below stay inside these ranges and needn't reach their ends.
All inputs are finite; a program needn't handle non-finite values.
Results may differ from the reference program's by a relative error of at most 0.027.
Values may be sent and summed in bfloat16 or wider, within the bound.
No kernel may reach another device: no remote copies, remote signals or barrier semaphores. Data moves between devices by JAX's collectives and lax.ppermute only.
A program may use at most 64 MiB of HBM per device.

```python
import math
import jax
import jax.numpy as jnp
from jax import lax

D = 5120
HD = 128
HEADS = 24
TOKENS = 2048
N_TP = 2


def base_field(key):
    values = jax.random.normal(key, (TOKENS, HEADS * HD), jnp.float32)
    return jnp.clip(values, -6.0, 6.0) * 1.75


def draw_query_vectors(key, part):
    values = base_field(jax.random.fold_in(key, 1))
    return values.astype(jnp.bfloat16)


def draw_key_vectors(key, part):
    values = base_field(jax.random.fold_in(key, 2))
    return values.astype(jnp.bfloat16)


def level_of(stream_key, shape, shards, low, high):
    gain = 1.0
    for position, blocks in shards:
        heights = jax.random.uniform(jax.random.fold_in(jax.random.fold_in(stream_key, 6), position), (blocks,), jnp.float32, low / len(shards), high / len(shards))
        gain = gain * jnp.repeat(jnp.exp(heights), shape[position] // blocks).reshape((-1,) + (1,) * (len(shape) - 1 - position))
    return gain


def gaussian(own_key, shape, deviation, limit, cuts=(), dtype=jnp.bfloat16):
    gain = level_of(own_key, shape, cuts, -0.22, 0.18) if cuts else 1.0
    values = jax.random.normal(own_key, shape, jnp.float32) * deviation * gain
    return jnp.minimum(jnp.maximum(values, -limit), limit).astype(dtype)


def setup_inputs(seed: int = 0) -> dict:
    seeds = jax.random.split(jax.random.key(seed), 5)
    query_vectors = draw_query_vectors(jax.random.fold_in(seeds[4], 71), 0)
    key_vectors = draw_key_vectors(jax.random.fold_in(seeds[4], 71), 0)
    value_vectors = gaussian(seeds[2], (TOKENS, HEADS * HD), 1.0, 6.0, ((0, 32),))
    out_weight = gaussian(seeds[3], (HEADS * HD, D), (HEADS * HD) ** -0.5, 0.109375, ((0, 2),))
    return dict(query_vectors=query_vectors, key_vectors=key_vectors, value_vectors=value_vectors, out_weight=out_weight)


def reference(query_vectors, key_vectors, value_vectors, out_weight):
    score_scale = 1.0 / math.sqrt(HD)
    query_heads = query_vectors.astype(jnp.float32).reshape(TOKENS, HEADS, HD)
    key_heads = key_vectors.astype(jnp.float32).reshape(TOKENS, HEADS, HD)
    value_heads = value_vectors.astype(jnp.float32).reshape(TOKENS, HEADS, HD)
    block_rows = math.gcd(TOKENS, 128)
    block_count = TOKENS // block_rows

    def attend_block(query_block):
        scores = jnp.einsum('ihd,jhd->ihj', query_block, key_heads, precision=lax.Precision.HIGHEST) * score_scale
        row_peak = lax.optimization_barrier(jnp.max(scores, axis=-1))
        weights_low = jnp.exp(scores - row_peak[..., None]).astype(jnp.bfloat16)
        weights_wide = weights_low.astype(jnp.float32)
        row_total = lax.optimization_barrier(jnp.sum(weights_wide, axis=-1))
        weighted = jnp.einsum('ihj,jhd->ihd', weights_wide, value_heads, precision=lax.Precision.HIGHEST)
        return (weighted / row_total[..., None]).astype(jnp.bfloat16).reshape(block_rows, HEADS * HD)
    attended = lax.map(attend_block, query_heads.reshape(block_count, block_rows, HEADS, HD))
    attended = attended.reshape(TOKENS, HEADS * HD)
    group_cols = HEADS // N_TP * HD
    mixed = jnp.zeros((TOKENS, D), jnp.float32)
    for group in range(N_TP):
        partial_low = jnp.dot(attended[:, group * group_cols:(group + 1) * group_cols], out_weight[group * group_cols:(group + 1) * group_cols, :], preferred_element_type=jnp.float32).astype(jnp.bfloat16)
        partial_low = lax.optimization_barrier(partial_low)
        mixed = mixed + partial_low.astype(jnp.float32)
    return mixed.astype(jnp.bfloat16)
```

```python
import functools
import math

import jax
import jax.numpy as jnp
from jax import lax
from jax.experimental import pallas as pl
from jax.experimental.pallas import tpu as pltpu
from jax.sharding import PartitionSpec as P

HD = 128
AXES = ("ctx", "tp")
MIB = 1024 * 1024
F32 = jnp.float32
BF16 = jnp.bfloat16


class Plan:
    def __init__(self, head_count):
        self.C = lax.axis_size("ctx")
        self.T = lax.axis_size("tp")
        self.G = math.gcd(head_count // self.T, self.C)
        self.R = self.C // self.G
        self.heads = head_count // (self.T * self.G)
        self.cols = self.heads * HD
        ctx = lax.axis_index("ctx")
        self.g = ctx // self.R
        self.t = lax.axis_index("tp")

    def flat(self, g, r, t):
        return (g % self.G * self.R + r) * self.T + t % self.T

    def move(self, x, dg=0, dt=0, r_map=lambda r: r):
        pairs = [
            (self.flat(g, r, t), self.flat(g + dg, r_map(r), t + dt))
            for g in range(self.G)
            for r in range(self.R)
            for t in range(self.T)
        ]
        return lax.ppermute(x, AXES, pairs)


def pack_kernel(offset_ref, q_ref, k_ref, v_ref, *out_refs):
    cols = out_refs[0].shape[-1]
    for index, out_ref in enumerate(out_refs):
        start = pl.multiple_of(offset_ref[index], HD)
        for slot, in_ref in enumerate((q_ref, k_ref, v_ref)):
            out_ref[slot] = in_ref[:, pl.ds(start, cols)]


def pack(plan, offsets, q, k, v):
    rows = q.shape[0]
    count = plan.G * plan.T
    return pl.pallas_call(
        pack_kernel,
        out_shape=[jax.ShapeDtypeStruct((3, rows, plan.cols), BF16)] * count,
        in_specs=[pl.BlockSpec(memory_space=pltpu.SMEM)]
        + [pl.BlockSpec(memory_space=pltpu.VMEM)] * 3,
        out_specs=[pl.BlockSpec(memory_space=pltpu.VMEM)] * count,
        compiler_params=pltpu.CompilerParams(vmem_limit_bytes=32 * MIB),
        name="pack_heads",
    )(offsets, q, k, v)


def attend_kernel(tile, q_ref, *refs):
    kv_refs, out_ref, scores = refs[:-2], refs[-2], refs[-1]
    scale = math.log2(math.e) / math.sqrt(HD)
    for first in range(0, q_ref.shape[0], tile):
        rows = pl.ds(first, tile)
        q = q_ref[rows, :]
        peak = None
        at = 0
        for kv_ref in kv_refs:
            count = kv_ref.shape[1]
            part = lax.dot_general(
                q, kv_ref[0], (((1,), (1,)), ((), ())), preferred_element_type=F32
            )
            scores[rows, pl.ds(at, count)] = part
            top = jnp.max(part, axis=-1, keepdims=True)
            peak = top if peak is None else jnp.maximum(peak, top)
            at += count
        peak = peak * scale
        weighted = jnp.zeros((tile, HD), F32)
        total = jnp.zeros((tile, 1), F32)
        at = 0
        for kv_ref in kv_refs:
            count = kv_ref.shape[1]
            probs = jnp.exp2(scores[rows, pl.ds(at, count)] * scale - peak).astype(BF16)
            total += jnp.sum(probs.astype(F32), axis=-1, keepdims=True)
            weighted += jnp.dot(probs, kv_ref[1], preferred_element_type=F32)
            at += count
        out_ref[rows, :] = (weighted / total).astype(BF16)


def attend(plan, q, kvs):
    rows = q.shape[0]
    keys = sum(kv.shape[1] for kv in kvs)
    return pl.pallas_call(
        functools.partial(attend_kernel, math.gcd(rows, 256)),
        out_shape=jax.ShapeDtypeStruct((rows, plan.cols), BF16),
        grid=(plan.heads,),
        in_specs=[pl.BlockSpec((rows, HD), lambda h: (0, h))]
        + [pl.BlockSpec((2, kv.shape[1], HD), lambda h: (0, 0, h)) for kv in kvs],
        out_specs=pl.BlockSpec((rows, HD), lambda h: (0, h)),
        scratch_shapes=[pltpu.VMEM((rows, keys), F32)],
        compiler_params=pltpu.CompilerParams(vmem_limit_bytes=48 * MIB),
        cost_estimate=pl.CostEstimate(
            flops=4 * rows * keys * plan.cols,
            bytes_accessed=2 * plan.cols * (2 * rows + 2 * keys),
            transcendentals=rows * keys * plan.heads,
        ),
        name="attend",
    )(q, *kvs)


def project_kernel(group_count, group_ref, *refs):
    parts, w_ref, outs, mixed = refs[:group_count], refs[group_count], refs[group_count + 1 : -1], refs[-1]
    cols = parts[0].shape[1]

    @pl.when(pl.program_id(0) == 0)
    def _():
        for shift, part in enumerate(parts):
            place = lax.rem(group_ref[0] + shift, group_count) * cols
            mixed[:, pl.ds(pl.multiple_of(place, HD), cols)] = part[...]

    share = jnp.dot(mixed[...], w_ref[...], preferred_element_type=F32).astype(BF16)
    rows = outs[0].shape[0]
    for index, out in enumerate(outs):
        out[...] = share[index * rows : (index + 1) * rows]


def project(plan, group, parts, w, first, count, tile):
    rows = parts[0].shape[0]
    depth = w.shape[0]
    own = rows // plan.T
    return pl.pallas_call(
        functools.partial(project_kernel, len(parts)),
        out_shape=[jax.ShapeDtypeStruct((own, count), BF16)] * plan.T,
        grid=(count // tile,),
        in_specs=[pl.BlockSpec(memory_space=pltpu.SMEM)]
        + [pl.BlockSpec(part.shape, lambda j: (0, 0)) for part in parts]
        + [pl.BlockSpec((depth, tile), lambda j: (0, first // tile + j))],
        out_specs=[pl.BlockSpec((own, tile), lambda j: (0, j))] * plan.T,
        scratch_shapes=[pltpu.VMEM((rows, depth), BF16)],
        compiler_params=pltpu.CompilerParams(vmem_limit_bytes=32 * MIB),
        cost_estimate=pl.CostEstimate(
            flops=2 * rows * depth * count,
            bytes_accessed=2 * depth * count,
            transcendentals=0,
        ),
        name="project",
    )(group, *parts, w)


def local(query_vectors, key_vectors, value_vectors, out_weight):
    plan = Plan(query_vectors.shape[1] // HD)
    G, R, T = plan.G, plan.R, plan.T
    rows = query_vectors.shape[0]
    shifts = [(dg, dt) for dg in range(G) for dt in range(T)]

    offsets = jnp.stack(
        [((plan.t + dt) % T * G + (plan.g + dg) % G) * plan.cols for dg, dt in shifts]
    ).astype(jnp.int32)
    packed = pack(plan, offsets, query_vectors, key_vectors, value_vectors)
    arrived = [
        block if (dg, dt) == (0, 0) else plan.move(block, dg, dt)
        for (dg, dt), block in zip(shifts, packed)
    ]
    gathered = jnp.concatenate(arrived, axis=1)
    queries, own_kv = gathered[0], gathered[1:]

    if R % 2 == 0 and R <= 8:
        kvs = [own_kv] + [
            plan.move(own_kv, r_map=lambda r, s=s: (r + 2 * s) % R) for s in range(1, R // 2)
        ]
        kvs = kvs + [plan.move(kv, r_map=lambda r: r ^ 1) for kv in kvs]
    else:
        groups = [[g * R + r for r in range(R)] for g in range(G)]
        kvs = [lax.all_gather(own_kv, "ctx", axis=1, tiled=True, axis_index_groups=groups)]

    attended = attend(plan, queries, kvs)
    blocks = [attended[dg * T * rows : (dg + 1) * T * rows] for dg in range(G)]
    parts = [blocks[0]] + [plan.move(blocks[dg], -dg) for dg in range(1, G)]

    group = jnp.reshape(plan.g, (1,)).astype(jnp.int32)
    width = out_weight.shape[1]
    chunk = width // 4
    outs = []
    for first in range(0, width, chunk):
        shares = project(plan, group, parts, out_weight, first, chunk, math.gcd(chunk, 256))
        total = shares[0].astype(F32)
        for dt in range(1, T):
            total = total + plan.move(shares[dt], 0, -dt).astype(F32)
        outs.append(total.astype(BF16))
    return jnp.concatenate(outs, axis=1)


def solution(mesh):
    spec = P(AXES, None)
    return jax.shard_map(
        local,
        mesh=mesh,
        in_specs=(spec, spec, spec, P("tp", None)),
        out_specs=spec,
        check_vma=False,
    )
```

```python
import functools
import math

import jax
import jax.numpy as jnp
from jax import lax
from jax.experimental import pallas as pl
from jax.experimental.pallas import tpu as pltpu
from jax.sharding import PartitionSpec as P

HD = 128
AXES = ("ctx", "tp")
MIB = 1024 * 1024
F32 = jnp.float32
BF16 = jnp.bfloat16


class Plan:
    def __init__(self, head_count):
        self.C = lax.axis_size("ctx")
        self.T = lax.axis_size("tp")
        self.G = math.gcd(head_count // self.T, self.C)
        self.R = self.C // self.G
        self.heads = head_count // (self.T * self.G)
        self.cols = self.heads * HD

    def flat(self, g, r, t):
        return (g % self.G * self.R + r) * self.T + t % self.T

    def move(self, x, dg=0, dt=0, r_map=lambda r: r):
        pairs = [
            (self.flat(g, r, t), self.flat(g + dg, r_map(r), t + dt))
            for g in range(self.G)
            for r in range(self.R)
            for t in range(self.T)
        ]
        return lax.ppermute(x, AXES, pairs)

    def spread(self, x):
        groups = [
            [self.flat(g, r, t) for g in range(self.G) for t in range(self.T)]
            for r in range(self.R)
        ]
        return lax.all_to_all(x, AXES, 0, 0, axis_index_groups=groups, tiled=True)

    def collect(self, x):
        if self.G == 1:
            return x
        groups = [[g * self.R + r for g in range(self.G)] for r in range(self.R)]
        return lax.all_to_all(x, "ctx", 0, 0, axis_index_groups=groups, tiled=True)


def pack_kernel(G, T, in_ref, out_ref, sem):
    rows = in_ref.shape[0]
    cols = in_ref.shape[1] // (G * T)
    copies = [
        pltpu.make_async_copy(
            in_ref.at[:, pl.ds((t * G + g) * cols, cols)],
            out_ref.at[pl.ds((g * T + t) * rows, rows), :],
            sem.at[g * T + t],
        )
        for g in range(G)
        for t in range(T)
    ]
    for copy in copies:
        copy.start()
    for copy in copies:
        copy.wait()


def pack(plan, x, name):
    rows = x.shape[0]
    count = plan.G * plan.T
    return pl.pallas_call(
        functools.partial(pack_kernel, plan.G, plan.T),
        out_shape=jax.ShapeDtypeStruct((count * rows, plan.cols), BF16),
        in_specs=[pl.BlockSpec(memory_space=pl.ANY)],
        out_specs=pl.BlockSpec(memory_space=pltpu.VMEM),
        scratch_shapes=[pltpu.SemaphoreType.DMA((count,))],
        compiler_params=pltpu.CompilerParams(vmem_limit_bytes=8 * MIB),
        name=name,
    )(x)


def attend_kernel(tile, piece_count, q_ref, *refs):
    k_refs, v_refs = refs[:piece_count], refs[piece_count : 2 * piece_count]
    out_ref, scores = refs[-2], refs[-1]
    scale = math.log2(math.e) / math.sqrt(HD)
    for first in range(0, q_ref.shape[0], tile):
        rows = pl.ds(first, tile)
        q = q_ref[rows, :]
        peak = None
        at = 0
        for k_ref in k_refs:
            count = k_ref.shape[0]
            part = lax.dot_general(
                q, k_ref[...], (((1,), (1,)), ((), ())), preferred_element_type=F32
            )
            scores[rows, pl.ds(at, count)] = part
            top = jnp.max(part, axis=-1, keepdims=True)
            peak = top if peak is None else jnp.maximum(peak, top)
            at += count
        peak = peak * scale
        weighted = jnp.zeros((tile, HD), F32)
        total = jnp.zeros((tile, 1), F32)
        at = 0
        for v_ref in v_refs:
            count = v_ref.shape[0]
            probs = jnp.exp2(scores[rows, pl.ds(at, count)] * scale - peak).astype(BF16)
            total += jnp.sum(probs.astype(F32), axis=-1, keepdims=True)
            weighted += jnp.dot(probs, v_ref[...], preferred_element_type=F32)
            at += count
        out_ref[rows, :] = (weighted / total).astype(BF16)


def attend(plan, q, ks, vs):
    rows = q.shape[0]
    keys = sum(k.shape[0] for k in ks)
    return pl.pallas_call(
        functools.partial(attend_kernel, math.gcd(rows, 256), len(ks)),
        out_shape=jax.ShapeDtypeStruct((rows, plan.cols), BF16),
        grid=(plan.heads,),
        in_specs=[pl.BlockSpec((x.shape[0], HD), lambda h: (0, h)) for x in (q, *ks, *vs)],
        out_specs=pl.BlockSpec((rows, HD), lambda h: (0, h)),
        scratch_shapes=[pltpu.VMEM((rows, keys), F32)],
        compiler_params=pltpu.CompilerParams(
            vmem_limit_bytes=8 * MIB + 4 * rows * keys + 8 * HD * (rows + 2 * keys)
        ),
        cost_estimate=pl.CostEstimate(
            flops=4 * rows * keys * plan.cols,
            bytes_accessed=2 * plan.cols * (2 * rows + 2 * keys),
            transcendentals=rows * keys * plan.heads,
        ),
        name="attend",
    )(q, *ks, *vs)


def fetch_kernel(pieces, w_ref, out_ref, sem):
    depth = w_ref.shape[0] // pieces
    copies = [
        pltpu.make_async_copy(
            w_ref.at[pl.ds(i * depth, depth), :], out_ref.at[pl.ds(i * depth, depth), :], sem.at[i]
        )
        for i in range(pieces)
    ]
    for copy in copies:
        copy.start()
    for copy in copies:
        copy.wait()


def fetch(w):
    size = 2 * w.shape[0] * w.shape[1]
    return pl.pallas_call(
        functools.partial(fetch_kernel, 8),
        out_shape=jax.ShapeDtypeStruct(w.shape, w.dtype),
        in_specs=[pl.BlockSpec(memory_space=pltpu.HBM)],
        out_specs=pl.BlockSpec(memory_space=pltpu.VMEM),
        scratch_shapes=[pltpu.SemaphoreType.DMA((8,))],
        compiler_params=pltpu.CompilerParams(vmem_limit_bytes=32 * MIB),
        cost_estimate=pl.CostEstimate(flops=0, bytes_accessed=2 * size, transcendentals=0),
        name="fetch_weight",
    )(w)


def project_kernel(G, T, first, own_ref, part_ref, w_ref, *refs):
    outs, mixed, share = refs[:-2], refs[-2], refs[-1]
    cols = part_ref.shape[1]
    block = part_ref.shape[0] // G
    rows = block // T

    for g in range(G):
        mixed[:, g * cols : (g + 1) * cols] = part_ref[g * block : (g + 1) * block, :]

    count = outs[0].shape[1]
    share[...] = jnp.dot(
        mixed[...], w_ref[:, first : first + count], preferred_element_type=F32
    ).astype(BF16)
    for shift, out in enumerate(outs):
        start = lax.rem(own_ref[0] + T - shift, T) * rows
        out[...] = share[pl.ds(pl.multiple_of(start, rows), rows), :]


def project(plan, own, parts, w, first, count):
    depth = w.shape[0]
    block = parts.shape[0] // plan.G
    rows = block // plan.T
    return pl.pallas_call(
        functools.partial(project_kernel, plan.G, plan.T, first),
        out_shape=[jax.ShapeDtypeStruct((rows, count), BF16)] * plan.T,
        in_specs=[
            pl.BlockSpec(memory_space=pltpu.SMEM),
            pl.BlockSpec(memory_space=pltpu.VMEM),
            pl.BlockSpec(memory_space=pltpu.VMEM),
        ],
        out_specs=[pl.BlockSpec(memory_space=pltpu.VMEM)] * plan.T,
        scratch_shapes=[pltpu.VMEM((block, depth), BF16), pltpu.VMEM((block, count), BF16)],
        compiler_params=pltpu.CompilerParams(vmem_limit_bytes=20 * MIB),
        cost_estimate=pl.CostEstimate(
            flops=2 * block * depth * count,
            bytes_accessed=2 * depth * count,
            transcendentals=0,
        ),
        name="project",
    )(own, parts, w)


def local(query_vectors, key_vectors, value_vectors, out_weight):
    plan = Plan(query_vectors.shape[1] // HD)
    G, R, T = plan.G, plan.R, plan.T
    weight = fetch(out_weight)

    def widen(own):
        if R % 2 == 0 and R <= 8:
            pieces = [own] + [
                plan.move(own, r_map=lambda r, s=s: (r + 2 * s) % R) for s in range(1, R // 2)
            ]
            return pieces + [plan.move(piece, r_map=lambda r: r ^ 1) for piece in pieces]
        groups = [[g * R + r for r in range(R)] for g in range(G)]
        return [lax.all_gather(own, "ctx", axis=0, tiled=True, axis_index_groups=groups)]

    ks = widen(plan.spread(pack(plan, key_vectors, "pack_keys")))
    vs = widen(plan.spread(pack(plan, value_vectors, "pack_values")))
    queries = plan.spread(pack(plan, query_vectors, "pack_queries"))
    attended = attend(plan, queries, ks, vs)
    parts = plan.collect(attended)

    own = jnp.reshape(lax.axis_index("tp"), (1,)).astype(jnp.int32)
    width = out_weight.shape[1]
    chunk = width // 4
    outs = []
    for first in range(0, width, chunk):
        shares = project(plan, own, parts, weight, first, chunk)
        total = shares[0].astype(F32)
        for dt in range(1, T):
            total = total + plan.move(shares[dt], 0, -dt).astype(F32)
        outs.append(total.astype(BF16))
    return jnp.concatenate(outs, axis=1)


def solution(mesh):
    spec = P(AXES, None)
    return jax.shard_map(
        local,
        mesh=mesh,
        in_specs=(spec, spec, spec, P("tp", None)),
        out_specs=spec,
        check_vma=False,
    )
```

```python
import functools
import math

import jax
import jax.numpy as jnp
from jax import lax
from jax.experimental import pallas as pl
from jax.experimental.pallas import tpu as pltpu
from jax.sharding import PartitionSpec as P

HD = 128
AXES = ("ctx", "tp")
MIB = 1024 * 1024
F32 = jnp.float32
BF16 = jnp.bfloat16


class Plan:
    def __init__(self, head_count):
        self.C = lax.axis_size("ctx")
        self.T = lax.axis_size("tp")
        self.G = math.gcd(head_count // self.T, self.C)
        self.R = self.C // self.G
        self.heads = head_count // (self.T * self.G)
        self.cols = self.heads * HD
        self.g = lax.axis_index("ctx") // self.R
        self.t = lax.axis_index("tp")

    def flat(self, g, r, t):
        return (g % self.G * self.R + r) * self.T + t % self.T

    def move(self, x, dg=0, dt=0, r_map=lambda r: r):
        pairs = [
            (self.flat(g, r, t), self.flat(g + dg, r_map(r), t + dt))
            for g in range(self.G)
            for r in range(self.R)
            for t in range(self.T)
        ]
        return lax.ppermute(x, AXES, pairs)


def pack_kernel(in_count, offset_ref, *refs):
    in_refs, out_refs, sem = refs[:in_count], refs[in_count:-1], refs[-1]
    cols = out_refs[0].shape[-1]
    copies = []
    for index, out_ref in enumerate(out_refs):
        start = pl.multiple_of(offset_ref[index], HD)
        for slot, in_ref in enumerate(in_refs):
            copies.append(
                pltpu.make_async_copy(
                    in_ref.at[:, pl.ds(start, cols)], out_ref.at[slot], sem.at[len(copies)]
                )
            )
            copies[-1].start()
    for copy in copies:
        copy.wait()


def pack(plan, offsets, arrays, name):
    rows = arrays[0].shape[0]
    count = offsets.shape[0]
    return pl.pallas_call(
        functools.partial(pack_kernel, len(arrays)),
        out_shape=[jax.ShapeDtypeStruct((len(arrays), rows, plan.cols), BF16)] * count,
        in_specs=[pl.BlockSpec(memory_space=pltpu.SMEM)]
        + [pl.BlockSpec(memory_space=pl.ANY)] * len(arrays),
        out_specs=[pl.BlockSpec(memory_space=pl.ANY)] * count,
        scratch_shapes=[pltpu.SemaphoreType.DMA((count * len(arrays),))],
        compiler_params=pltpu.CompilerParams(vmem_limit_bytes=62 * MIB),
        name=name,
    )(offsets, *arrays)


def attend_kernel(tile, q_ref, *refs):
    kv_refs, out_ref, scores = refs[:-2], refs[-2], refs[-1]
    scale = math.log2(math.e) / math.sqrt(HD)
    for first in range(0, q_ref.shape[0], tile):
        rows = pl.ds(first, tile)
        q = q_ref[rows, :]
        peak = None
        at = 0
        for kv_ref in kv_refs:
            count = kv_ref.shape[1]
            part = lax.dot_general(
                q, kv_ref[0], (((1,), (1,)), ((), ())), preferred_element_type=F32
            )
            scores[rows, pl.ds(at, count)] = part
            top = jnp.max(part, axis=-1, keepdims=True)
            peak = top if peak is None else jnp.maximum(peak, top)
            at += count
        peak = peak * scale
        weighted = jnp.zeros((tile, HD), F32)
        total = jnp.zeros((tile, 1), F32)
        at = 0
        for kv_ref in kv_refs:
            count = kv_ref.shape[1]
            probs = jnp.exp2(scores[rows, pl.ds(at, count)] * scale - peak).astype(BF16)
            total += jnp.sum(probs.astype(F32), axis=-1, keepdims=True)
            weighted += jnp.dot(probs, kv_ref[1], preferred_element_type=F32)
            at += count
        out_ref[rows, :] = (weighted / total).astype(BF16)


def attend(plan, q, kvs, name):
    rows = q.shape[0]
    keys = sum(kv.shape[1] for kv in kvs)
    return pl.pallas_call(
        functools.partial(attend_kernel, math.gcd(rows, 256)),
        out_shape=jax.ShapeDtypeStruct((rows, plan.cols), BF16),
        grid=(plan.heads,),
        in_specs=[pl.BlockSpec((rows, HD), lambda h: (0, h))]
        + [pl.BlockSpec((2, kv.shape[1], HD), lambda h: (0, 0, h)) for kv in kvs],
        out_specs=pl.BlockSpec((rows, HD), lambda h: (0, h)),
        scratch_shapes=[pltpu.VMEM((rows, keys), F32)],
        compiler_params=pltpu.CompilerParams(
            vmem_limit_bytes=8 * MIB + 4 * rows * keys + 8 * HD * (rows + 2 * keys)
        ),
        cost_estimate=pl.CostEstimate(
            flops=4 * rows * keys * plan.cols,
            bytes_accessed=2 * plan.cols * (2 * rows + 2 * keys),
            transcendentals=rows * keys * plan.heads,
        ),
        name=name,
    )(q, *kvs)


def project_kernel(group_count, first, tile, group_ref, *refs):
    parts, w_ref, out_ref = refs[:group_count], refs[group_count], refs[group_count + 1]
    mixed, held, sem = refs[group_count + 2 :]
    cols = parts[0].shape[1]
    count = out_ref.shape[1]
    copies = []
    for index, at in enumerate(range(0, count, tile)):
        copies.append(
            pltpu.make_async_copy(
                w_ref.at[:, pl.ds(first + at, tile)], held.at[index], sem.at[index]
            )
        )
        copies[-1].start()
    for shift, part in enumerate(parts):
        place = lax.rem(group_ref[0] + shift, group_count) * cols
        mixed[:, pl.ds(pl.multiple_of(place, HD), cols)] = part[...]
    for index, at in enumerate(range(0, count, tile)):
        copies[index].wait()
        out_ref[:, at : at + tile] = jnp.dot(
            mixed[...], held[index], preferred_element_type=F32
        ).astype(BF16)


def project(plan, group, parts, w, first, count, name):
    rows = parts[0].shape[0]
    depth = w.shape[0]
    tile = math.gcd(count, 256)
    return pl.pallas_call(
        functools.partial(project_kernel, len(parts), first, tile),
        out_shape=jax.ShapeDtypeStruct((rows, count), BF16),
        in_specs=[pl.BlockSpec(memory_space=pltpu.SMEM)]
        + [pl.BlockSpec(memory_space=pltpu.VMEM)] * len(parts)
        + [pl.BlockSpec(memory_space=pl.ANY)],
        out_specs=pl.BlockSpec(memory_space=pltpu.VMEM),
        scratch_shapes=[
            pltpu.VMEM((rows, depth), BF16),
            pltpu.VMEM((count // tile, depth, tile), BF16),
            pltpu.SemaphoreType.DMA((count // tile,)),
        ],
        compiler_params=pltpu.CompilerParams(vmem_limit_bytes=52 * MIB),
        cost_estimate=pl.CostEstimate(
            flops=2 * rows * depth * count,
            bytes_accessed=2 * depth * count,
            transcendentals=0,
        ),
        name=name,
    )(group, *parts, w)


def local(query_vectors, key_vectors, value_vectors, out_weight):
    plan = Plan(query_vectors.shape[1] // HD)
    G, R, T = plan.G, plan.R, plan.T
    rows = query_vectors.shape[0]

    def offsets(shifts):
        return jnp.stack(
            [((plan.t + dt) % T * G + (plan.g + dg) % G) * plan.cols for dg, dt in shifts]
        ).astype(jnp.int32)

    def spread(shifts, blocks):
        return [
            block if shift == (0, 0) else plan.move(block, *shift)
            for shift, block in zip(shifts, blocks)
        ]

    shifts = [(dg, dt) for dg in range(G) for dt in range(T)]
    blocks = pack(plan, offsets(shifts), [key_vectors, value_vectors], "pack_kv")
    arrived = spread(shifts, blocks)
    half = max(G // 2, 1) * T
    wide = R % 2 == 0 and R <= 8
    owns = [
        jnp.concatenate(arrived[first : first + half], axis=1)
        for first in range(0, len(shifts), half)
    ]
    nears = [
        [own]
        + [
            plan.move(own, r_map=lambda r, s=s: (r + 2 * s) % R)
            for s in range(1, R // 2 if wide else 1)
        ]
        for own in owns
    ]

    shifts = [(dg, dt) for dg in range(G) for dt in range(1, T)] + [(dg, 0) for dg in range(G)]
    blocks = pack(plan, offsets(shifts), [query_vectors], "pack_q")
    others = G * (T - 1)
    asked = spread(shifts[:others], blocks[:others])
    nears, asked, kept = lax.optimization_barrier((nears, asked, blocks[others:]))
    kept = spread(shifts[others:], kept)

    kvs = []
    for near in nears:
        near = jnp.concatenate(near, axis=1)
        if wide:
            kvs += [near, plan.move(near, r_map=lambda r: r ^ 1)]
        else:
            groups = [[g * R + r for r in range(R)] for g in range(G)]
            kvs.append(lax.all_gather(near, "ctx", axis=1, tiled=True, axis_index_groups=groups))

    group = jnp.reshape(plan.g, (1,)).astype(jnp.int32)
    width = out_weight.shape[1]
    chunk = width // 4

    def shares(queries, name):
        count = len(queries) // G * rows
        q = jnp.concatenate(queries, axis=1)[0]
        attended = attend(plan, q, kvs, "attend_" + name)
        attended = [attended[dg * count : (dg + 1) * count] for dg in range(G)]
        parts = [attended[0]] + [plan.move(attended[dg], -dg) for dg in range(1, G)]
        return [
            project(plan, group, parts, out_weight, first, chunk, "project_" + name)
            for first in range(0, width, chunk)
        ]

    sent = shares(asked, "others")
    received = [
        [
            plan.move(share[(dt - 1) * rows : dt * rows], 0, -dt)
            for dt in range(1, T)
        ]
        for share in sent
    ]
    kept = shares(kept, "own")
    outs = []
    for own, pieces in zip(kept, received):
        total = own.astype(F32)
        for piece in pieces:
            total = total + piece.astype(F32)
        outs.append(total.astype(BF16))
    return jnp.concatenate(outs, axis=1)


def solution(mesh):
    spec = P(AXES, None)
    return jax.shard_map(
        local,
        mesh=mesh,
        in_specs=(spec, spec, spec, P("tp", None)),
        out_specs=spec,
        check_vma=False,
    )
```

```python
import functools
import math

import jax
import jax.numpy as jnp
from jax import lax
from jax.experimental import pallas as pl
from jax.experimental.pallas import tpu as pltpu
from jax.sharding import PartitionSpec as P

HD = 128
AXES = ("ctx", "tp")
MIB = 1024 * 1024
F32 = jnp.float32
BF16 = jnp.bfloat16


class Plan:
    def __init__(self, head_count):
        self.C = lax.axis_size("ctx")
        self.T = lax.axis_size("tp")
        self.G = math.gcd(head_count // self.T, self.C)
        self.R = self.C // self.G
        self.heads = head_count // (self.T * self.G)
        self.cols = self.heads * HD
        self.where = jnp.reshape(lax.axis_index(AXES), (1,)).astype(jnp.int32)

    def flat(self, g, r, t):
        return (g % self.G * self.R + r) * self.T + t % self.T

    def move(self, x, dg=0, dt=0, r_map=lambda r: r):
        pairs = [
            (self.flat(g, r, t), self.flat(g + dg, r_map(r), t + dt))
            for g in range(self.G)
            for r in range(self.R)
            for t in range(self.T)
        ]
        return lax.ppermute(x, AXES, pairs)


def pack_kernel(starts_of, where_ref, *refs):
    in_count, out_count, starts = starts_of
    in_refs, out_refs = refs[:in_count], refs[in_count : in_count + out_count]
    held, in_sem, out_sem = refs[in_count + out_count :]
    cols = out_refs[0].shape[-1]
    inward, outward = [], []
    for index, start in enumerate(starts(where_ref[0])):
        if not isinstance(start, int):
            start = pl.multiple_of(start, HD)
        for slot, in_ref in enumerate(in_refs):
            inward.append(
                pltpu.make_async_copy(
                    in_ref.at[:, pl.ds(start, cols)],
                    held.at[index, slot],
                    in_sem.at[index * in_count + slot],
                )
            )
            inward[-1].start()
    blocks = held.shape[0] // out_count
    for index, out_ref in enumerate(out_refs):
        first = index * blocks
        for copy in inward[first * in_count : (first + blocks) * in_count]:
            copy.wait()
        outward.append(
            pltpu.make_async_copy(
                held.at[index] if blocks == 1 else held, out_ref, out_sem.at[index]
            )
        )
        outward[-1].start()
    for copy in outward:
        copy.wait()


def pack(plan, starts, count, arrays, split, name):
    rows = arrays[0].shape[0]
    block = (len(arrays), rows, plan.cols)
    outs = count if split else 1
    return pl.pallas_call(
        functools.partial(pack_kernel, (len(arrays), outs, starts)),
        out_shape=[jax.ShapeDtypeStruct(block if split else (count, *block), BF16)] * outs,
        in_specs=[pl.BlockSpec(memory_space=pltpu.SMEM)]
        + [pl.BlockSpec(memory_space=pl.ANY)] * len(arrays),
        out_specs=[pl.BlockSpec(memory_space=pl.ANY)] * outs,
        scratch_shapes=[
            pltpu.VMEM((count, *block), BF16),
            pltpu.SemaphoreType.DMA((count * len(arrays),)),
            pltpu.SemaphoreType.DMA((outs,)),
        ],
        compiler_params=pltpu.CompilerParams(vmem_limit_bytes=60 * MIB),
        name=name,
    )(plan.where, *arrays)


def attend_kernel(G, T, rows, first, where_ref, q_ref, *refs):
    kv_refs, out_ref, scores = refs[:-2], refs[-2], refs[-1]
    scale = math.log2(math.e) / math.sqrt(HD)
    own = lax.rem(where_ref[0], T)
    per_group = out_ref.shape[0] // (G * rows)
    tile_groups = math.gcd(G, max(256 // (per_group * rows), 1))
    tile = tile_groups * per_group * rows
    for at in range(0, G, tile_groups):
        pieces = []
        for g in range(at, at + tile_groups):
            for dt in range(first, first + per_group):
                block = g * T + lax.rem(own + dt, T)
                pieces.append(q_ref[pl.ds(pl.multiple_of(block * rows, rows), rows), :])
        q = jnp.concatenate(pieces, axis=0)
        place = pl.ds(at * per_group * rows, tile)
        peak = None
        key = 0
        for kv_ref in kv_refs:
            count = kv_ref.shape[1]
            part = lax.dot_general(
                q, kv_ref[0], (((1,), (1,)), ((), ())), preferred_element_type=F32
            )
            scores[place, pl.ds(key, count)] = part
            top = jnp.max(part, axis=-1, keepdims=True)
            peak = top if peak is None else jnp.maximum(peak, top)
            key += count
        peak = peak * scale
        weighted = jnp.zeros((tile, HD), F32)
        total = jnp.zeros((tile, 1), F32)
        key = 0
        for kv_ref in kv_refs:
            count = kv_ref.shape[1]
            probs = jnp.exp2(scores[place, pl.ds(key, count)] * scale - peak).astype(BF16)
            total += jnp.sum(probs.astype(F32), axis=-1, keepdims=True)
            weighted += jnp.dot(probs, kv_ref[1], preferred_element_type=F32)
            key += count
        out_ref[place, :] = (weighted / total).astype(BF16)


def attend(plan, q, kvs, first, count, name):
    rows = q.shape[0] // (plan.G * plan.T)
    asked = plan.G * count * rows
    keys = sum(kv.shape[1] for kv in kvs)
    return pl.pallas_call(
        functools.partial(attend_kernel, plan.G, plan.T, rows, first),
        out_shape=jax.ShapeDtypeStruct((asked, plan.cols), BF16),
        grid=(plan.heads,),
        in_specs=[
            pl.BlockSpec(memory_space=pltpu.SMEM),
            pl.BlockSpec((q.shape[0], HD), lambda h: (0, h)),
        ]
        + [pl.BlockSpec((2, kv.shape[1], HD), lambda h: (0, 0, h)) for kv in kvs],
        out_specs=pl.BlockSpec((asked, HD), lambda h: (0, h)),
        scratch_shapes=[pltpu.VMEM((asked, keys), F32)],
        compiler_params=pltpu.CompilerParams(
            vmem_limit_bytes=8 * MIB + 4 * asked * keys + 8 * HD * (asked + 2 * keys)
        ),
        cost_estimate=pl.CostEstimate(
            flops=4 * asked * keys * plan.cols,
            bytes_accessed=2 * plan.cols * (2 * asked + 2 * keys),
            transcendentals=asked * keys * plan.heads,
        ),
        name=name,
    )(plan.where, q, *kvs)


def project_kernel(G, first, part_ref, w_ref, out_ref, mixed, held, sem):
    count = out_ref.shape[1]
    pieces, depth = held.shape[0], held.shape[1]
    copies = []
    for index in range(pieces):
        copies.append(
            pltpu.make_async_copy(
                w_ref.at[pl.ds(index * depth, depth), pl.ds(first, count)],
                held.at[index],
                sem.at[index],
            )
        )
        copies[-1].start()
    rows, cols = part_ref.shape[0] // G, part_ref.shape[1]
    for g in range(G):
        mixed[:, g * cols : (g + 1) * cols] = part_ref[g * rows : (g + 1) * rows, :]
    total = None
    for index in range(pieces):
        copies[index].wait()
        share = jnp.dot(
            mixed[:, index * depth : (index + 1) * depth],
            held[index],
            preferred_element_type=F32,
        )
        total = share if total is None else total + share
    out_ref[...] = total.astype(BF16)


def project(plan, parts, w, first, count, name):
    rows = parts.shape[0] // plan.G
    depth = w.shape[0]
    piece = math.gcd(depth, 512)
    return pl.pallas_call(
        functools.partial(project_kernel, plan.G, first),
        out_shape=jax.ShapeDtypeStruct((rows, count), BF16),
        in_specs=[pl.BlockSpec(memory_space=pltpu.VMEM), pl.BlockSpec(memory_space=pl.ANY)],
        out_specs=pl.BlockSpec(memory_space=pltpu.VMEM),
        scratch_shapes=[
            pltpu.VMEM((rows, depth), BF16),
            pltpu.VMEM((depth // piece, piece, count), BF16),
            pltpu.SemaphoreType.DMA((depth // piece,)),
        ],
        compiler_params=pltpu.CompilerParams(vmem_limit_bytes=52 * MIB),
        cost_estimate=pl.CostEstimate(
            flops=2 * rows * depth * count,
            bytes_accessed=2 * depth * count,
            transcendentals=0,
        ),
        name=name,
    )(parts, w)


def local(query_vectors, key_vectors, value_vectors, out_weight):
    plan = Plan(query_vectors.shape[1] // HD)
    G, R, T = plan.G, plan.R, plan.T
    rows = query_vectors.shape[0]

    shifts = [(dg, dt) for dg in range(G) for dt in range(T)]

    def starts(where):
        g, t = where // (R * T), where % T
        return [((t + dt) % T * G + (g + dg) % G) * plan.cols for dg, dt in shifts]

    blocks = pack(plan, starts, G * T, [key_vectors, value_vectors], True, "pack_kv")
    arrived = [
        block if shift == (0, 0) else plan.move(block, *shift)
        for shift, block in zip(shifts, blocks)
    ]
    half = max(G // 2, 1) * T
    wide = R % 2 == 0 and R <= 8
    owns = [
        jnp.concatenate(arrived[first : first + half], axis=1)
        for first in range(0, len(shifts), half)
    ]
    nears = [
        [own]
        + [
            plan.move(own, r_map=lambda r, s=s: (r + 2 * s) % R)
            for s in range(1, R // 2 if wide else 1)
        ]
        for own in owns
    ]

    def fixed_starts(where):
        return [(t * G + g) * plan.cols for g in range(G) for t in range(T)]

    queries = pack(plan, fixed_starts, G * T, [query_vectors], False, "pack_q")[0]
    owns[0], queries = lax.optimization_barrier((owns[0], queries))
    groups = [[plan.flat(g, r, t) for g in range(G) for t in range(T)] for r in range(R)]
    queries = lax.all_to_all(
        queries.reshape(-1, plan.cols), AXES, 0, 0, axis_index_groups=groups, tiled=True
    )
    nears, queries = lax.optimization_barrier((nears, queries))

    kvs = []
    for near in nears:
        near = jnp.concatenate(near, axis=1)
        if wide:
            kvs += [near, plan.move(near, r_map=lambda r: r ^ 1)]
        else:
            groups = [[g * R + r for r in range(R)] for g in range(G)]
            kvs.append(lax.all_gather(near, "ctx", axis=1, tiled=True, axis_index_groups=groups))

    width = out_weight.shape[1]
    chunk = width // 4

    def give_back(attended):
        if G == 1:
            return attended
        groups = [[g * R + r for g in range(G)] for r in range(R)]
        return lax.all_to_all(attended, "ctx", 0, 0, axis_index_groups=groups, tiled=True)

    def shares(parts, name):
        return [
            project(plan, parts, out_weight, first, chunk, name)
            for first in range(0, width, chunk)
        ]

    others = attend(plan, queries, kvs, 1, T - 1, "attend_others")
    own = attend(plan, queries, kvs, 0, 1, "attend_own")
    sent = shares(give_back(others), "project_others")
    received = [
        [plan.move(share[(dt - 1) * rows : dt * rows], 0, -dt) for dt in range(1, T)]
        for share in sent
    ]
    own, _ = lax.optimization_barrier((own, sent[0]))
    kept = shares(give_back(own), "project_own")
    outs = []
    for mine, pieces in zip(kept, received):
        total = mine.astype(F32)
        for piece in pieces:
            total = total + piece.astype(F32)
        outs.append(total.astype(BF16))
    return jnp.concatenate(outs, axis=1)


def solution(mesh):
    spec = P(AXES, None)
    return jax.shard_map(
        local,
        mesh=mesh,
        in_specs=(spec, spec, spec, P("tp", None)),
        out_specs=spec,
        check_vma=False,
    )
```

```python
import functools
import math

import jax
import jax.numpy as jnp
from jax import lax
from jax.experimental import pallas as pl
from jax.experimental.pallas import tpu as pltpu
from jax.sharding import PartitionSpec as P

HD = 128
AXES = ("ctx", "tp")
MIB = 1024 * 1024
F32 = jnp.float32
BF16 = jnp.bfloat16


class Plan:
    def __init__(self, head_count):
        self.C = lax.axis_size("ctx")
        self.T = lax.axis_size("tp")
        self.G = math.gcd(head_count // self.T, self.C)
        self.R = self.C // self.G
        self.heads = head_count // (self.T * self.G)
        self.cols = self.heads * HD
        self.where = jnp.reshape(lax.axis_index(AXES), (1,)).astype(jnp.int32)

    def flat(self, g, r, t):
        return (g % self.G * self.R + r) * self.T + t % self.T

    def move(self, x, dg=0, dt=0, r_map=lambda r: r):
        pairs = [
            (self.flat(g, r, t), self.flat(g + dg, r_map(r), t + dt))
            for g in range(self.G)
            for r in range(self.R)
            for t in range(self.T)
        ]
        return lax.ppermute(x, AXES, pairs)


def pack_kernel(plan, shifts, where_ref, k_ref, v_ref, q_ref, *refs):
    kv_outs, q_out, held_kv, held_q, in_sem, out_sem = refs[:-5], *refs[-5:]
    G, R, T, cols = plan.G, plan.R, plan.T, plan.cols
    g, t = where_ref[0] // (R * T), lax.rem(where_ref[0], T)
    inward, outward = [], []
    for index, (dg, dt) in enumerate(shifts):
        start = (lax.rem(t + dt, T) * G + lax.rem(g + dg, G)) * cols
        for slot, in_ref in enumerate((k_ref, v_ref)):
            inward.append(
                pltpu.make_async_copy(
                    in_ref.at[:, pl.ds(pl.multiple_of(start, HD), cols)],
                    held_kv.at[index, slot],
                    in_sem.at[2 * index + slot],
                )
            )
    for index in range(G * T):
        start = (index % T * G + index // T) * cols
        inward.append(
            pltpu.make_async_copy(
                q_ref.at[:, start : start + cols], held_q.at[index], in_sem.at[2 * G * T + index]
            )
        )
    for copy in inward:
        copy.start()
    for index, out_ref in enumerate(kv_outs):
        inward[2 * index].wait()
        inward[2 * index + 1].wait()
        outward.append(pltpu.make_async_copy(held_kv.at[index], out_ref, out_sem.at[index]))
        outward[-1].start()
    for copy in inward[2 * G * T :]:
        copy.wait()
    outward.append(pltpu.make_async_copy(held_q, q_out, out_sem.at[G * T]))
    outward[-1].start()
    for copy in outward:
        copy.wait()


def pack(plan, shifts, k, v, q):
    rows = q.shape[0]
    count = plan.G * plan.T
    block = (2, rows, plan.cols)
    return pl.pallas_call(
        functools.partial(pack_kernel, plan, shifts),
        out_shape=[jax.ShapeDtypeStruct(block, BF16)] * count
        + [jax.ShapeDtypeStruct((count, rows, plan.cols), BF16)],
        in_specs=[pl.BlockSpec(memory_space=pltpu.SMEM)] + [pl.BlockSpec(memory_space=pl.ANY)] * 3,
        out_specs=[pl.BlockSpec(memory_space=pl.ANY)] * (count + 1),
        scratch_shapes=[
            pltpu.VMEM((count, *block), BF16),
            pltpu.VMEM((count, rows, plan.cols), BF16),
            pltpu.SemaphoreType.DMA((3 * count,)),
            pltpu.SemaphoreType.DMA((count + 1,)),
        ],
        compiler_params=pltpu.CompilerParams(vmem_limit_bytes=60 * MIB),
        name="pack",
    )(plan.where, k, v, q)


def attend_kernel(plan, first, count, kv_count, where_ref, q_ref, *refs):
    kv_refs, refs = refs[:kv_count], refs[kv_count:]
    copies = []
    if len(refs) > plan.G + 1:
        w_ref, refs = refs[0], refs[1:]
        w_out, w_sem = refs[plan.G], refs[-1]
        depth = w_ref.shape[0] // w_sem.shape[0]
        for index in range(w_sem.shape[0]):
            rows = pl.ds(index * depth, depth)
            copies.append(
                pltpu.make_async_copy(w_ref.at[rows, :], w_out.at[rows, :], w_sem.at[index])
            )
            copies[-1].start()
    out_refs, scores = refs[: plan.G], refs[-2] if copies else refs[-1]
    G, R, T = plan.G, plan.R, plan.T
    scale = math.log2(math.e) / math.sqrt(HD)
    own_g, own_t = where_ref[0] // (R * T), lax.rem(where_ref[0], T)
    rows = out_refs[0].shape[0] // count
    tile_groups = math.gcd(G, max(256 // (count * rows), 1))
    tile = tile_groups * count * rows
    for head in range(plan.heads):
        cols = slice(head * HD, (head + 1) * HD)
        for at in range(0, G, tile_groups):
            pieces = []
            for dg in range(at, at + tile_groups):
                g = lax.rem(own_g + G - dg, G)
                for dt in range(first, first + count):
                    start = (g * T + lax.rem(own_t + T - dt, T)) * rows
                    pieces.append(q_ref[pl.ds(pl.multiple_of(start, rows), rows), cols])
            q = jnp.concatenate(pieces, axis=0)
            peak = None
            key = 0
            for kv_ref in kv_refs:
                keys = kv_ref.shape[1]
                part = lax.dot_general(
                    q, kv_ref[0, :, cols], (((1,), (1,)), ((), ())), preferred_element_type=F32
                )
                scores[head % 2, :, pl.ds(key, keys)] = part
                top = jnp.max(part, axis=-1, keepdims=True)
                peak = top if peak is None else jnp.maximum(peak, top)
                key += keys
            peak = peak * scale
            weighted = jnp.zeros((tile, HD), F32)
            total = jnp.zeros((tile, 1), F32)
            key = 0
            for kv_ref in kv_refs:
                keys = kv_ref.shape[1]
                probs = jnp.exp2(scores[head % 2, :, pl.ds(key, keys)] * scale - peak).astype(BF16)
                total += jnp.sum(probs.astype(F32), axis=-1, keepdims=True)
                weighted += jnp.dot(probs, kv_ref[1, :, cols], preferred_element_type=F32)
                key += keys
            attended = (weighted / total).astype(BF16)
            for index in range(tile_groups):
                block = attended[index * count * rows : (index + 1) * count * rows]
                out_refs[at + index][:, cols] = block
    for copy in copies:
        copy.wait()


def attend(plan, q, kvs, first, count, name, weight=None):
    rows = q.shape[0] // (plan.G * plan.T)
    asked = plan.G * count * rows
    keys = sum(kv.shape[1] for kv in kvs)
    tile = math.gcd(plan.G, max(256 // (count * rows), 1)) * count * rows
    vmem = pl.BlockSpec(memory_space=pltpu.VMEM)
    extra = [] if weight is None else [weight]
    return pl.pallas_call(
        functools.partial(attend_kernel, plan, first, count, len(kvs)),
        out_shape=[jax.ShapeDtypeStruct((count * rows, plan.cols), BF16)] * plan.G
        + [jax.ShapeDtypeStruct(w.shape, w.dtype) for w in extra],
        in_specs=[pl.BlockSpec(memory_space=pltpu.SMEM), vmem]
        + [vmem] * len(kvs)
        + [pl.BlockSpec(memory_space=pl.ANY)] * len(extra),
        out_specs=[vmem] * (plan.G + len(extra)),
        scratch_shapes=[pltpu.VMEM((2, tile, keys), F32)]
        + [pltpu.SemaphoreType.DMA((4,))] * len(extra),
        compiler_params=pltpu.CompilerParams(vmem_limit_bytes=(33 if extra else 20) * MIB),
        cost_estimate=pl.CostEstimate(
            flops=4 * asked * keys * plan.cols,
            bytes_accessed=2 * plan.cols * (2 * asked + 2 * keys),
            transcendentals=asked * keys * plan.heads,
        ),
        name=name,
    )(plan.where, q, *kvs, *extra)


def project_kernel(plan, first, where_ref, *refs):
    parts, (w_ref, out_ref, mixed) = refs[:-3], refs[-3:]
    count = out_ref.shape[1]
    own_g = where_ref[0] // (plan.R * plan.T)
    for dg, part in enumerate(parts):
        place = lax.rem(own_g + dg, plan.G) * plan.cols
        mixed[:, pl.ds(pl.multiple_of(place, HD), plan.cols)] = part[...]
    out_ref[...] = jnp.dot(
        mixed[...], w_ref[:, first : first + count], preferred_element_type=F32
    ).astype(BF16)


def project(plan, parts, w, first, count, name):
    rows = parts[0].shape[0]
    depth = w.shape[0]
    vmem = pl.BlockSpec(memory_space=pltpu.VMEM)
    return pl.pallas_call(
        functools.partial(project_kernel, plan, first),
        out_shape=jax.ShapeDtypeStruct((rows, count), BF16),
        in_specs=[pl.BlockSpec(memory_space=pltpu.SMEM)] + [vmem] * (len(parts) + 1),
        out_specs=vmem,
        scratch_shapes=[pltpu.VMEM((rows, depth), BF16)],
        compiler_params=pltpu.CompilerParams(vmem_limit_bytes=20 * MIB),
        cost_estimate=pl.CostEstimate(
            flops=2 * rows * depth * count,
            bytes_accessed=2 * depth * count,
            transcendentals=0,
        ),
        name=name,
    )(plan.where, *parts, w)


def add_kernel(counts, kept_ref, *refs):
    out_ref, refs = refs[-1], list(refs[:-1])
    first = 0
    for count in counts:
        pieces, refs = refs[:count], refs[count:]
        cols = slice(first, first + pieces[0].shape[1])
        total = kept_ref[:, cols].astype(F32)
        for piece in pieces:
            total += piece[...].astype(F32)
        out_ref[:, cols] = total.astype(BF16)
        first = cols.stop


def add_up(kept, received):
    vmem = pl.BlockSpec(memory_space=pltpu.VMEM)
    pieces = [piece for group in received for piece in group]
    return pl.pallas_call(
        functools.partial(add_kernel, [len(group) for group in received]),
        out_shape=jax.ShapeDtypeStruct(kept.shape, BF16),
        in_specs=[vmem] * (1 + len(pieces)),
        out_specs=vmem,
        compiler_params=pltpu.CompilerParams(vmem_limit_bytes=20 * MIB),
        name="add_shares",
    )(kept, *pieces)


def local(query_vectors, key_vectors, value_vectors, out_weight):
    plan = Plan(query_vectors.shape[1] // HD)
    G, R, T = plan.G, plan.R, plan.T
    rows = query_vectors.shape[0]

    order = sorted(range(G), key=lambda dg: (-min(dg, G - dg), dg))
    halves = [order[: G // 2 - 1] + order[-1:], order[G // 2 - 1 : -1]] if G > 2 else [order]
    shifts = [(dg, dt) for half in halves for dg in half for dt in range(T)]
    *blocks, queries = pack(plan, shifts, key_vectors, value_vectors, query_vectors)
    arrived = {
        shift: block if shift == (0, 0) else plan.move(block, *shift)
        for shift, block in zip(shifts, blocks)
    }
    wide = R % 2 == 0 and R <= 8
    owns = [
        jnp.concatenate([arrived[dg, dt] for dg in half for dt in range(T)], axis=1)
        for half in halves
    ]
    nears = [
        [own]
        + [
            plan.move(own, r_map=lambda r, s=s: (r + 2 * s) % R)
            for s in range(1, R // 2 if wide else 1)
        ]
        for own in owns
    ]

    owns[0], queries = lax.optimization_barrier((owns[0], queries))
    groups = [[plan.flat(g, r, t) for g in range(G) for t in range(T)] for r in range(R)]
    queries = lax.all_to_all(
        queries.reshape(-1, plan.cols), AXES, 0, 0, axis_index_groups=groups, tiled=True
    )
    nears, queries = lax.optimization_barrier((nears, queries))

    kvs = []
    for near in nears:
        near = jnp.concatenate(near, axis=1)
        if wide:
            kvs += [near, plan.move(near, r_map=lambda r: r ^ 1)]
        else:
            groups = [[g * R + r for r in range(R)] for g in range(G)]
            kvs.append(lax.all_gather(near, "ctx", axis=1, tiled=True, axis_index_groups=groups))

    def give_back(attended):
        return [attended[0]] + [plan.move(attended[dg], -dg) for dg in range(1, G)]

    others = attend(plan, queries, kvs, 1, T - 1, "attend_others")
    *own, weight = attend(plan, queries, kvs, 0, 1, "attend_own", out_weight)
    width = out_weight.shape[1]
    edges = [0, width // 4, width]
    parts = give_back(others)
    sent = [
        project(plan, parts, weight, first, last - first, "project_others")
        for first, last in zip(edges, edges[1:])
    ]
    received = [
        [plan.move(share[(dt - 1) * rows : dt * rows], 0, -dt) for dt in range(1, T)]
        for share in sent
    ]
    own, received[0], _ = lax.optimization_barrier((own, received[0], sent[1]))
    kept = project(plan, give_back(own), weight, 0, width, "project_own")
    return add_up(kept, received)


def solution(mesh):
    spec = P(AXES, None)
    return jax.shard_map(
        local,
        mesh=mesh,
        in_specs=(spec, spec, spec, P("tp", None)),
        out_specs=spec,
        check_vma=False,
    )
```

```python
import functools
import math

import jax
import jax.numpy as jnp
from jax import lax
from jax.experimental import pallas as pl
from jax.experimental.pallas import tpu as pltpu
from jax.sharding import PartitionSpec as P

HD = 128
AXES = ("ctx", "tp")
MIB = 1024 * 1024
F32 = jnp.float32
BF16 = jnp.bfloat16


class Plan:
    def __init__(self, head_count):
        self.C = lax.axis_size("ctx")
        self.T = lax.axis_size("tp")
        self.G = math.gcd(head_count // self.T, self.C)
        self.R = self.C // self.G
        self.heads = head_count // (self.T * self.G)
        self.cols = self.heads * HD
        self.where = jnp.reshape(lax.axis_index(AXES), (1,)).astype(jnp.int32)

    def flat(self, g, r, t):
        return (g % self.G * self.R + r) * self.T + t % self.T

    def move(self, x, dg=0, dt=0, r_map=lambda r: r):
        pairs = [
            (self.flat(g, r, t), self.flat(g + dg, r_map(r), t + dt))
            for g in range(self.G)
            for r in range(self.R)
            for t in range(self.T)
        ]
        return lax.ppermute(x, AXES, pairs)


def pack_kernel(plan, shifts, where_ref, k_ref, v_ref, q_ref, *refs):
    kv_outs, q_out, held_kv, held_q, in_sem, out_sem = refs[:-5], *refs[-5:]
    G, R, T, cols = plan.G, plan.R, plan.T, plan.cols
    g, t = where_ref[0] // (R * T), lax.rem(where_ref[0], T)
    inward, outward = [], []
    for index, (dg, dt) in enumerate(shifts):
        start = (lax.rem(t + dt, T) * G + lax.rem(g + dg, G)) * cols
        for slot, in_ref in enumerate((k_ref, v_ref)):
            inward.append(
                pltpu.make_async_copy(
                    in_ref.at[:, pl.ds(pl.multiple_of(start, HD), cols)],
                    held_kv.at[index, slot],
                    in_sem.at[2 * index + slot],
                )
            )
    for index in range(G * T):
        start = (index % T * G + index // T) * cols
        inward.append(
            pltpu.make_async_copy(
                q_ref.at[:, start : start + cols], held_q.at[index], in_sem.at[2 * G * T + index]
            )
        )
    for copy in inward:
        copy.start()
    for index, out_ref in enumerate(kv_outs):
        inward[2 * index].wait()
        inward[2 * index + 1].wait()
        outward.append(pltpu.make_async_copy(held_kv.at[index], out_ref, out_sem.at[index]))
        outward[-1].start()
    for copy in inward[2 * G * T :]:
        copy.wait()
    outward.append(pltpu.make_async_copy(held_q, q_out, out_sem.at[G * T]))
    outward[-1].start()
    for copy in outward:
        copy.wait()


def pack(plan, shifts, k, v, q):
    rows = q.shape[0]
    count = plan.G * plan.T
    block = (2, rows, plan.cols)
    return pl.pallas_call(
        functools.partial(pack_kernel, plan, shifts),
        out_shape=[jax.ShapeDtypeStruct(block, BF16)] * count
        + [jax.ShapeDtypeStruct((count, rows, plan.cols), BF16)],
        in_specs=[pl.BlockSpec(memory_space=pltpu.SMEM)] + [pl.BlockSpec(memory_space=pl.ANY)] * 3,
        out_specs=[pl.BlockSpec(memory_space=pl.ANY)] * (count + 1),
        scratch_shapes=[
            pltpu.VMEM((count, *block), BF16),
            pltpu.VMEM((count, rows, plan.cols), BF16),
            pltpu.SemaphoreType.DMA((3 * count,)),
            pltpu.SemaphoreType.DMA((count + 1,)),
        ],
        compiler_params=pltpu.CompilerParams(vmem_limit_bytes=60 * MIB),
        name="pack",
    )(plan.where, k, v, q)


def join_kernel(*refs):
    out_ref = refs[-1]
    first = 0
    for in_ref in refs[:-1]:
        count = in_ref.shape[1]
        out_ref[:, first : first + count, :] = in_ref[...]
        first += count


def join(pieces):
    shape = (pieces[0].shape[0], sum(piece.shape[1] for piece in pieces), pieces[0].shape[2])
    vmem = pl.BlockSpec(memory_space=pltpu.VMEM)
    return pl.pallas_call(
        join_kernel,
        out_shape=jax.ShapeDtypeStruct(shape, BF16),
        in_specs=[vmem] * len(pieces),
        out_specs=vmem,
        compiler_params=pltpu.CompilerParams(vmem_limit_bytes=20 * MIB),
        name="join",
    )(*pieces)


def fetch_kernel(w_ref, out_ref, sem):
    depth = w_ref.shape[0] // sem.shape[0]
    copies = []
    for index in range(sem.shape[0]):
        rows = pl.ds(index * depth, depth)
        copies.append(pltpu.make_async_copy(w_ref.at[rows, :], out_ref.at[rows, :], sem.at[index]))
        copies[-1].start()
    for copy in copies:
        copy.wait()


def fetch(w):
    return pl.pallas_call(
        fetch_kernel,
        out_shape=jax.ShapeDtypeStruct(w.shape, w.dtype),
        in_specs=[pl.BlockSpec(memory_space=pl.ANY)],
        out_specs=pl.BlockSpec(memory_space=pltpu.VMEM),
        scratch_shapes=[pltpu.SemaphoreType.DMA((4,))],
        compiler_params=pltpu.CompilerParams(vmem_limit_bytes=33 * MIB),
        cost_estimate=pl.CostEstimate(
            flops=0, bytes_accessed=4 * w.shape[0] * w.shape[1], transcendentals=0
        ),
        name="fetch_weight",
    )(w)


def attend_kernel(plan, first, count, kv_count, where_ref, q_ref, *refs):
    kv_refs, refs = refs[:kv_count], refs[kv_count:]
    out_refs, scores = refs[:-1], refs[-1]
    G, R, T = plan.G, plan.R, plan.T
    scale = math.log2(math.e) / math.sqrt(HD)
    own_g, own_t = where_ref[0] // (R * T), lax.rem(where_ref[0], T)
    rows = out_refs[0].shape[0] // count
    tile_groups = math.gcd(G, max(256 // (count * rows), 1))
    tile = tile_groups * count * rows
    for head in range(plan.heads):
        cols = slice(head * HD, (head + 1) * HD)
        for at in range(0, G, tile_groups):
            pieces = []
            for dg in range(at, at + tile_groups):
                g = lax.rem(own_g + G - dg, G)
                for dt in range(first, first + count):
                    start = (g * T + lax.rem(own_t + T - dt, T)) * rows
                    pieces.append(q_ref[pl.ds(pl.multiple_of(start, rows), rows), cols])
            q = jnp.concatenate(pieces, axis=0)
            peak = None
            key = 0
            for kv_ref in kv_refs:
                keys = kv_ref.shape[1]
                part = lax.dot_general(
                    q, kv_ref[0, :, cols], (((1,), (1,)), ((), ())), preferred_element_type=F32
                )
                scores[head % 2, :, pl.ds(key, keys)] = part
                top = jnp.max(part, axis=-1, keepdims=True)
                peak = top if peak is None else jnp.maximum(peak, top)
                key += keys
            peak = peak * scale
            weighted = jnp.zeros((tile, HD), F32)
            total = jnp.zeros((tile, 1), F32)
            key = 0
            for kv_ref in kv_refs:
                keys = kv_ref.shape[1]
                probs = jnp.exp2(scores[head % 2, :, pl.ds(key, keys)] * scale - peak).astype(BF16)
                total += jnp.sum(probs.astype(F32), axis=-1, keepdims=True)
                weighted += jnp.dot(probs, kv_ref[1, :, cols], preferred_element_type=F32)
                key += keys
            attended = (weighted / total).astype(BF16)
            for index in range(tile_groups):
                block = attended[index * count * rows : (index + 1) * count * rows]
                out_refs[at + index][:, cols] = block


def attend(plan, q, kvs, first, count, name):
    rows = q.shape[0] // (plan.G * plan.T)
    asked = plan.G * count * rows
    keys = sum(kv.shape[1] for kv in kvs)
    tile = math.gcd(plan.G, max(256 // (count * rows), 1)) * count * rows
    vmem = pl.BlockSpec(memory_space=pltpu.VMEM)
    return pl.pallas_call(
        functools.partial(attend_kernel, plan, first, count, len(kvs)),
        out_shape=[jax.ShapeDtypeStruct((count * rows, plan.cols), BF16)] * plan.G,
        in_specs=[pl.BlockSpec(memory_space=pltpu.SMEM), vmem] + [vmem] * len(kvs),
        out_specs=[vmem] * plan.G,
        scratch_shapes=[pltpu.VMEM((2, tile, keys), F32)],
        compiler_params=pltpu.CompilerParams(vmem_limit_bytes=20 * MIB),
        cost_estimate=pl.CostEstimate(
            flops=4 * asked * keys * plan.cols,
            bytes_accessed=2 * plan.cols * (2 * asked + 2 * keys),
            transcendentals=asked * keys * plan.heads,
        ),
        name=name,
    )(plan.where, q, *kvs)


def project_kernel(plan, first, where_ref, *refs):
    parts, (w_ref, out_ref, mixed) = refs[:-3], refs[-3:]
    count = out_ref.shape[1]
    own_g = where_ref[0] // (plan.R * plan.T)
    for dg, part in enumerate(parts):
        place = lax.rem(own_g + dg, plan.G) * plan.cols
        mixed[:, pl.ds(pl.multiple_of(place, HD), plan.cols)] = part[...]
    out_ref[...] = jnp.dot(
        mixed[...], w_ref[:, first : first + count], preferred_element_type=F32
    ).astype(BF16)


def project(plan, parts, w, first, count, name):
    rows = parts[0].shape[0]
    depth = w.shape[0]
    vmem = pl.BlockSpec(memory_space=pltpu.VMEM)
    return pl.pallas_call(
        functools.partial(project_kernel, plan, first),
        out_shape=jax.ShapeDtypeStruct((rows, count), BF16),
        in_specs=[pl.BlockSpec(memory_space=pltpu.SMEM)] + [vmem] * (len(parts) + 1),
        out_specs=vmem,
        scratch_shapes=[pltpu.VMEM((rows, depth), BF16)],
        compiler_params=pltpu.CompilerParams(vmem_limit_bytes=20 * MIB),
        cost_estimate=pl.CostEstimate(
            flops=2 * rows * depth * count,
            bytes_accessed=2 * depth * count,
            transcendentals=0,
        ),
        name=name,
    )(plan.where, *parts, w)


def add_kernel(counts, kept_ref, *refs):
    out_ref, refs = refs[-1], list(refs[:-1])
    first = 0
    for count in counts:
        pieces, refs = refs[:count], refs[count:]
        cols = slice(first, first + pieces[0].shape[1])
        total = kept_ref[:, cols].astype(F32)
        for piece in pieces:
            total += piece[...].astype(F32)
        out_ref[:, cols] = total.astype(BF16)
        first = cols.stop


def add_up(kept, received):
    vmem = pl.BlockSpec(memory_space=pltpu.VMEM)
    pieces = [piece for group in received for piece in group]
    return pl.pallas_call(
        functools.partial(add_kernel, [len(group) for group in received]),
        out_shape=jax.ShapeDtypeStruct(kept.shape, BF16),
        in_specs=[vmem] * (1 + len(pieces)),
        out_specs=vmem,
        compiler_params=pltpu.CompilerParams(vmem_limit_bytes=20 * MIB),
        name="add_shares",
    )(kept, *pieces)


def local(query_vectors, key_vectors, value_vectors, out_weight):
    plan = Plan(query_vectors.shape[1] // HD)
    G, R, T = plan.G, plan.R, plan.T
    rows = query_vectors.shape[0]

    shifts = [(dg, dt) for dg in range(G) for dt in range(T)]
    if G > 3:
        shifts = [(0, 0), (0, 1), (1, 0)] + [(dg, dt) for dg, dt in shifts if dg == G // 2] + [
            (dg, dt) for dg, dt in shifts if dg != G // 2 and (dg, dt) not in ((0, 0), (0, 1), (1, 0))
        ]
    halves = [range(G // 2), range(G // 2, G)] if G > 1 else [range(1)]
    *blocks, queries = pack(plan, shifts, key_vectors, value_vectors, query_vectors)
    arrived = {
        shift: block if shift == (0, 0) else plan.move(block, *shift)
        for shift, block in zip(shifts, blocks)
    }
    wide = R % 2 == 0 and R <= 8
    owns = [
        join([arrived[dg, dt] for dg in half for dt in range(T)]) for half in halves
    ]
    nears = [
        [own]
        + [
            plan.move(own, r_map=lambda r, s=s: (r + 2 * s) % R)
            for s in range(1, R // 2 if wide else 1)
        ]
        for own in owns
    ]

    owns[0], queries = lax.optimization_barrier((owns[0], queries))
    groups = [[plan.flat(g, r, t) for g in range(G) for t in range(T)] for r in range(R)]
    queries = lax.all_to_all(
        queries.reshape(-1, plan.cols), AXES, 0, 0, axis_index_groups=groups, tiled=True
    )
    nears, queries, weight = lax.optimization_barrier((nears, queries, out_weight))
    weight = fetch(weight)

    kvs = []
    for near in nears:
        near = join(near) if len(near) > 1 else near[0]
        if wide:
            kvs += [near, plan.move(near, r_map=lambda r: r ^ 1)]
        else:
            groups = [[g * R + r for r in range(R)] for g in range(G)]
            kvs.append(lax.all_gather(near, "ctx", axis=1, tiled=True, axis_index_groups=groups))

    def give_back(attended):
        return [attended[0]] + [plan.move(attended[dg], -dg) for dg in range(1, G)]

    queries, weight = lax.optimization_barrier((queries, weight))
    others = attend(plan, queries, kvs, 1, T - 1, "attend_others")
    own = attend(plan, queries, kvs, 0, 1, "attend_own")
    width = out_weight.shape[1]
    edges = [0, width // 4, width]
    parts = give_back(others)
    sent = []
    for first, last in zip(edges, edges[1:]):
        sent.append(project(plan, parts, weight, first, last - first, "project_others"))
        parts, sent[-1] = lax.optimization_barrier((parts, sent[-1]))
    received = [
        [plan.move(share[(dt - 1) * rows : dt * rows], 0, -dt) for dt in range(1, T)]
        for share in sent
    ]
    own, received[0], _ = lax.optimization_barrier((own, received[0], parts))
    kept = project(plan, give_back(own), weight, 0, width, "project_own")
    return add_up(kept, received)


def solution(mesh):
    spec = P(AXES, None)
    return jax.shard_map(
        local,
        mesh=mesh,
        in_specs=(spec, spec, spec, P("tp", None)),
        out_specs=spec,
        check_vma=False,
    )
```

```python
import functools
import math

import jax
import jax.numpy as jnp
from jax import lax
from jax.experimental import pallas as pl
from jax.experimental.pallas import tpu as pltpu
from jax.sharding import PartitionSpec as P

HD = 128
AXES = ("ctx", "tp")
MIB = 1024 * 1024
F32 = jnp.float32
BF16 = jnp.bfloat16


class Plan:
    def __init__(self, head_count):
        self.C = lax.axis_size("ctx")
        self.T = lax.axis_size("tp")
        self.G = math.gcd(head_count // self.T, self.C)
        self.R = self.C // self.G
        self.heads = head_count // (self.T * self.G)
        self.cols = self.heads * HD
        self.where = jnp.reshape(lax.axis_index(AXES), (1,)).astype(jnp.int32)

    def flat(self, g, r, t):
        return (g % self.G * self.R + r) * self.T + t % self.T

    def move(self, x, dg=0, dt=0, r_map=lambda r: r):
        pairs = [
            (self.flat(g, r, t), self.flat(g + dg, r_map(r), t + dt))
            for g in range(self.G)
            for r in range(self.R)
            for t in range(self.T)
        ]
        return lax.ppermute(x, AXES, pairs)


def pack_kernel(plan, shifts, where_ref, k_ref, v_ref, q_ref, *refs):
    kv_outs, q_out, held_kv, held_q, in_sem, out_sem = refs[:-5], *refs[-5:]
    G, R, T, cols = plan.G, plan.R, plan.T, plan.cols
    g, t = where_ref[0] // (R * T), lax.rem(where_ref[0], T)
    inward, outward = [], []
    for index, (dg, dt) in enumerate(shifts):
        start = (lax.rem(t + dt, T) * G + lax.rem(g + dg, G)) * cols
        for slot, in_ref in enumerate((k_ref, v_ref)):
            inward.append(
                pltpu.make_async_copy(
                    in_ref.at[:, pl.ds(pl.multiple_of(start, HD), cols)],
                    held_kv.at[index, slot],
                    in_sem.at[2 * index + slot],
                )
            )
    for index in range(G * T):
        start = (index % T * G + index // T) * cols
        inward.append(
            pltpu.make_async_copy(
                q_ref.at[:, start : start + cols], held_q.at[index], in_sem.at[2 * G * T + index]
            )
        )
    for copy in inward:
        copy.start()
    for index, out_ref in enumerate(kv_outs):
        inward[2 * index].wait()
        inward[2 * index + 1].wait()
        outward.append(pltpu.make_async_copy(held_kv.at[index], out_ref, out_sem.at[index]))
        outward[-1].start()
    for copy in inward[2 * G * T :]:
        copy.wait()
    outward.append(pltpu.make_async_copy(held_q, q_out, out_sem.at[G * T]))
    outward[-1].start()
    for copy in outward:
        copy.wait()


def pack(plan, shifts, k, v, q):
    rows = q.shape[0]
    count = plan.G * plan.T
    block = (2, rows, plan.cols)
    return pl.pallas_call(
        functools.partial(pack_kernel, plan, shifts),
        out_shape=[jax.ShapeDtypeStruct(block, BF16)] * count
        + [jax.ShapeDtypeStruct((count, rows, plan.cols), BF16)],
        in_specs=[pl.BlockSpec(memory_space=pltpu.SMEM)] + [pl.BlockSpec(memory_space=pl.ANY)] * 3,
        out_specs=[pl.BlockSpec(memory_space=pl.ANY)] * (count + 1),
        scratch_shapes=[
            pltpu.VMEM((count, *block), BF16),
            pltpu.VMEM((count, rows, plan.cols), BF16),
            pltpu.SemaphoreType.DMA((3 * count,)),
            pltpu.SemaphoreType.DMA((count + 1,)),
        ],
        compiler_params=pltpu.CompilerParams(vmem_limit_bytes=60 * MIB),
        name="pack",
    )(plan.where, k, v, q)


def fetch_kernel(first, w_ref, out_ref, sem):
    depth = out_ref.shape[0] // sem.shape[0]
    copies = []
    for index in range(sem.shape[0]):
        copies.append(
            pltpu.make_async_copy(
                w_ref.at[pl.ds(first + index * depth, depth), :],
                out_ref.at[pl.ds(index * depth, depth), :],
                sem.at[index],
            )
        )
        copies[-1].start()
    for copy in copies:
        copy.wait()


def fetch(w, first, count):
    return pl.pallas_call(
        functools.partial(fetch_kernel, first),
        out_shape=jax.ShapeDtypeStruct((count, w.shape[1]), w.dtype),
        in_specs=[pl.BlockSpec(memory_space=pl.ANY)],
        out_specs=pl.BlockSpec(memory_space=pltpu.VMEM),
        scratch_shapes=[pltpu.SemaphoreType.DMA((2,))],
        compiler_params=pltpu.CompilerParams(vmem_limit_bytes=38 * MIB),
        cost_estimate=pl.CostEstimate(
            flops=0, bytes_accessed=4 * count * w.shape[1], transcendentals=0
        ),
        name="fetch_weight",
    )(w)


def attend_kernel(plan, first, count, kv_count, where_ref, q_ref, *refs):
    kv_refs, refs = refs[:kv_count], refs[kv_count:]
    out_refs, scores = refs[:-1], refs[-1]
    G, R, T = plan.G, plan.R, plan.T
    scale = math.log2(math.e) / math.sqrt(HD)
    own_g, own_t = where_ref[0] // (R * T), lax.rem(where_ref[0], T)
    rows = out_refs[0].shape[0] // count
    tile_groups = math.gcd(G, max(256 // (count * rows), 1))
    tile = tile_groups * count * rows
    for head in range(plan.heads):
        cols = slice(head * HD, (head + 1) * HD)
        for at in range(0, G, tile_groups):
            pieces = []
            for dg in range(at, at + tile_groups):
                g = lax.rem(own_g + G - dg, G)
                for dt in range(first, first + count):
                    start = (g * T + lax.rem(own_t + T - dt, T)) * rows
                    pieces.append(q_ref[pl.ds(pl.multiple_of(start, rows), rows), cols])
            q = jnp.concatenate(pieces, axis=0)
            peak = None
            key = 0
            for kv_ref in kv_refs:
                keys = kv_ref.shape[1]
                part = lax.dot_general(
                    q, kv_ref[0, :, cols], (((1,), (1,)), ((), ())), preferred_element_type=F32
                )
                scores[head % 2, :, pl.ds(key, keys)] = part
                top = jnp.max(part, axis=-1, keepdims=True)
                peak = top if peak is None else jnp.maximum(peak, top)
                key += keys
            peak = peak * scale
            weighted = jnp.zeros((tile, HD), F32)
            total = jnp.zeros((tile, 1), F32)
            key = 0
            for kv_ref in kv_refs:
                keys = kv_ref.shape[1]
                probs = jnp.exp2(scores[head % 2, :, pl.ds(key, keys)] * scale - peak).astype(BF16)
                total += jnp.sum(probs.astype(F32), axis=-1, keepdims=True)
                weighted += jnp.dot(probs, kv_ref[1, :, cols], preferred_element_type=F32)
                key += keys
            attended = (weighted / total).astype(BF16)
            for index in range(tile_groups):
                block = attended[index * count * rows : (index + 1) * count * rows]
                out_refs[at + index][:, cols] = block


def attend(plan, q, kvs, first, count, name):
    rows = q.shape[0] // (plan.G * plan.T)
    asked = plan.G * count * rows
    keys = sum(kv.shape[1] for kv in kvs)
    tile = math.gcd(plan.G, max(256 // (count * rows), 1)) * count * rows
    vmem = pl.BlockSpec(memory_space=pltpu.VMEM)
    return pl.pallas_call(
        functools.partial(attend_kernel, plan, first, count, len(kvs)),
        out_shape=[jax.ShapeDtypeStruct((count * rows, plan.cols), BF16)] * plan.G,
        in_specs=[pl.BlockSpec(memory_space=pltpu.SMEM), vmem] + [vmem] * len(kvs),
        out_specs=[vmem] * plan.G,
        scratch_shapes=[pltpu.VMEM((2, tile, keys), F32)],
        compiler_params=pltpu.CompilerParams(vmem_limit_bytes=20 * MIB),
        cost_estimate=pl.CostEstimate(
            flops=4 * asked * keys * plan.cols,
            bytes_accessed=2 * plan.cols * (2 * asked + 2 * keys),
            transcendentals=asked * keys * plan.heads,
        ),
        name=name,
    )(plan.where, q, *kvs)


def project_kernel(plan, weight_count, where_ref, *refs):
    parts, w_refs, (out_ref, mixed) = (
        refs[: plan.G],
        refs[plan.G : plan.G + weight_count],
        refs[plan.G + weight_count :],
    )
    own_g = where_ref[0] // (plan.R * plan.T)
    for dg, part in enumerate(parts):
        place = lax.rem(own_g + dg, plan.G) * plan.cols
        mixed[:, pl.ds(pl.multiple_of(place, HD), plan.cols)] = part[...]
    total = None
    depth = 0
    for w_ref in w_refs:
        share = jnp.dot(
            mixed[:, depth : depth + w_ref.shape[0]],
            w_ref[...],
            preferred_element_type=F32,
        )
        total = share if total is None else total + share
        depth += w_ref.shape[0]
    out_ref[...] = total.astype(BF16)


def project(plan, parts, weights, flops, name):
    rows = parts[0].shape[0]
    depth = sum(w.shape[0] for w in weights)
    vmem = pl.BlockSpec(memory_space=pltpu.VMEM)
    return pl.pallas_call(
        functools.partial(project_kernel, plan, len(weights)),
        out_shape=jax.ShapeDtypeStruct((rows, weights[0].shape[1]), BF16),
        in_specs=[pl.BlockSpec(memory_space=pltpu.SMEM)] + [vmem] * (len(parts) + len(weights)),
        out_specs=vmem,
        scratch_shapes=[pltpu.VMEM((rows, depth), BF16)],
        compiler_params=pltpu.CompilerParams(vmem_limit_bytes=20 * MIB),
        cost_estimate=pl.CostEstimate(flops=flops, bytes_accessed=flops // 64, transcendentals=0),
        name=name,
    )(plan.where, *parts, *weights)


def add_kernel(*refs):
    total = refs[0][...].astype(F32)
    for in_ref in refs[1:-1]:
        total += in_ref[...].astype(F32)
    refs[-1][...] = total.astype(BF16)


def add_up(kept, received):
    vmem = pl.BlockSpec(memory_space=pltpu.VMEM)
    return pl.pallas_call(
        add_kernel,
        out_shape=jax.ShapeDtypeStruct(kept.shape, BF16),
        in_specs=[vmem] * (1 + len(received)),
        out_specs=vmem,
        compiler_params=pltpu.CompilerParams(vmem_limit_bytes=20 * MIB),
        cost_estimate=pl.CostEstimate(flops=0, bytes_accessed=0, transcendentals=0),
        name="add_shares",
    )(kept, *received)


def local(query_vectors, key_vectors, value_vectors, out_weight):
    plan = Plan(query_vectors.shape[1] // HD)
    G, R, T = plan.G, plan.R, plan.T
    rows = query_vectors.shape[0]

    shifts = [(dg, dt) for dg in range(G) for dt in range(T)]
    if G > 3:
        shifts = [(0, 0), (0, 1), (1, 0)] + [(dg, dt) for dg, dt in shifts if dg == G // 2] + [
            (dg, dt) for dg, dt in shifts if dg != G // 2 and (dg, dt) not in ((0, 0), (0, 1), (1, 0))
        ]
    halves = [range(G // 2), range(G // 2, G)] if G > 1 else [range(1)]
    *blocks, queries = pack(plan, shifts, key_vectors, value_vectors, query_vectors)
    arrived = {
        shift: block if shift == (0, 0) else plan.move(block, *shift)
        for shift, block in zip(shifts, blocks)
    }
    wide = R % 2 == 0 and R <= 8
    owns = [
        jnp.concatenate([arrived[dg, dt] for dg in half for dt in range(T)], axis=1)
        for half in halves
    ]
    nears = [
        [own]
        + [
            plan.move(own, r_map=lambda r, s=s: (r + 2 * s) % R)
            for s in range(1, R // 2 if wide else 1)
        ]
        for own in owns
    ]

    owns[0], queries = lax.optimization_barrier((owns[0], queries))
    groups = [[plan.flat(g, r, t) for g in range(G) for t in range(T)] for r in range(R)]
    queries = lax.all_to_all(
        queries.reshape(-1, plan.cols), AXES, 0, 0, axis_index_groups=groups, tiled=True
    )
    nears, queries = lax.optimization_barrier((nears, queries))
    nears = [jnp.concatenate(near, axis=1) if len(near) > 1 else near[0] for near in nears]
    nears, queries, weight = lax.optimization_barrier((nears, queries, out_weight))
    half = weight.shape[0] // 2
    upper = fetch(weight, 0, half)
    kvs = []
    for near in nears:
        if wide:
            kvs += [near, plan.move(near, r_map=lambda r: r ^ 1)]
        else:
            groups = [[g * R + r for r in range(R)] for g in range(G)]
            kvs.append(lax.all_gather(near, "ctx", axis=1, tiled=True, axis_index_groups=groups))

    def give_back(attended):
        return [attended[0]] + [plan.move(attended[dg], -dg) for dg in range(1, G)]

    queries, upper = lax.optimization_barrier((queries, upper))
    others = list(attend(plan, queries, kvs, 1, T - 1, "attend_others"))
    queries, others[0], weight = lax.optimization_barrier((queries, others[0], weight))
    own = attend(plan, queries, kvs, 0, 1, "attend_own")
    weights = [upper, fetch(weight, half, half)]
    parts = give_back(others)
    parts, weights, own = lax.optimization_barrier((parts, weights, own))
    flops = 2 * (T - 1) * rows * weight.shape[0] * weight.shape[1]
    sent = project(plan, parts, weights, flops, "project_others")
    own, sent = lax.optimization_barrier((own, sent))
    received = [
        plan.move(sent[(dt - 1) * rows : dt * rows], 0, -dt) for dt in range(1, T)
    ]
    kept = project(plan, give_back(own), weights, 0, "project_own")
    return add_up(kept, received)


def solution(mesh):
    spec = P(AXES, None)
    return jax.shard_map(
        local,
        mesh=mesh,
        in_specs=(spec, spec, spec, P("tp", None)),
        out_specs=spec,
        check_vma=False,
    )
```

```python
import functools
import math

import jax
import jax.numpy as jnp
from jax import lax
from jax.experimental import pallas as pl
from jax.experimental.pallas import tpu as pltpu
from jax.sharding import PartitionSpec as P

HD = 128
AXES = ("ctx", "tp")
MIB = 1024 * 1024
F32 = jnp.float32
BF16 = jnp.bfloat16


class Plan:
    def __init__(self, head_count):
        self.C = lax.axis_size("ctx")
        self.T = lax.axis_size("tp")
        self.G = math.gcd(head_count // self.T, self.C)
        self.R = self.C // self.G
        self.heads = head_count // (self.T * self.G)
        self.cols = self.heads * HD
        self.where = jnp.reshape(lax.axis_index(AXES), (1,)).astype(jnp.int32)

    def flat(self, g, r, t):
        return (g % self.G * self.R + r) * self.T + t % self.T

    def move(self, x, dg=0, dt=0, r_map=lambda r: r):
        pairs = [
            (self.flat(g, r, t), self.flat(g + dg, r_map(r), t + dt))
            for g in range(self.G)
            for r in range(self.R)
            for t in range(self.T)
        ]
        return lax.ppermute(x, AXES, pairs)


def pack_kernel(plan, shifts, where_ref, k_ref, v_ref, q_ref, *refs):
    outs, held_kv, held_q, in_sem, out_sem = refs[:-4], *refs[-4:]
    G, R, T, cols = plan.G, plan.R, plan.T, plan.cols
    g, t = where_ref[0] // (R * T), lax.rem(where_ref[0], T)
    groups = []
    for slots in (((k_ref, 0), (v_ref, 1)), ((q_ref, 2),)):
        for index, (dg, dt) in enumerate(shifts):
            start = (lax.rem(t + dt, T) * G + lax.rem(g + dg, G)) * cols
            columns = pl.ds(pl.multiple_of(start, HD), cols)
            groups.append([])
            for in_ref, slot in slots:
                held = held_q.at[index] if slot == 2 else held_kv.at[index, slot]
                copy = pltpu.make_async_copy(
                    in_ref.at[:, columns], held, in_sem.at[3 * index + slot]
                )
                copy.start()
                groups[-1].append(copy)
    outward = []
    for index, (group, out_ref) in enumerate(zip(groups, outs)):
        for copy in group:
            copy.wait()
        count = len(shifts)
        held = held_kv.at[index] if index < count else held_q.at[index - count]
        outward.append(pltpu.make_async_copy(held, out_ref, out_sem.at[index]))
        outward[-1].start()
    for copy in outward:
        copy.wait()


def pack(plan, shifts, k, v, q):
    rows = q.shape[0]
    count = len(shifts)
    kv_shape, q_shape = (2, rows, plan.cols), (rows, plan.cols)
    outs = pl.pallas_call(
        functools.partial(pack_kernel, plan, shifts),
        out_shape=[jax.ShapeDtypeStruct(kv_shape, BF16)] * count
        + [jax.ShapeDtypeStruct(q_shape, BF16)] * count,
        in_specs=[pl.BlockSpec(memory_space=pltpu.SMEM)] + [pl.BlockSpec(memory_space=pl.ANY)] * 3,
        out_specs=[pl.BlockSpec(memory_space=pl.ANY)] * (2 * count),
        scratch_shapes=[
            pltpu.VMEM((count, *kv_shape), BF16),
            pltpu.VMEM((count, *q_shape), BF16),
            pltpu.SemaphoreType.DMA((3 * count,)),
            pltpu.SemaphoreType.DMA((2 * count,)),
        ],
        compiler_params=pltpu.CompilerParams(vmem_limit_bytes=60 * MIB),
        name="pack",
    )(plan.where, k, v, q)
    return dict(zip(shifts, outs[:count])), dict(zip(shifts, outs[count:]))


def join_kernel(*refs):
    out_ref = refs[-1]
    first = 0
    for in_ref in refs[:-1]:
        count = in_ref.shape[1]
        out_ref[:, first : first + count, :] = in_ref[...]
        first += count


def join(pieces):
    if len(pieces) == 1:
        return pieces[0]
    shape = (pieces[0].shape[0], sum(piece.shape[1] for piece in pieces), pieces[0].shape[2])
    vmem = pl.BlockSpec(memory_space=pltpu.VMEM)
    return pl.pallas_call(
        join_kernel,
        out_shape=jax.ShapeDtypeStruct(shape, BF16),
        in_specs=[vmem] * len(pieces),
        out_specs=vmem,
        compiler_params=pltpu.CompilerParams(vmem_limit_bytes=20 * MIB),
        cost_estimate=pl.CostEstimate(flops=0, bytes_accessed=0, transcendentals=0),
        name="join",
    )(*pieces)


def fetch_kernel(first, w_ref, out_ref, sem):
    depth = out_ref.shape[0] // sem.shape[0]
    copies = []
    for index in range(sem.shape[0]):
        copies.append(
            pltpu.make_async_copy(
                w_ref.at[pl.ds(first + index * depth, depth), :],
                out_ref.at[pl.ds(index * depth, depth), :],
                sem.at[index],
            )
        )
        copies[-1].start()
    for copy in copies:
        copy.wait()


def fetch(w, first, count):
    return pl.pallas_call(
        functools.partial(fetch_kernel, first),
        out_shape=jax.ShapeDtypeStruct((count, w.shape[1]), w.dtype),
        in_specs=[pl.BlockSpec(memory_space=pl.ANY)],
        out_specs=pl.BlockSpec(memory_space=pltpu.VMEM),
        scratch_shapes=[pltpu.SemaphoreType.DMA((2,))],
        compiler_params=pltpu.CompilerParams(vmem_limit_bytes=38 * MIB),
        cost_estimate=pl.CostEstimate(
            flops=0, bytes_accessed=4 * count * w.shape[1], transcendentals=0
        ),
        name="fetch_weight",
    )(w)


def attend_kernel(q_count, kv_count, heads, tile_blocks, *refs):
    q_refs, kv_refs = refs[:q_count], refs[q_count : q_count + kv_count]
    out_refs, scores = refs[q_count + kv_count : -1], refs[-1]
    scale = math.log2(math.e) / math.sqrt(HD)
    rows = q_refs[0].shape[0]
    per_out = q_count // len(out_refs)
    for head in range(heads):
        cols = slice(head * HD, (head + 1) * HD)
        for at in range(0, q_count, tile_blocks):
            q = jnp.concatenate([ref[:, cols] for ref in q_refs[at : at + tile_blocks]], axis=0)
            peak = None
            key = 0
            for kv_ref in kv_refs:
                keys = kv_ref.shape[1]
                part = lax.dot_general(
                    q, kv_ref[0, :, cols], (((1,), (1,)), ((), ())), preferred_element_type=F32
                )
                scores[head % 2, :, pl.ds(key, keys)] = part
                top = jnp.max(part, axis=-1, keepdims=True)
                peak = top if peak is None else jnp.maximum(peak, top)
                key += keys
            peak = peak * scale
            weighted = jnp.zeros((q.shape[0], HD), F32)
            total = jnp.zeros((q.shape[0], 1), F32)
            key = 0
            for kv_ref in kv_refs:
                keys = kv_ref.shape[1]
                probs = jnp.exp2(scores[head % 2, :, pl.ds(key, keys)] * scale - peak).astype(BF16)
                total += jnp.sum(probs.astype(F32), axis=-1, keepdims=True)
                weighted += jnp.dot(probs, kv_ref[1, :, cols], preferred_element_type=F32)
                key += keys
            attended = (weighted / total).astype(BF16)
            for index in range(at, at + tile_blocks):
                place = slice(index % per_out * rows, (index % per_out + 1) * rows)
                block = attended[(index - at) * rows : (index - at + 1) * rows]
                out_refs[index // per_out][place, cols] = block


def attend(plan, queries, kvs, name):
    rows = queries[0].shape[0]
    count = len(queries)
    keys = sum(kv.shape[1] for kv in kvs)
    tile_blocks = math.gcd(count, max(256 // rows, 1))
    vmem = pl.BlockSpec(memory_space=pltpu.VMEM)
    return list(
        pl.pallas_call(
            functools.partial(attend_kernel, count, len(kvs), plan.heads, tile_blocks),
            out_shape=[jax.ShapeDtypeStruct((count // plan.G * rows, plan.cols), BF16)] * plan.G,
            in_specs=[vmem] * (count + len(kvs)),
            out_specs=[vmem] * plan.G,
            scratch_shapes=[pltpu.VMEM((2, tile_blocks * rows, keys), F32)],
            compiler_params=pltpu.CompilerParams(vmem_limit_bytes=20 * MIB),
            cost_estimate=pl.CostEstimate(
                flops=4 * count * rows * keys * plan.cols,
                bytes_accessed=4 * plan.cols * (count * rows + keys),
                transcendentals=count * rows * keys * plan.heads,
            ),
            name=name,
        )(*queries, *kvs)
    )


def project_kernel(plan, weight_count, where_ref, *refs):
    parts, w_refs, (out_ref, mixed) = (
        refs[: plan.G],
        refs[plan.G : plan.G + weight_count],
        refs[plan.G + weight_count :],
    )
    own_g = where_ref[0] // (plan.R * plan.T)
    for dg, part in enumerate(parts):
        place = lax.rem(own_g + dg, plan.G) * plan.cols
        mixed[:, pl.ds(pl.multiple_of(place, HD), plan.cols)] = part[...]
    total = None
    depth = 0
    for w_ref in w_refs:
        share = jnp.dot(
            mixed[:, depth : depth + w_ref.shape[0]],
            w_ref[...],
            preferred_element_type=F32,
        )
        total = share if total is None else total + share
        depth += w_ref.shape[0]
    out_ref[...] = total.astype(BF16)


def project(plan, parts, weights, flops, name):
    rows = parts[0].shape[0]
    depth = sum(w.shape[0] for w in weights)
    vmem = pl.BlockSpec(memory_space=pltpu.VMEM)
    return pl.pallas_call(
        functools.partial(project_kernel, plan, len(weights)),
        out_shape=jax.ShapeDtypeStruct((rows, weights[0].shape[1]), BF16),
        in_specs=[pl.BlockSpec(memory_space=pltpu.SMEM)] + [vmem] * (len(parts) + len(weights)),
        out_specs=vmem,
        scratch_shapes=[pltpu.VMEM((rows, depth), BF16)],
        compiler_params=pltpu.CompilerParams(vmem_limit_bytes=20 * MIB),
        cost_estimate=pl.CostEstimate(flops=flops, bytes_accessed=flops // 64, transcendentals=0),
        name=name,
    )(plan.where, *parts, *weights)


def add_kernel(*refs):
    total = refs[0][...].astype(F32)
    for in_ref in refs[1:-1]:
        total += in_ref[...].astype(F32)
    refs[-1][...] = total.astype(BF16)


def add_up(kept, received):
    vmem = pl.BlockSpec(memory_space=pltpu.VMEM)
    return pl.pallas_call(
        add_kernel,
        out_shape=jax.ShapeDtypeStruct(kept.shape, BF16),
        in_specs=[vmem] * (1 + len(received)),
        out_specs=vmem,
        compiler_params=pltpu.CompilerParams(vmem_limit_bytes=20 * MIB),
        cost_estimate=pl.CostEstimate(flops=0, bytes_accessed=0, transcendentals=0),
        name="add_shares",
    )(kept, *received)


def local(query_vectors, key_vectors, value_vectors, out_weight):
    plan = Plan(query_vectors.shape[1] // HD)
    G, R, T = plan.G, plan.R, plan.T
    rows = query_vectors.shape[0]

    shifts = [(dg, dt) for dg in range(G) for dt in range(T)]
    blocks, asked = pack(plan, shifts, key_vectors, value_vectors, query_vectors)

    def spread(shifts, blocks):
        return [
            blocks[shift] if shift == (0, 0) else plan.move(blocks[shift], *shift)
            for shift in shifts
        ]

    wide = R % 2 == 0 and R <= 8

    def across(own):
        shifts = range(1, R // 2 if wide else 1)
        return [own] + [plan.move(own, r_map=lambda r, s=s: (r + 2 * s) % R) for s in shifts]

    half = max(G // 2, 1) * T
    depth = out_weight.shape[0] // 2
    nears = [across(jnp.concatenate(spread(shifts[:half], blocks), axis=1))]
    first_own, weight = lax.optimization_barrier((nears[0][0], out_weight))
    nears[0][0] = first_own
    upper = fetch(weight, 0, depth)
    if half < len(shifts):
        arrived = spread(shifts[half:], blocks)
        arrived, upper = lax.optimization_barrier((arrived, upper))
        nears.append(across(join(arrived)))

    nears[-1][0], asked = lax.optimization_barrier((nears[-1][0], asked))
    others = spread([(dg, dt) for dg in range(G) for dt in range(1, T)], asked)
    kept = spread([(dg, 0) for dg in range(G)], asked)
    nears, others, kept, upper, weight = lax.optimization_barrier(
        (nears, others, kept, upper, weight)
    )
    lower = fetch(weight, depth, depth)
    kvs = []
    for near in nears:
        near = join(near)
        if wide:
            kvs += [near, plan.move(near, r_map=lambda r: r ^ 1)]
        else:
            groups = [[g * R + r for r in range(R)] for g in range(G)]
            kvs.append(lax.all_gather(near, "ctx", axis=1, tiled=True, axis_index_groups=groups))

    def give_back(attended):
        return [attended[0]] + [plan.move(attended[dg], -dg) for dg in range(1, G)]

    others, lower = lax.optimization_barrier((others, lower))
    weights = [upper, lower]
    others = attend(plan, others, kvs, "attend_others")
    kept, others[0] = lax.optimization_barrier((kept, others[0]))
    kept = attend(plan, kept, kvs, "attend_own")
    parts = give_back(others)
    parts, kept = lax.optimization_barrier((parts, kept))
    flops = 2 * (T - 1) * rows * weight.shape[0] * weight.shape[1]
    sent = project(plan, parts, weights, flops, "project_others")
    kept, sent = lax.optimization_barrier((kept, sent))
    received = [
        plan.move(sent[(dt - 1) * rows : dt * rows], 0, -dt) for dt in range(1, T)
    ]
    kept = project(plan, give_back(kept), weights, 0, "project_own")
    return add_up(kept, received)


def solution(mesh):
    spec = P(AXES, None)
    return jax.shard_map(
        local,
        mesh=mesh,
        in_specs=(spec, spec, spec, P("tp", None)),
        out_specs=spec,
        check_vma=False,
    )
```

```python
import functools
import math

import jax
import jax.numpy as jnp
from jax import lax
from jax.experimental import pallas as pl
from jax.experimental.pallas import tpu as pltpu
from jax.sharding import PartitionSpec as P

HD = 128
AXES = ("ctx", "tp")
MIB = 1024 * 1024
F32 = jnp.float32
BF16 = jnp.bfloat16


class Plan:
    def __init__(self, head_count):
        self.C = lax.axis_size("ctx")
        self.T = lax.axis_size("tp")
        self.G = math.gcd(head_count // self.T, self.C)
        self.R = self.C // self.G
        self.heads = head_count // (self.T * self.G)
        self.cols = self.heads * HD
        self.where = jnp.reshape(lax.axis_index(AXES), (1,)).astype(jnp.int32)

    def flat(self, g, r, t):
        return (g % self.G * self.R + r) * self.T + t % self.T

    def move(self, x, dg=0, dt=0, r_map=lambda r: r):
        pairs = [
            (self.flat(g, r, t), self.flat(g + dg, r_map(r), t + dt))
            for g in range(self.G)
            for r in range(self.R)
            for t in range(self.T)
        ]
        return lax.ppermute(x, AXES, pairs)


def pack_kernel(plan, pieces, where_ref, k_ref, v_ref, q_ref, *refs):
    outs, held, in_sem, out_sem = refs[:-3], *refs[-3:]
    G, R, T, cols = plan.G, plan.R, plan.T, plan.cols
    g, t = where_ref[0] // (R * T), lax.rem(where_ref[0], T)
    in_refs = (k_ref, v_ref, q_ref)
    groups = []
    place = 0
    for (dg, dt), slots in pieces:
        start = (lax.rem(t + dt, T) * G + lax.rem(g + dg, G)) * cols
        columns = pl.ds(pl.multiple_of(start, HD), cols)
        groups.append([])
        for slot in slots:
            copy = pltpu.make_async_copy(
                in_refs[slot].at[:, columns], held.at[place], in_sem.at[place]
            )
            copy.start()
            groups[-1].append(copy)
            place += 1
    outward = []
    place = 0
    for group, out_ref in zip(groups, outs):
        for copy in group:
            copy.wait()
        source = held.at[pl.ds(place, len(group))]
        outward.append(pltpu.make_async_copy(source, out_ref, out_sem.at[len(outward)]))
        outward[-1].start()
        place += len(group)
    for copy in outward:
        copy.wait()


def pack(plan, pieces, k, v, q):
    rows = q.shape[0]
    total = sum(len(slots) for shift, slots in pieces)
    outs = pl.pallas_call(
        functools.partial(pack_kernel, plan, pieces),
        out_shape=[
            jax.ShapeDtypeStruct((len(slots), rows, plan.cols), BF16) for shift, slots in pieces
        ],
        in_specs=[pl.BlockSpec(memory_space=pltpu.SMEM)] + [pl.BlockSpec(memory_space=pl.ANY)] * 3,
        out_specs=[pl.BlockSpec(memory_space=pl.ANY)] * len(pieces),
        scratch_shapes=[
            pltpu.VMEM((total, rows, plan.cols), BF16),
            pltpu.SemaphoreType.DMA((total,)),
            pltpu.SemaphoreType.DMA((len(pieces),)),
        ],
        compiler_params=pltpu.CompilerParams(vmem_limit_bytes=60 * MIB),
        name="pack",
    )(plan.where, k, v, q)
    return dict(zip(pieces, outs))


def join_kernel(*refs):
    out_ref = refs[-1]
    first = 0
    for in_ref in refs[:-1]:
        count = in_ref.shape[1]
        out_ref[:, first : first + count, :] = in_ref[0:2]
        first += count


def join(pieces):
    if len(pieces) == 1:
        return pieces[0]
    shape = (2, sum(piece.shape[1] for piece in pieces), pieces[0].shape[2])
    vmem = pl.BlockSpec(memory_space=pltpu.VMEM)
    return pl.pallas_call(
        join_kernel,
        out_shape=jax.ShapeDtypeStruct(shape, BF16),
        in_specs=[vmem] * len(pieces),
        out_specs=vmem,
        compiler_params=pltpu.CompilerParams(vmem_limit_bytes=20 * MIB),
        cost_estimate=pl.CostEstimate(flops=0, bytes_accessed=0, transcendentals=0),
        name="join",
    )(*pieces)


def fetch_kernel(first, w_ref, out_ref, sem):
    depth = out_ref.shape[0] // sem.shape[0]
    copies = []
    for index in range(sem.shape[0]):
        copies.append(
            pltpu.make_async_copy(
                w_ref.at[pl.ds(first + index * depth, depth), :],
                out_ref.at[pl.ds(index * depth, depth), :],
                sem.at[index],
            )
        )
        copies[-1].start()
    for copy in copies:
        copy.wait()


def fetch(w, first, count):
    return pl.pallas_call(
        functools.partial(fetch_kernel, first),
        out_shape=jax.ShapeDtypeStruct((count, w.shape[1]), w.dtype),
        in_specs=[pl.BlockSpec(memory_space=pl.ANY)],
        out_specs=pl.BlockSpec(memory_space=pltpu.VMEM),
        scratch_shapes=[pltpu.SemaphoreType.DMA((2,))],
        compiler_params=pltpu.CompilerParams(vmem_limit_bytes=38 * MIB),
        cost_estimate=pl.CostEstimate(
            flops=0, bytes_accessed=4 * count * w.shape[1], transcendentals=0
        ),
        name="fetch_weight",
    )(w)


def attend_kernel(q_count, kv_count, heads, tile_blocks, *refs):
    q_refs, kv_refs = refs[:q_count], refs[q_count : q_count + kv_count]
    out_refs, scores = refs[q_count + kv_count : -1], refs[-1]
    scale = math.log2(math.e) / math.sqrt(HD)
    rows = q_refs[0].shape[1]
    per_out = q_count // len(out_refs)
    for head in range(heads):
        cols = slice(head * HD, (head + 1) * HD)
        for at in range(0, q_count, tile_blocks):
            q = jnp.concatenate(
                [ref[ref.shape[0] - 1, :, cols] for ref in q_refs[at : at + tile_blocks]], axis=0
            )
            peak = None
            key = 0
            for kv_ref in kv_refs:
                keys = kv_ref.shape[1]
                part = lax.dot_general(
                    q, kv_ref[0, :, cols], (((1,), (1,)), ((), ())), preferred_element_type=F32
                )
                scores[head % 2, :, pl.ds(key, keys)] = part
                top = jnp.max(part, axis=-1, keepdims=True)
                peak = top if peak is None else jnp.maximum(peak, top)
                key += keys
            peak = peak * scale
            weighted = jnp.zeros((q.shape[0], HD), F32)
            total = jnp.zeros((q.shape[0], 1), F32)
            key = 0
            for kv_ref in kv_refs:
                keys = kv_ref.shape[1]
                probs = jnp.exp2(scores[head % 2, :, pl.ds(key, keys)] * scale - peak).astype(BF16)
                total += jnp.sum(probs.astype(F32), axis=-1, keepdims=True)
                weighted += jnp.dot(probs, kv_ref[1, :, cols], preferred_element_type=F32)
                key += keys
            attended = (weighted / total).astype(BF16)
            for index in range(at, at + tile_blocks):
                place = slice(index % per_out * rows, (index % per_out + 1) * rows)
                block = attended[(index - at) * rows : (index - at + 1) * rows]
                out_refs[index // per_out][place, cols] = block


def attend(plan, queries, kvs, name):
    rows = queries[0].shape[1]
    count = len(queries)
    keys = sum(kv.shape[1] for kv in kvs)
    tile_blocks = math.gcd(count, max(256 // rows, 1))
    vmem = pl.BlockSpec(memory_space=pltpu.VMEM)
    return list(
        pl.pallas_call(
            functools.partial(attend_kernel, count, len(kvs), plan.heads, tile_blocks),
            out_shape=[jax.ShapeDtypeStruct((count // plan.G * rows, plan.cols), BF16)] * plan.G,
            in_specs=[vmem] * (count + len(kvs)),
            out_specs=[vmem] * plan.G,
            scratch_shapes=[pltpu.VMEM((2, tile_blocks * rows, keys), F32)],
            compiler_params=pltpu.CompilerParams(vmem_limit_bytes=20 * MIB),
            cost_estimate=pl.CostEstimate(
                flops=4 * count * rows * keys * plan.cols,
                bytes_accessed=4 * plan.cols * (count * rows + keys),
                transcendentals=count * rows * keys * plan.heads,
            ),
            name=name,
        )(*queries, *kvs)
    )


def project_kernel(plan, weight_count, where_ref, *refs):
    parts, w_refs, (out_ref, mixed) = (
        refs[: plan.G],
        refs[plan.G : plan.G + weight_count],
        refs[plan.G + weight_count :],
    )
    own_g = where_ref[0] // (plan.R * plan.T)
    for dg, part in enumerate(parts):
        place = lax.rem(own_g + dg, plan.G) * plan.cols
        mixed[:, pl.ds(pl.multiple_of(place, HD), plan.cols)] = part[...]
    total = None
    depth = 0
    for w_ref in w_refs:
        share = jnp.dot(
            mixed[:, depth : depth + w_ref.shape[0]],
            w_ref[...],
            preferred_element_type=F32,
        )
        total = share if total is None else total + share
        depth += w_ref.shape[0]
    out_ref[...] = total.astype(BF16)


def project(plan, parts, weights, flops, name):
    rows = parts[0].shape[0]
    depth = sum(w.shape[0] for w in weights)
    vmem = pl.BlockSpec(memory_space=pltpu.VMEM)
    return pl.pallas_call(
        functools.partial(project_kernel, plan, len(weights)),
        out_shape=jax.ShapeDtypeStruct((rows, weights[0].shape[1]), BF16),
        in_specs=[pl.BlockSpec(memory_space=pltpu.SMEM)] + [vmem] * (len(parts) + len(weights)),
        out_specs=vmem,
        scratch_shapes=[pltpu.VMEM((rows, depth), BF16)],
        compiler_params=pltpu.CompilerParams(vmem_limit_bytes=20 * MIB),
        cost_estimate=pl.CostEstimate(flops=flops, bytes_accessed=flops // 64, transcendentals=0),
        name=name,
    )(plan.where, *parts, *weights)


def add_kernel(*refs):
    total = refs[0][...].astype(F32)
    for in_ref in refs[1:-1]:
        total += in_ref[...].astype(F32)
    refs[-1][...] = total.astype(BF16)


def add_up(kept, received):
    vmem = pl.BlockSpec(memory_space=pltpu.VMEM)
    return pl.pallas_call(
        add_kernel,
        out_shape=jax.ShapeDtypeStruct(kept.shape, BF16),
        in_specs=[vmem] * (1 + len(received)),
        out_specs=vmem,
        compiler_params=pltpu.CompilerParams(vmem_limit_bytes=20 * MIB),
        cost_estimate=pl.CostEstimate(flops=0, bytes_accessed=0, transcendentals=0),
        name="add_shares",
    )(kept, *received)


def local(query_vectors, key_vectors, value_vectors, out_weight):
    plan = Plan(query_vectors.shape[1] // HD)
    G, R, T = plan.G, plan.R, plan.T
    rows = query_vectors.shape[0]

    shifts = [(dg, dt) for dg in range(G) for dt in range(T)]
    near_count = max(G // 2, 1) * T
    near = [(shift, (0, 1, 2)) for shift in shifts[:near_count]]
    far = [(shift, (0, 1)) for shift in shifts[near_count:]]
    late = [(shift, (2,)) for shift in shifts[near_count:]]
    blocks = pack(plan, near + far + late, key_vectors, value_vectors, query_vectors)

    def spread(piece):
        shift = piece[0]
        return blocks[piece] if shift == (0, 0) else plan.move(blocks[piece], *shift)

    wide = R % 2 == 0 and R <= 8

    def across(own):
        shifts = range(1, R // 2 if wide else 1)
        return [own] + [plan.move(own, r_map=lambda r, s=s: (r + 2 * s) % R) for s in shifts]

    depth = out_weight.shape[0] // 2
    arrived = [spread(piece) for piece in near]
    queries = {piece[0]: block for piece, block in zip(near, arrived)}
    gathered = [across(jnp.concatenate([block[:2] for block in arrived], axis=1))]
    gathered[0][0], weight = lax.optimization_barrier((gathered[0][0], out_weight))
    upper = fetch(weight, 0, depth)
    if far:
        arrived = [spread(piece) for piece in far]
        arrived, upper = lax.optimization_barrier((arrived, upper))
        gathered.append(across(join(arrived)))
        asked = [blocks[piece] for piece in late]
        gathered[1][0], asked, weight = lax.optimization_barrier((gathered[1][0], asked, weight))
        blocks.update(zip(late, asked))
        queries.update({piece[0]: spread(piece) for piece in late})
    lower = fetch(weight, depth, depth)
    others = [queries[dg, dt] for dg in range(G) for dt in range(1, T)]
    kept = [queries[dg, 0] for dg in range(G)]
    gathered, others, kept, upper, lower = lax.optimization_barrier(
        (gathered, others, kept, upper, lower)
    )
    gathered = [join(pieces) for pieces in gathered]
    kvs = []
    for pieces in gathered:
        if wide:
            kvs += [pieces, plan.move(pieces, r_map=lambda r: r ^ 1)]
        else:
            groups = [[g * R + r for r in range(R)] for g in range(G)]
            kvs.append(lax.all_gather(pieces, "ctx", axis=1, tiled=True, axis_index_groups=groups))

    def give_back(attended):
        return [attended[0]] + [plan.move(attended[dg], -dg) for dg in range(1, G)]

    others = attend(plan, others, kvs, "attend_others")
    kept, others[0] = lax.optimization_barrier((kept, others[0]))
    kept = attend(plan, kept, kvs, "attend_own")
    parts = give_back(others)
    parts, kept = lax.optimization_barrier((parts, kept))
    flops = 2 * (T - 1) * rows * weight.shape[0] * weight.shape[1]
    sent = project(plan, parts, [upper, lower], flops, "project_others")
    kept, sent = lax.optimization_barrier((kept, sent))
    received = [
        plan.move(sent[(dt - 1) * rows : dt * rows], 0, -dt) for dt in range(1, T)
    ]
    kept = project(plan, give_back(kept), [upper, lower], 0, "project_own")
    return add_up(kept, received)


def solution(mesh):
    spec = P(AXES, None)
    return jax.shard_map(
        local,
        mesh=mesh,
        in_specs=(spec, spec, spec, P("tp", None)),
        out_specs=spec,
        check_vma=False,
    )
```

```python
import functools
import math

import jax
import jax.numpy as jnp
from jax import lax
from jax.experimental import pallas as pl
from jax.experimental.pallas import tpu as pltpu
from jax.sharding import PartitionSpec as P

HD = 128
AXES = ("ctx", "tp")
MIB = 1024 * 1024
F32 = jnp.float32
BF16 = jnp.bfloat16


class Plan:
    def __init__(self, head_count):
        self.C = lax.axis_size("ctx")
        self.T = lax.axis_size("tp")
        self.G = math.gcd(head_count // self.T, self.C)
        self.R = self.C // self.G
        self.heads = head_count // (self.T * self.G)
        self.cols = self.heads * HD
        self.where = jnp.reshape(lax.axis_index(AXES), (1,)).astype(jnp.int32)

    def flat(self, g, r, t):
        return (g % self.G * self.R + r) * self.T + t % self.T

    def move(self, x, dg=0, dt=0, r_map=lambda r: r):
        pairs = [
            (self.flat(g, r, t), self.flat(g + dg, r_map(r), t + dt))
            for g in range(self.G)
            for r in range(self.R)
            for t in range(self.T)
        ]
        return lax.ppermute(x, AXES, pairs)


def pack_kernel(plan, pieces, where_ref, k_ref, v_ref, q_ref, *refs):
    outs, held, in_sem, out_sem = refs[:-3], *refs[-3:]
    G, R, T, cols = plan.G, plan.R, plan.T, plan.cols
    g, t = where_ref[0] // (R * T), lax.rem(where_ref[0], T)
    in_refs = (k_ref, v_ref, q_ref)
    groups = []
    place = 0
    for (dg, dt), slots in pieces:
        start = (lax.rem(t + dt, T) * G + lax.rem(g + dg, G)) * cols
        columns = pl.ds(pl.multiple_of(start, HD), cols)
        groups.append([])
        for slot in slots:
            copy = pltpu.make_async_copy(
                in_refs[slot].at[:, columns], held.at[place], in_sem.at[place]
            )
            copy.start()
            groups[-1].append(copy)
            place += 1
    outward = []
    place = 0
    for group, out_ref in zip(groups, outs):
        for copy in group:
            copy.wait()
        source = held.at[pl.ds(place, len(group))]
        outward.append(pltpu.make_async_copy(source, out_ref, out_sem.at[len(outward)]))
        outward[-1].start()
        place += len(group)
    for copy in outward:
        copy.wait()


def pack(plan, pieces, k, v, q):
    rows = q.shape[0]
    total = sum(len(slots) for shift, slots in pieces)
    outs = pl.pallas_call(
        functools.partial(pack_kernel, plan, pieces),
        out_shape=[
            jax.ShapeDtypeStruct((len(slots), rows, plan.cols), BF16) for shift, slots in pieces
        ],
        in_specs=[pl.BlockSpec(memory_space=pltpu.SMEM)] + [pl.BlockSpec(memory_space=pl.ANY)] * 3,
        out_specs=[pl.BlockSpec(memory_space=pl.ANY)] * len(pieces),
        scratch_shapes=[
            pltpu.VMEM((total, rows, plan.cols), BF16),
            pltpu.SemaphoreType.DMA((total,)),
            pltpu.SemaphoreType.DMA((len(pieces),)),
        ],
        compiler_params=pltpu.CompilerParams(vmem_limit_bytes=60 * MIB),
        name="pack",
    )(plan.where, k, v, q)
    return dict(zip(pieces, outs))


def join_kernel(*refs):
    out_ref = refs[-1]
    first = 0
    for in_ref in refs[:-1]:
        count = in_ref.shape[1]
        out_ref[:, first : first + count, :] = in_ref[0:2]
        first += count


def join(pieces):
    if len(pieces) == 1:
        return pieces[0]
    shape = (2, sum(piece.shape[1] for piece in pieces), pieces[0].shape[2])
    vmem = pl.BlockSpec(memory_space=pltpu.VMEM)
    return pl.pallas_call(
        join_kernel,
        out_shape=jax.ShapeDtypeStruct(shape, BF16),
        in_specs=[vmem] * len(pieces),
        out_specs=vmem,
        compiler_params=pltpu.CompilerParams(vmem_limit_bytes=20 * MIB),
        cost_estimate=pl.CostEstimate(flops=0, bytes_accessed=0, transcendentals=0),
        name="join",
    )(*pieces)


def fetch_kernel(first, w_ref, out_ref, sem):
    depth = out_ref.shape[0] // sem.shape[0]
    copies = []
    for index in range(sem.shape[0]):
        copies.append(
            pltpu.make_async_copy(
                w_ref.at[pl.ds(first + index * depth, depth), :],
                out_ref.at[pl.ds(index * depth, depth), :],
                sem.at[index],
            )
        )
        copies[-1].start()
    for copy in copies:
        copy.wait()


def fetch(w, first, count):
    return pl.pallas_call(
        functools.partial(fetch_kernel, first),
        out_shape=jax.ShapeDtypeStruct((count, w.shape[1]), w.dtype),
        in_specs=[pl.BlockSpec(memory_space=pl.ANY)],
        out_specs=pl.BlockSpec(memory_space=pltpu.VMEM),
        scratch_shapes=[pltpu.SemaphoreType.DMA((2,))],
        compiler_params=pltpu.CompilerParams(vmem_limit_bytes=38 * MIB),
        cost_estimate=pl.CostEstimate(
            flops=0, bytes_accessed=4 * count * w.shape[1], transcendentals=0
        ),
        name="fetch_weight",
    )(w)


def attend_kernel(q_count, kv_count, heads, tile_blocks, *refs):
    q_refs, kv_refs = refs[:q_count], refs[q_count : q_count + kv_count]
    out_refs, scores = refs[q_count + kv_count : -1], refs[-1]
    scale = math.log2(math.e) / math.sqrt(HD)
    rows = q_refs[0].shape[1]
    per_out = q_count // len(out_refs)
    for head in range(heads):
        cols = slice(head * HD, (head + 1) * HD)
        for at in range(0, q_count, tile_blocks):
            q = jnp.concatenate(
                [ref[ref.shape[0] - 1, :, cols] for ref in q_refs[at : at + tile_blocks]], axis=0
            )
            peak = None
            key = 0
            for kv_ref in kv_refs:
                keys = kv_ref.shape[1]
                part = lax.dot_general(
                    q, kv_ref[0, :, cols], (((1,), (1,)), ((), ())), preferred_element_type=F32
                )
                scores[head % 2, :, pl.ds(key, keys)] = part
                top = jnp.max(part, axis=-1, keepdims=True)
                peak = top if peak is None else jnp.maximum(peak, top)
                key += keys
            peak = peak * scale
            weighted = jnp.zeros((q.shape[0], HD), F32)
            total = jnp.zeros((q.shape[0], 1), F32)
            key = 0
            for kv_ref in kv_refs:
                keys = kv_ref.shape[1]
                probs = jnp.exp2(scores[head % 2, :, pl.ds(key, keys)] * scale - peak).astype(BF16)
                total += jnp.sum(probs.astype(F32), axis=-1, keepdims=True)
                weighted += jnp.dot(probs, kv_ref[1, :, cols], preferred_element_type=F32)
                key += keys
            attended = (weighted / total).astype(BF16)
            for index in range(at, at + tile_blocks):
                place = slice(index % per_out * rows, (index % per_out + 1) * rows)
                block = attended[(index - at) * rows : (index - at + 1) * rows]
                out_refs[index // per_out][place, cols] = block


def attend(plan, queries, kvs, name):
    rows = queries[0].shape[1]
    count = len(queries)
    keys = sum(kv.shape[1] for kv in kvs)
    tile_blocks = math.gcd(count, max(256 // rows, 1))
    vmem = pl.BlockSpec(memory_space=pltpu.VMEM)
    return list(
        pl.pallas_call(
            functools.partial(attend_kernel, count, len(kvs), plan.heads, tile_blocks),
            out_shape=[jax.ShapeDtypeStruct((count // plan.G * rows, plan.cols), BF16)] * plan.G,
            in_specs=[vmem] * (count + len(kvs)),
            out_specs=[vmem] * plan.G,
            scratch_shapes=[pltpu.VMEM((2, tile_blocks * rows, keys), F32)],
            compiler_params=pltpu.CompilerParams(vmem_limit_bytes=20 * MIB),
            cost_estimate=pl.CostEstimate(
                flops=4 * count * rows * keys * plan.cols,
                bytes_accessed=4 * plan.cols * (count * rows + keys),
                transcendentals=count * rows * keys * plan.heads,
            ),
            name=name,
        )(*queries, *kvs)
    )


def project_kernel(plan, weight_count, where_ref, *refs):
    parts, w_refs, (out_ref, mixed) = (
        refs[: plan.G],
        refs[plan.G : plan.G + weight_count],
        refs[plan.G + weight_count :],
    )
    own_g = where_ref[0] // (plan.R * plan.T)
    for dg, part in enumerate(parts):
        place = lax.rem(own_g + dg, plan.G) * plan.cols
        mixed[:, pl.ds(pl.multiple_of(place, HD), plan.cols)] = part[...]
    total = None
    depth = 0
    for w_ref in w_refs:
        share = jnp.dot(
            mixed[:, depth : depth + w_ref.shape[0]],
            w_ref[...],
            preferred_element_type=F32,
        )
        total = share if total is None else total + share
        depth += w_ref.shape[0]
    out_ref[...] = total.astype(BF16)


def project(plan, parts, weights, flops, name):
    rows = parts[0].shape[0]
    depth = sum(w.shape[0] for w in weights)
    vmem = pl.BlockSpec(memory_space=pltpu.VMEM)
    return pl.pallas_call(
        functools.partial(project_kernel, plan, len(weights)),
        out_shape=jax.ShapeDtypeStruct((rows, weights[0].shape[1]), BF16),
        in_specs=[pl.BlockSpec(memory_space=pltpu.SMEM)] + [vmem] * (len(parts) + len(weights)),
        out_specs=vmem,
        scratch_shapes=[pltpu.VMEM((rows, depth), BF16)],
        compiler_params=pltpu.CompilerParams(vmem_limit_bytes=20 * MIB),
        cost_estimate=pl.CostEstimate(flops=flops, bytes_accessed=flops // 64, transcendentals=0),
        name=name,
    )(plan.where, *parts, *weights)


def add_kernel(*refs):
    total = refs[0][...].astype(F32)
    for in_ref in refs[1:-1]:
        total += in_ref[...].astype(F32)
    refs[-1][...] = total.astype(BF16)


def add_up(kept, received):
    vmem = pl.BlockSpec(memory_space=pltpu.VMEM)
    return pl.pallas_call(
        add_kernel,
        out_shape=jax.ShapeDtypeStruct(kept.shape, BF16),
        in_specs=[vmem] * (1 + len(received)),
        out_specs=vmem,
        compiler_params=pltpu.CompilerParams(vmem_limit_bytes=20 * MIB),
        cost_estimate=pl.CostEstimate(flops=0, bytes_accessed=0, transcendentals=0),
        name="add_shares",
    )(kept, *received)


def local(query_vectors, key_vectors, value_vectors, out_weight):
    plan = Plan(query_vectors.shape[1] // HD)
    G, R, T = plan.G, plan.R, plan.T
    rows = query_vectors.shape[0]

    shifts = [(dg, dt) for dg in range(G) for dt in range(T)]
    near_count = max(G // 2, 1) * T
    near = [(shift, (0, 1, 2)) for shift in shifts[:near_count]]
    far = [(shift, (0, 1)) for shift in shifts[near_count:]]
    late = [(shift, (2,)) for shift in shifts[near_count:]]
    blocks = pack(plan, near + far + late, key_vectors, value_vectors, query_vectors)

    def spread(piece):
        shift = piece[0]
        return blocks[piece] if shift == (0, 0) else plan.move(blocks[piece], *shift)

    wide = R % 2 == 0 and R <= 8

    def across(own):
        shifts = range(1, R // 2 if wide else 1)
        return [own] + [plan.move(own, r_map=lambda r, s=s: (r + 2 * s) % R) for s in shifts]

    def exchange(pieces):
        pieces = join(pieces)
        if wide:
            return [pieces, plan.move(pieces, r_map=lambda r: r ^ 1)]
        groups = [[g * R + r for r in range(R)] for g in range(G)]
        return [lax.all_gather(pieces, "ctx", axis=1, tiled=True, axis_index_groups=groups)]

    depth = out_weight.shape[0]
    edges = [0, depth // 6, depth // 2, depth]
    arrived = [spread(piece) for piece in near]
    queries = {piece[0]: block for piece, block in zip(near, arrived)}
    gathered = [across(jnp.concatenate([block[:2] for block in arrived], axis=1))]
    gathered[0][0], weight = lax.optimization_barrier((gathered[0][0], out_weight))
    weights = [fetch(weight, 0, edges[1])]
    if far:
        arrived = [spread(piece) for piece in far]
        arrived, weights[0] = lax.optimization_barrier((arrived, weights[0]))
        gathered.append(across(join(arrived)))
        asked = [blocks[piece] for piece in late]
        gathered[1][0], asked, weight = lax.optimization_barrier((gathered[1][0], asked, weight))
        blocks.update(zip(late, asked))
        queries.update({piece[0]: spread(piece) for piece in late})
    weights.append(fetch(weight, edges[1], edges[2] - edges[1]))
    others = [queries[dg, dt] for dg in range(G) for dt in range(1, T)]
    kept = [queries[dg, 0] for dg in range(G)]
    gathered, others, kept, weights, weight = lax.optimization_barrier(
        (gathered, others, kept, weights, weight)
    )
    kvs = [kv for pieces in gathered for kv in exchange(pieces)]
    weights = list(weights) + [fetch(weight, edges[2], edges[3] - edges[2])]
    others, weights[2] = lax.optimization_barrier((others, weights[2]))

    def give_back(attended):
        return [attended[0]] + [plan.move(attended[dg], -dg) for dg in range(1, G)]

    others = attend(plan, others, kvs, "attend_others")
    kept, others[0] = lax.optimization_barrier((kept, others[0]))
    kept = attend(plan, kept, kvs, "attend_own")
    parts = give_back(others)
    parts, kept = lax.optimization_barrier((parts, kept))
    flops = 2 * (T - 1) * rows * weight.shape[0] * weight.shape[1]
    sent = project(plan, parts, weights, flops, "project_others")
    kept, sent = lax.optimization_barrier((kept, sent))
    received = [
        plan.move(sent[(dt - 1) * rows : dt * rows], 0, -dt) for dt in range(1, T)
    ]
    kept = project(plan, give_back(kept), weights, 0, "project_own")
    return add_up(kept, received)


def solution(mesh):
    spec = P(AXES, None)
    return jax.shard_map(
        local,
        mesh=mesh,
        in_specs=(spec, spec, spec, P("tp", None)),
        out_specs=spec,
        check_vma=False,
    )
```

```python
import functools
import math

import jax
import jax.numpy as jnp
from jax import lax
from jax.experimental import pallas as pl
from jax.experimental.pallas import tpu as pltpu
from jax.sharding import PartitionSpec as P

HD = 128
AXES = ("ctx", "tp")
MIB = 1024 * 1024
F32 = jnp.float32
BF16 = jnp.bfloat16


class Plan:
    def __init__(self, head_count):
        self.C = lax.axis_size("ctx")
        self.T = lax.axis_size("tp")
        self.G = math.gcd(head_count // self.T, self.C)
        self.R = self.C // self.G
        self.heads = head_count // (self.T * self.G)
        self.cols = self.heads * HD
        self.where = jnp.reshape(lax.axis_index(AXES), (1,)).astype(jnp.int32)

    def flat(self, g, r, t):
        return (g % self.G * self.R + r) * self.T + t % self.T

    def move(self, x, dg=0, dt=0, r_map=lambda r: r):
        pairs = [
            (self.flat(g, r, t), self.flat(g + dg, r_map(r), t + dt))
            for g in range(self.G)
            for r in range(self.R)
            for t in range(self.T)
        ]
        return lax.ppermute(x, AXES, pairs)


def pack_kernel(plan, shifts, where_ref, *refs):
    in_refs, outs, (held, in_sem, out_sem) = refs[:3], refs[3:-3], refs[-3:]
    G, R, T, cols = plan.G, plan.R, plan.T, plan.cols
    g, t = where_ref[0] // (R * T), lax.rem(where_ref[0], T)
    inward, outward = [], []
    for index, (dg, dt) in enumerate(shifts):
        start = (lax.rem(t + dt, T) * G + lax.rem(g + dg, G)) * cols
        columns = pl.ds(pl.multiple_of(start, HD), cols)
        for slot, in_ref in enumerate(in_refs):
            inward.append(
                pltpu.make_async_copy(
                    in_ref.at[:, columns], held.at[index, slot], in_sem.at[index, slot]
                )
            )
            inward[-1].start()
    for index, out_ref in enumerate(outs):
        for copy in inward[3 * index : 3 * index + 3]:
            copy.wait()
        outward.append(pltpu.make_async_copy(held.at[index], out_ref, out_sem.at[index]))
        outward[-1].start()
    for copy in outward:
        copy.wait()


def pack(plan, shifts, k, v, q):
    count = len(shifts)
    block = (3, q.shape[0], plan.cols)
    outs = pl.pallas_call(
        functools.partial(pack_kernel, plan, shifts),
        out_shape=[jax.ShapeDtypeStruct(block, BF16)] * count,
        in_specs=[pl.BlockSpec(memory_space=pltpu.SMEM)] + [pl.BlockSpec(memory_space=pl.ANY)] * 3,
        out_specs=[pl.BlockSpec(memory_space=pl.ANY)] * count,
        scratch_shapes=[
            pltpu.VMEM((count, *block), BF16),
            pltpu.SemaphoreType.DMA((count, 3)),
            pltpu.SemaphoreType.DMA((count,)),
        ],
        compiler_params=pltpu.CompilerParams(vmem_limit_bytes=60 * MIB),
        name="pack",
    )(plan.where, k, v, q)
    return dict(zip(shifts, outs))


def join_kernel(*refs):
    out_ref = refs[-1]
    first = 0
    for in_ref in refs[:-1]:
        count = in_ref.shape[1]
        out_ref[:, first : first + count, :] = in_ref[0:2]
        first += count


def join(pieces):
    if len(pieces) == 1:
        return pieces[0]
    shape = (2, sum(piece.shape[1] for piece in pieces), pieces[0].shape[2])
    vmem = pl.BlockSpec(memory_space=pltpu.VMEM)
    return pl.pallas_call(
        join_kernel,
        out_shape=jax.ShapeDtypeStruct(shape, BF16),
        in_specs=[vmem] * len(pieces),
        out_specs=vmem,
        compiler_params=pltpu.CompilerParams(vmem_limit_bytes=20 * MIB),
        cost_estimate=pl.CostEstimate(flops=0, bytes_accessed=0, transcendentals=0),
        name="join",
    )(*pieces)


def fetch_kernel(first, w_ref, out_ref, sem):
    depth = out_ref.shape[0] // sem.shape[0]
    copies = []
    for index in range(sem.shape[0]):
        copies.append(
            pltpu.make_async_copy(
                w_ref.at[pl.ds(first + index * depth, depth), :],
                out_ref.at[pl.ds(index * depth, depth), :],
                sem.at[index],
            )
        )
        copies[-1].start()
    for copy in copies:
        copy.wait()


def fetch(w, first, count):
    return pl.pallas_call(
        functools.partial(fetch_kernel, first),
        out_shape=jax.ShapeDtypeStruct((count, w.shape[1]), w.dtype),
        in_specs=[pl.BlockSpec(memory_space=pl.ANY)],
        out_specs=pl.BlockSpec(memory_space=pltpu.VMEM),
        scratch_shapes=[pltpu.SemaphoreType.DMA((2,))],
        compiler_params=pltpu.CompilerParams(vmem_limit_bytes=38 * MIB),
        cost_estimate=pl.CostEstimate(
            flops=0, bytes_accessed=4 * count * w.shape[1], transcendentals=0
        ),
        name="fetch_weight",
    )(w)


def attend_kernel(q_count, kv_count, heads, tile_blocks, *refs):
    q_refs, kv_refs = refs[:q_count], refs[q_count : q_count + kv_count]
    out_refs, scores = refs[q_count + kv_count : -1], refs[-1]
    scale = math.log2(math.e) / math.sqrt(HD)
    rows = q_refs[0].shape[1]
    per_out = q_count // len(out_refs)
    for head in range(heads):
        cols = slice(head * HD, (head + 1) * HD)
        for at in range(0, q_count, tile_blocks):
            q = jnp.concatenate(
                [ref[ref.shape[0] - 1, :, cols] for ref in q_refs[at : at + tile_blocks]], axis=0
            )
            peak = None
            key = 0
            for kv_ref in kv_refs:
                keys = kv_ref.shape[1]
                part = lax.dot_general(
                    q, kv_ref[0, :, cols], (((1,), (1,)), ((), ())), preferred_element_type=F32
                )
                scores[head % 2, :, pl.ds(key, keys)] = part
                top = jnp.max(part, axis=-1, keepdims=True)
                peak = top if peak is None else jnp.maximum(peak, top)
                key += keys
            peak = peak * scale
            weighted = jnp.zeros((q.shape[0], HD), F32)
            total = jnp.zeros((q.shape[0], 1), F32)
            key = 0
            for kv_ref in kv_refs:
                keys = kv_ref.shape[1]
                probs = jnp.exp2(scores[head % 2, :, pl.ds(key, keys)] * scale - peak).astype(BF16)
                total += jnp.sum(probs.astype(F32), axis=-1, keepdims=True)
                weighted += jnp.dot(probs, kv_ref[1, :, cols], preferred_element_type=F32)
                key += keys
            attended = (weighted / total).astype(BF16)
            for index in range(at, at + tile_blocks):
                place = slice(index % per_out * rows, (index % per_out + 1) * rows)
                block = attended[(index - at) * rows : (index - at + 1) * rows]
                out_refs[index // per_out][place, cols] = block


def attend(plan, queries, kvs, name):
    rows = queries[0].shape[1]
    count = len(queries)
    keys = sum(kv.shape[1] for kv in kvs)
    tile_blocks = math.gcd(count, max(256 // rows, 1))
    vmem = pl.BlockSpec(memory_space=pltpu.VMEM)
    return list(
        pl.pallas_call(
            functools.partial(attend_kernel, count, len(kvs), plan.heads, tile_blocks),
            out_shape=[jax.ShapeDtypeStruct((count // plan.G * rows, plan.cols), BF16)] * plan.G,
            in_specs=[vmem] * (count + len(kvs)),
            out_specs=[vmem] * plan.G,
            scratch_shapes=[pltpu.VMEM((2, tile_blocks * rows, keys), F32)],
            compiler_params=pltpu.CompilerParams(vmem_limit_bytes=20 * MIB),
            cost_estimate=pl.CostEstimate(
                flops=4 * count * rows * keys * plan.cols,
                bytes_accessed=4 * plan.cols * (count * rows + keys),
                transcendentals=count * rows * keys * plan.heads,
            ),
            name=name,
        )(*queries, *kvs)
    )


def project_kernel(plan, weight_count, where_ref, *refs):
    parts, w_refs, (out_ref, mixed) = (
        refs[: plan.G],
        refs[plan.G : plan.G + weight_count],
        refs[plan.G + weight_count :],
    )
    own_g = where_ref[0] // (plan.R * plan.T)
    for dg, part in enumerate(parts):
        place = lax.rem(own_g + dg, plan.G) * plan.cols
        mixed[:, pl.ds(pl.multiple_of(place, HD), plan.cols)] = part[...]
    total = None
    depth = 0
    for w_ref in w_refs:
        share = jnp.dot(
            mixed[:, depth : depth + w_ref.shape[0]],
            w_ref[...],
            preferred_element_type=F32,
        )
        total = share if total is None else total + share
        depth += w_ref.shape[0]
    out_ref[...] = total.astype(BF16)


def project(plan, parts, weights, flops, name):
    rows = parts[0].shape[0]
    depth = sum(w.shape[0] for w in weights)
    vmem = pl.BlockSpec(memory_space=pltpu.VMEM)
    return pl.pallas_call(
        functools.partial(project_kernel, plan, len(weights)),
        out_shape=jax.ShapeDtypeStruct((rows, weights[0].shape[1]), BF16),
        in_specs=[pl.BlockSpec(memory_space=pltpu.SMEM)] + [vmem] * (len(parts) + len(weights)),
        out_specs=vmem,
        scratch_shapes=[pltpu.VMEM((rows, depth), BF16)],
        compiler_params=pltpu.CompilerParams(vmem_limit_bytes=20 * MIB),
        cost_estimate=pl.CostEstimate(flops=flops, bytes_accessed=flops // 64, transcendentals=0),
        name=name,
    )(plan.where, *parts, *weights)


def add_kernel(*refs):
    total = refs[0][...].astype(F32)
    for in_ref in refs[1:-1]:
        total += in_ref[...].astype(F32)
    refs[-1][...] = total.astype(BF16)


def add_up(kept, received):
    vmem = pl.BlockSpec(memory_space=pltpu.VMEM)
    return pl.pallas_call(
        add_kernel,
        out_shape=jax.ShapeDtypeStruct(kept.shape, BF16),
        in_specs=[vmem] * (1 + len(received)),
        out_specs=vmem,
        compiler_params=pltpu.CompilerParams(vmem_limit_bytes=20 * MIB),
        cost_estimate=pl.CostEstimate(flops=0, bytes_accessed=0, transcendentals=0),
        name="add_shares",
    )(kept, *received)


def local(query_vectors, key_vectors, value_vectors, out_weight):
    plan = Plan(query_vectors.shape[1] // HD)
    G, R, T = plan.G, plan.R, plan.T
    rows = query_vectors.shape[0]

    shifts = [(dg, dt) for dg in range(G) for dt in range(T)]
    near_count = max(G // 2, 1) * T
    near, far = shifts[:near_count], shifts[near_count:]
    blocks = pack(plan, shifts, key_vectors, value_vectors, query_vectors)

    def spread(shift):
        return blocks[shift] if shift == (0, 0) else plan.move(blocks[shift], *shift)

    wide = R % 2 == 0 and R <= 8

    def across(own):
        shifts = range(1, R // 2 if wide else 1)
        return [own] + [plan.move(own, r_map=lambda r, s=s: (r + 2 * s) % R) for s in shifts]

    def exchange(pieces):
        pieces = join(pieces)
        if wide:
            return [pieces, plan.move(pieces, r_map=lambda r: r ^ 1)]
        groups = [[g * R + r for r in range(R)] for g in range(G)]
        return [lax.all_gather(pieces, "ctx", axis=1, tiled=True, axis_index_groups=groups)]

    depth = out_weight.shape[0]
    cut = depth // 6
    arrived = [spread(shift) for shift in near]
    if far:
        held = [blocks[shift] for shift in far]
        arrived[1], held = lax.optimization_barrier((arrived[1], held))
        blocks.update(zip(far, held))
    queries = dict(zip(near, arrived))
    gathered = [across(jnp.concatenate([block[:2] for block in arrived], axis=1))]
    gathered[0][0], weight = lax.optimization_barrier((gathered[0][0], out_weight))
    weights = [fetch(weight, 0, cut)]
    if far:
        arrived = [spread(shift) for shift in far]
        arrived, weights[0] = lax.optimization_barrier((arrived, weights[0]))
        queries.update(zip(far, arrived))
        gathered.append(across(join(arrived)))
        gathered[1][0], weight = lax.optimization_barrier((gathered[1][0], weight))
    weights.append(fetch(weight, cut, depth - cut))
    others = [queries[dg, dt] for dg in range(G) for dt in range(1, T)]
    kept = [queries[dg, 0] for dg in range(G)]
    gathered, others, kept, weights = lax.optimization_barrier((gathered, others, kept, weights))
    kvs = [kv for pieces in gathered for kv in exchange(pieces)]

    def give_back(attended):
        return [attended[0]] + [plan.move(attended[dg], -dg) for dg in range(1, G)]

    others = attend(plan, others, kvs, "attend_others")
    kept, others[0] = lax.optimization_barrier((kept, others[0]))
    kept = attend(plan, kept, kvs, "attend_own")
    parts = give_back(others)
    parts, kept = lax.optimization_barrier((parts, kept))
    flops = 2 * (T - 1) * rows * weight.shape[0] * weight.shape[1]
    sent = project(plan, parts, weights, flops, "project_others")
    kept, sent = lax.optimization_barrier((kept, sent))
    received = [
        plan.move(sent[(dt - 1) * rows : dt * rows], 0, -dt) for dt in range(1, T)
    ]
    kept = project(plan, give_back(kept), weights, 0, "project_own")
    return add_up(kept, received)


def solution(mesh):
    spec = P(AXES, None)
    return jax.shard_map(
        local,
        mesh=mesh,
        in_specs=(spec, spec, spec, P("tp", None)),
        out_specs=spec,
        check_vma=False,
    )
```

```python
import functools
import math

import jax
import jax.numpy as jnp
from jax import lax
from jax.experimental import pallas as pl
from jax.experimental.pallas import tpu as pltpu
from jax.sharding import PartitionSpec as P

HD = 128
AXES = ("ctx", "tp")
MIB = 1024 * 1024
F32 = jnp.float32
BF16 = jnp.bfloat16


class Plan:
    def __init__(self, head_count):
        self.C = lax.axis_size("ctx")
        self.T = lax.axis_size("tp")
        self.G = math.gcd(head_count // self.T, self.C)
        self.R = self.C // self.G
        self.heads = head_count // (self.T * self.G)
        self.cols = self.heads * HD
        self.where = jnp.reshape(lax.axis_index(AXES), (1,)).astype(jnp.int32)

    def flat(self, g, r, t):
        return (g % self.G * self.R + r) * self.T + t % self.T

    def move(self, x, dg=0, dt=0, r_map=lambda r: r):
        pairs = [
            (self.flat(g, r, t), self.flat(g + dg, r_map(r), t + dt))
            for g in range(self.G)
            for r in range(self.R)
            for t in range(self.T)
        ]
        return lax.ppermute(x, AXES, pairs)


def pack_kernel(plan, shifts, where_ref, *refs):
    in_refs, outs, (held, in_sem, out_sem) = refs[:3], refs[3:-3], refs[-3:]
    G, R, T, cols = plan.G, plan.R, plan.T, plan.cols
    g, t = where_ref[0] // (R * T), lax.rem(where_ref[0], T)
    inward, outward = [], []
    for index, (dg, dt) in enumerate(shifts):
        start = (lax.rem(t + dt, T) * G + lax.rem(g + dg, G)) * cols
        columns = pl.ds(pl.multiple_of(start, HD), cols)
        for slot, in_ref in enumerate(in_refs):
            inward.append(
                pltpu.make_async_copy(
                    in_ref.at[:, columns], held.at[index, slot], in_sem.at[index, slot]
                )
            )
            inward[-1].start()
    for index, out_ref in enumerate(outs):
        for copy in inward[3 * index : 3 * index + 3]:
            copy.wait()
        outward.append(pltpu.make_async_copy(held.at[index], out_ref, out_sem.at[index]))
        outward[-1].start()
    for copy in outward:
        copy.wait()


def pack(plan, shifts, k, v, q):
    count = len(shifts)
    block = (3, q.shape[0], plan.cols)
    outs = pl.pallas_call(
        functools.partial(pack_kernel, plan, shifts),
        out_shape=[jax.ShapeDtypeStruct(block, BF16)] * count,
        in_specs=[pl.BlockSpec(memory_space=pltpu.SMEM)] + [pl.BlockSpec(memory_space=pl.ANY)] * 3,
        out_specs=[pl.BlockSpec(memory_space=pl.ANY)] * count,
        scratch_shapes=[
            pltpu.VMEM((count, *block), BF16),
            pltpu.SemaphoreType.DMA((count, 3)),
            pltpu.SemaphoreType.DMA((count,)),
        ],
        compiler_params=pltpu.CompilerParams(vmem_limit_bytes=60 * MIB),
        name="pack",
    )(plan.where, k, v, q)
    return dict(zip(shifts, outs))


def join_kernel(*refs):
    out_ref = refs[-1]
    first = 0
    for in_ref in refs[:-1]:
        count = in_ref.shape[1]
        out_ref[:, first : first + count, :] = in_ref[0:2]
        first += count


def join(pieces):
    if len(pieces) == 1:
        return pieces[0]
    shape = (2, sum(piece.shape[1] for piece in pieces), pieces[0].shape[2])
    vmem = pl.BlockSpec(memory_space=pltpu.VMEM)
    return pl.pallas_call(
        join_kernel,
        out_shape=jax.ShapeDtypeStruct(shape, BF16),
        in_specs=[vmem] * len(pieces),
        out_specs=vmem,
        compiler_params=pltpu.CompilerParams(vmem_limit_bytes=20 * MIB),
        cost_estimate=pl.CostEstimate(flops=0, bytes_accessed=0, transcendentals=0),
        name="join",
    )(*pieces)


def fetch_kernel(first, w_ref, out_ref, sem):
    depth = out_ref.shape[0] // sem.shape[0]
    copies = []
    for index in range(sem.shape[0]):
        copies.append(
            pltpu.make_async_copy(
                w_ref.at[pl.ds(first + index * depth, depth), :],
                out_ref.at[pl.ds(index * depth, depth), :],
                sem.at[index],
            )
        )
        copies[-1].start()
    for copy in copies:
        copy.wait()


def fetch(w, first, count):
    return pl.pallas_call(
        functools.partial(fetch_kernel, first),
        out_shape=jax.ShapeDtypeStruct((count, w.shape[1]), w.dtype),
        in_specs=[pl.BlockSpec(memory_space=pl.ANY)],
        out_specs=pl.BlockSpec(memory_space=pltpu.VMEM),
        scratch_shapes=[pltpu.SemaphoreType.DMA((2,))],
        compiler_params=pltpu.CompilerParams(vmem_limit_bytes=38 * MIB),
        cost_estimate=pl.CostEstimate(
            flops=0, bytes_accessed=4 * count * w.shape[1], transcendentals=0
        ),
        name="fetch_weight",
    )(w)


def attend_kernel(q_count, kv_count, heads, tile_blocks, *refs):
    q_refs, kv_refs = refs[:q_count], refs[q_count : q_count + kv_count]
    out_refs, scores = refs[q_count + kv_count : -1], refs[-1]
    scale = math.log2(math.e) / math.sqrt(HD)
    rows = q_refs[0].shape[1]
    per_out = q_count // len(out_refs)
    for head in range(heads):
        cols = slice(head * HD, (head + 1) * HD)
        for at in range(0, q_count, tile_blocks):
            q = jnp.concatenate(
                [ref[ref.shape[0] - 1, :, cols] for ref in q_refs[at : at + tile_blocks]], axis=0
            )
            peak = None
            key = 0
            for kv_ref in kv_refs:
                keys = kv_ref.shape[1]
                part = lax.dot_general(
                    q, kv_ref[0, :, cols], (((1,), (1,)), ((), ())), preferred_element_type=F32
                )
                scores[head % 2, :, pl.ds(key, keys)] = part
                top = jnp.max(part, axis=-1, keepdims=True)
                peak = top if peak is None else jnp.maximum(peak, top)
                key += keys
            peak = peak * scale
            weighted = jnp.zeros((q.shape[0], HD), F32)
            total = jnp.zeros((q.shape[0], 1), F32)
            key = 0
            for kv_ref in kv_refs:
                keys = kv_ref.shape[1]
                probs = jnp.exp2(scores[head % 2, :, pl.ds(key, keys)] * scale - peak).astype(BF16)
                total += jnp.sum(probs.astype(F32), axis=-1, keepdims=True)
                weighted += jnp.dot(probs, kv_ref[1, :, cols], preferred_element_type=F32)
                key += keys
            attended = (weighted / total).astype(BF16)
            for index in range(at, at + tile_blocks):
                place = slice(index % per_out * rows, (index % per_out + 1) * rows)
                block = attended[(index - at) * rows : (index - at + 1) * rows]
                out_refs[index // per_out][place, cols] = block


def attend(plan, queries, kvs, name):
    rows = queries[0].shape[1]
    count = len(queries)
    keys = sum(kv.shape[1] for kv in kvs)
    tile_blocks = math.gcd(count, max(256 // rows, 1))
    vmem = pl.BlockSpec(memory_space=pltpu.VMEM)
    return list(
        pl.pallas_call(
            functools.partial(attend_kernel, count, len(kvs), plan.heads, tile_blocks),
            out_shape=[jax.ShapeDtypeStruct((count // plan.G * rows, plan.cols), BF16)] * plan.G,
            in_specs=[vmem] * (count + len(kvs)),
            out_specs=[vmem] * plan.G,
            scratch_shapes=[pltpu.VMEM((2, tile_blocks * rows, keys), F32)],
            compiler_params=pltpu.CompilerParams(vmem_limit_bytes=20 * MIB),
            cost_estimate=pl.CostEstimate(
                flops=4 * count * rows * keys * plan.cols,
                bytes_accessed=4 * plan.cols * (count * rows + keys),
                transcendentals=count * rows * keys * plan.heads,
            ),
            name=name,
        )(*queries, *kvs)
    )


def project_kernel(plan, weight_count, where_ref, *refs):
    parts, w_refs, (out_ref, mixed) = (
        refs[: plan.G],
        refs[plan.G : plan.G + weight_count],
        refs[plan.G + weight_count :],
    )
    own_g = where_ref[0] // (plan.R * plan.T)
    for dg, part in enumerate(parts):
        place = lax.rem(own_g + dg, plan.G) * plan.cols
        mixed[:, pl.ds(pl.multiple_of(place, HD), plan.cols)] = part[...]
    total = None
    depth = 0
    for w_ref in w_refs:
        share = jnp.dot(
            mixed[:, depth : depth + w_ref.shape[0]],
            w_ref[...],
            preferred_element_type=F32,
        )
        total = share if total is None else total + share
        depth += w_ref.shape[0]
    out_ref[...] = total.astype(BF16)


def project(plan, parts, weights, flops, name):
    rows = parts[0].shape[0]
    depth = sum(w.shape[0] for w in weights)
    vmem = pl.BlockSpec(memory_space=pltpu.VMEM)
    return pl.pallas_call(
        functools.partial(project_kernel, plan, len(weights)),
        out_shape=jax.ShapeDtypeStruct((rows, weights[0].shape[1]), BF16),
        in_specs=[pl.BlockSpec(memory_space=pltpu.SMEM)] + [vmem] * (len(parts) + len(weights)),
        out_specs=vmem,
        scratch_shapes=[pltpu.VMEM((rows, depth), BF16)],
        compiler_params=pltpu.CompilerParams(vmem_limit_bytes=20 * MIB),
        cost_estimate=pl.CostEstimate(flops=flops, bytes_accessed=flops // 64, transcendentals=0),
        name=name,
    )(plan.where, *parts, *weights)


def add_kernel(*refs):
    total = refs[0][...].astype(F32)
    for in_ref in refs[1:-1]:
        total += in_ref[...].astype(F32)
    refs[-1][...] = total.astype(BF16)


def add_up(kept, received):
    vmem = pl.BlockSpec(memory_space=pltpu.VMEM)
    return pl.pallas_call(
        add_kernel,
        out_shape=jax.ShapeDtypeStruct(kept.shape, BF16),
        in_specs=[vmem] * (1 + len(received)),
        out_specs=vmem,
        compiler_params=pltpu.CompilerParams(vmem_limit_bytes=20 * MIB),
        cost_estimate=pl.CostEstimate(flops=0, bytes_accessed=0, transcendentals=0),
        name="add_shares",
    )(kept, *received)


def local(query_vectors, key_vectors, value_vectors, out_weight):
    plan = Plan(query_vectors.shape[1] // HD)
    G, R, T = plan.G, plan.R, plan.T
    rows = query_vectors.shape[0]

    first = [(0, dt) for dt in range(T)]
    straight = [(dg, 0) for dg in range(1, G)]
    crossed = [(dg, dt) for dg in range(1, G) for dt in range(1, T)]
    blocks = pack(
        plan, first + straight + crossed, key_vectors, value_vectors, query_vectors
    )

    def spread(shift):
        return blocks[shift] if shift == (0, 0) else plan.move(blocks[shift], *shift)

    wide = R % 2 == 0 and R <= 8

    def across(own):
        shifts = range(1, R // 2 if wide else 1)
        return [own] + [plan.move(own, r_map=lambda r, s=s: (r + 2 * s) % R) for s in shifts]

    def exchange(pieces):
        pieces = join(pieces)
        if wide:
            return [pieces, plan.move(pieces, r_map=lambda r: r ^ 1)]
        groups = [[g * R + r for r in range(R)] for g in range(G)]
        return [lax.all_gather(pieces, "ctx", axis=1, tiled=True, axis_index_groups=groups)]

    depth = out_weight.shape[0]
    cut = depth // 6
    arrived = {shift: spread(shift) for shift in first + straight}
    gathered = [across(jnp.concatenate([arrived[shift][:2] for shift in first], axis=1))]
    weight, weights = out_weight, []
    if crossed:
        for index, shift in enumerate(crossed):
            before = straight[index % 2 if G > 2 else 0]
            arrived[before], blocks[shift] = lax.optimization_barrier(
                (arrived[before], blocks[shift])
            )
        arrived.update({shift: spread(shift) for shift in crossed})
        own = jnp.concatenate([arrived[shift][:2] for shift in straight], axis=1)
        gathered[0], own, weight = lax.optimization_barrier((gathered[0], own, weight))
        gathered.append(across(own))
        weights.append(fetch(weight, 0, cut))
        last, weights[0] = lax.optimization_barrier(
            ([arrived[shift] for shift in crossed], weights[0])
        )
        arrived.update(zip(crossed, last))
        own, weight = lax.optimization_barrier((join(last), weight))
        gathered.append(across(own))
        weights.append(fetch(weight, cut, depth - cut))
    else:
        weights.append(fetch(weight, 0, depth))
    others = [arrived[dg, dt] for dg in range(G) for dt in range(1, T)]
    kept = [arrived[dg, 0] for dg in range(G)]
    gathered, others, kept, weights = lax.optimization_barrier((gathered, others, kept, weights))
    halves = [gathered[:2], gathered[2:]] if len(gathered) > 2 else [gathered]
    kvs = [kv for pieces in halves for kv in exchange(sum(pieces, []))]

    def give_back(attended):
        return [attended[0]] + [plan.move(attended[dg], -dg) for dg in range(1, G)]

    others = attend(plan, others, kvs, "attend_others")
    kept, others[0] = lax.optimization_barrier((kept, others[0]))
    kept = attend(plan, kept, kvs, "attend_own")
    parts = give_back(others)
    parts, kept = lax.optimization_barrier((parts, kept))
    flops = 2 * (T - 1) * rows * weight.shape[0] * weight.shape[1]
    sent = project(plan, parts, weights, flops, "project_others")
    kept, sent = lax.optimization_barrier((kept, sent))
    received = [
        plan.move(sent[(dt - 1) * rows : dt * rows], 0, -dt) for dt in range(1, T)
    ]
    kept = project(plan, give_back(kept), weights, 0, "project_own")
    return add_up(kept, received)


def solution(mesh):
    spec = P(AXES, None)
    return jax.shard_map(
        local,
        mesh=mesh,
        in_specs=(spec, spec, spec, P("tp", None)),
        out_specs=spec,
        check_vma=False,
    )
```

```python
import functools
import math

import jax
import jax.numpy as jnp
from jax import lax
from jax.experimental import pallas as pl
from jax.experimental.pallas import tpu as pltpu
from jax.sharding import PartitionSpec as P

HD = 128
AXES = ("ctx", "tp")
MIB = 1024 * 1024
F32 = jnp.float32
BF16 = jnp.bfloat16


class Plan:
    def __init__(self, head_count):
        self.C = lax.axis_size("ctx")
        self.T = lax.axis_size("tp")
        self.G = math.gcd(head_count // self.T, self.C)
        self.R = self.C // self.G
        self.heads = head_count // (self.T * self.G)
        self.cols = self.heads * HD
        self.where = jnp.reshape(lax.axis_index(AXES), (1,)).astype(jnp.int32)

    def flat(self, g, r, t):
        return (g % self.G * self.R + r) * self.T + t % self.T

    def move(self, x, dg=0, dt=0, r_map=lambda r: r):
        pairs = [
            (self.flat(g, r, t), self.flat(g + dg, r_map(r), t + dt))
            for g in range(self.G)
            for r in range(self.R)
            for t in range(self.T)
        ]
        return lax.ppermute(x, AXES, pairs)


def pack_kernel(plan, shifts, where_ref, *refs):
    in_refs, outs, (held, in_sem, out_sem) = refs[:3], refs[3:-3], refs[-3:]
    G, R, T, cols = plan.G, plan.R, plan.T, plan.cols
    g, t = where_ref[0] // (R * T), lax.rem(where_ref[0], T)
    inward, outward = [], []
    for index, (dg, dt) in enumerate(shifts):
        start = (lax.rem(t + dt, T) * G + lax.rem(g + dg, G)) * cols
        columns = pl.ds(pl.multiple_of(start, HD), cols)
        for slot, in_ref in enumerate(in_refs):
            inward.append(
                pltpu.make_async_copy(
                    in_ref.at[:, columns], held.at[index, slot], in_sem.at[index, slot]
                )
            )
            inward[-1].start()
    for index, out_ref in enumerate(outs):
        for copy in inward[3 * index : 3 * index + 3]:
            copy.wait()
        outward.append(pltpu.make_async_copy(held.at[index], out_ref, out_sem.at[index]))
        outward[-1].start()
    for copy in outward:
        copy.wait()


def pack(plan, shifts, k, v, q):
    count = len(shifts)
    block = (3, q.shape[0], plan.cols)
    outs = pl.pallas_call(
        functools.partial(pack_kernel, plan, shifts),
        out_shape=[jax.ShapeDtypeStruct(block, BF16)] * count,
        in_specs=[pl.BlockSpec(memory_space=pltpu.SMEM)] + [pl.BlockSpec(memory_space=pl.ANY)] * 3,
        out_specs=[pl.BlockSpec(memory_space=pl.ANY)] * count,
        scratch_shapes=[
            pltpu.VMEM((count, *block), BF16),
            pltpu.SemaphoreType.DMA((count, 3)),
            pltpu.SemaphoreType.DMA((count,)),
        ],
        compiler_params=pltpu.CompilerParams(vmem_limit_bytes=60 * MIB),
        name="pack",
    )(plan.where, k, v, q)
    return dict(zip(shifts, outs))


def join_kernel(*refs):
    out_ref = refs[-1]
    first = 0
    for in_ref in refs[:-1]:
        count = in_ref.shape[1]
        out_ref[:, first : first + count, :] = in_ref[0:2]
        first += count


def join(pieces):
    if len(pieces) == 1:
        return pieces[0]
    shape = (2, sum(piece.shape[1] for piece in pieces), pieces[0].shape[2])
    vmem = pl.BlockSpec(memory_space=pltpu.VMEM)
    return pl.pallas_call(
        join_kernel,
        out_shape=jax.ShapeDtypeStruct(shape, BF16),
        in_specs=[vmem] * len(pieces),
        out_specs=vmem,
        compiler_params=pltpu.CompilerParams(vmem_limit_bytes=20 * MIB),
        cost_estimate=pl.CostEstimate(flops=0, bytes_accessed=0, transcendentals=0),
        name="join",
    )(*pieces)


def fetch_kernel(first, w_ref, out_ref, sem):
    depth = out_ref.shape[0] // sem.shape[0]
    copies = []
    for index in range(sem.shape[0]):
        copies.append(
            pltpu.make_async_copy(
                w_ref.at[pl.ds(first + index * depth, depth), :],
                out_ref.at[pl.ds(index * depth, depth), :],
                sem.at[index],
            )
        )
        copies[-1].start()
    for copy in copies:
        copy.wait()


def fetch(w, first, count):
    return pl.pallas_call(
        functools.partial(fetch_kernel, first),
        out_shape=jax.ShapeDtypeStruct((count, w.shape[1]), w.dtype),
        in_specs=[pl.BlockSpec(memory_space=pl.ANY)],
        out_specs=pl.BlockSpec(memory_space=pltpu.VMEM),
        scratch_shapes=[pltpu.SemaphoreType.DMA((2,))],
        compiler_params=pltpu.CompilerParams(vmem_limit_bytes=38 * MIB),
        cost_estimate=pl.CostEstimate(
            flops=0, bytes_accessed=4 * count * w.shape[1], transcendentals=0
        ),
        name="fetch_weight",
    )(w)


def attend_kernel(q_count, kv_count, heads, tile_blocks, *refs):
    q_refs, kv_refs = refs[:q_count], refs[q_count : q_count + kv_count]
    out_refs, scores = refs[q_count + kv_count : -1], refs[-1]
    scale = math.log2(math.e) / math.sqrt(HD)
    rows = q_refs[0].shape[1]
    per_out = q_count // len(out_refs)
    for head in range(heads):
        cols = slice(head * HD, (head + 1) * HD)
        for at in range(0, q_count, tile_blocks):
            q = jnp.concatenate(
                [ref[ref.shape[0] - 1, :, cols] for ref in q_refs[at : at + tile_blocks]], axis=0
            )
            peak = None
            key = 0
            for kv_ref in kv_refs:
                keys = kv_ref.shape[1]
                part = lax.dot_general(
                    q, kv_ref[0, :, cols], (((1,), (1,)), ((), ())), preferred_element_type=F32
                )
                scores[head % 2, :, pl.ds(key, keys)] = part
                top = jnp.max(part, axis=-1, keepdims=True)
                peak = top if peak is None else jnp.maximum(peak, top)
                key += keys
            peak = peak * scale
            weighted = jnp.zeros((q.shape[0], HD), F32)
            total = jnp.zeros((q.shape[0], 1), F32)
            key = 0
            for kv_ref in kv_refs:
                keys = kv_ref.shape[1]
                probs = jnp.exp2(scores[head % 2, :, pl.ds(key, keys)] * scale - peak).astype(BF16)
                total += jnp.sum(probs.astype(F32), axis=-1, keepdims=True)
                weighted += jnp.dot(probs, kv_ref[1, :, cols], preferred_element_type=F32)
                key += keys
            attended = (weighted / total).astype(BF16)
            for index in range(at, at + tile_blocks):
                place = slice(index % per_out * rows, (index % per_out + 1) * rows)
                block = attended[(index - at) * rows : (index - at + 1) * rows]
                out_refs[index // per_out][place, cols] = block


def attend(plan, queries, kvs, name):
    rows = queries[0].shape[1]
    count = len(queries)
    keys = sum(kv.shape[1] for kv in kvs)
    tile_blocks = math.gcd(count, max(256 // rows, 1))
    vmem = pl.BlockSpec(memory_space=pltpu.VMEM)
    return list(
        pl.pallas_call(
            functools.partial(attend_kernel, count, len(kvs), plan.heads, tile_blocks),
            out_shape=[jax.ShapeDtypeStruct((count // plan.G * rows, plan.cols), BF16)] * plan.G,
            in_specs=[vmem] * (count + len(kvs)),
            out_specs=[vmem] * plan.G,
            scratch_shapes=[pltpu.VMEM((2, tile_blocks * rows, keys), F32)],
            compiler_params=pltpu.CompilerParams(vmem_limit_bytes=20 * MIB),
            cost_estimate=pl.CostEstimate(
                flops=4 * count * rows * keys * plan.cols,
                bytes_accessed=4 * plan.cols * (count * rows + keys),
                transcendentals=count * rows * keys * plan.heads,
            ),
            name=name,
        )(*queries, *kvs)
    )


def project_kernel(plan, weight_count, where_ref, *refs):
    parts, w_refs, (out_ref, mixed) = (
        refs[: plan.G],
        refs[plan.G : plan.G + weight_count],
        refs[plan.G + weight_count :],
    )
    own_g = where_ref[0] // (plan.R * plan.T)
    for dg, part in enumerate(parts):
        place = lax.rem(own_g + dg, plan.G) * plan.cols
        mixed[:, pl.ds(pl.multiple_of(place, HD), plan.cols)] = part[...]
    total = None
    depth = 0
    for w_ref in w_refs:
        share = jnp.dot(
            mixed[:, depth : depth + w_ref.shape[0]],
            w_ref[...],
            preferred_element_type=F32,
        )
        total = share if total is None else total + share
        depth += w_ref.shape[0]
    out_ref[...] = total.astype(BF16)


def project(plan, parts, weights, flops, name):
    rows = parts[0].shape[0]
    depth = sum(w.shape[0] for w in weights)
    vmem = pl.BlockSpec(memory_space=pltpu.VMEM)
    return pl.pallas_call(
        functools.partial(project_kernel, plan, len(weights)),
        out_shape=jax.ShapeDtypeStruct((rows, weights[0].shape[1]), BF16),
        in_specs=[pl.BlockSpec(memory_space=pltpu.SMEM)] + [vmem] * (len(parts) + len(weights)),
        out_specs=vmem,
        scratch_shapes=[pltpu.VMEM((rows, depth), BF16)],
        compiler_params=pltpu.CompilerParams(vmem_limit_bytes=20 * MIB),
        cost_estimate=pl.CostEstimate(flops=flops, bytes_accessed=flops // 64, transcendentals=0),
        name=name,
    )(plan.where, *parts, *weights)


def add_kernel(*refs):
    total = refs[0][...].astype(F32)
    for in_ref in refs[1:-1]:
        total += in_ref[...].astype(F32)
    refs[-1][...] = total.astype(BF16)


def add_up(kept, received):
    vmem = pl.BlockSpec(memory_space=pltpu.VMEM)
    return pl.pallas_call(
        add_kernel,
        out_shape=jax.ShapeDtypeStruct(kept.shape, BF16),
        in_specs=[vmem] * (1 + len(received)),
        out_specs=vmem,
        compiler_params=pltpu.CompilerParams(vmem_limit_bytes=20 * MIB),
        cost_estimate=pl.CostEstimate(flops=0, bytes_accessed=0, transcendentals=0),
        name="add_shares",
    )(kept, *received)


def local(query_vectors, key_vectors, value_vectors, out_weight):
    plan = Plan(query_vectors.shape[1] // HD)
    G, R, T = plan.G, plan.R, plan.T
    rows = query_vectors.shape[0]

    shifts = [(dg, dt) for dg in range(G) for dt in range(T)]
    blocks = pack(plan, shifts, key_vectors, value_vectors, query_vectors)

    def spread(shift):
        return blocks[shift] if shift == (0, 0) else plan.move(blocks[shift], *shift)

    wide = R % 2 == 0 and R <= 8

    def across(own):
        shifts = range(1, R // 2 if wide else 1)
        return [own] + [plan.move(own, r_map=lambda r, s=s: (r + 2 * s) % R) for s in shifts]

    def exchange(pieces):
        pieces = join(pieces)
        if wide:
            return [pieces, plan.move(pieces, r_map=lambda r: r ^ 1)]
        groups = [[g * R + r for r in range(R)] for g in range(G)]
        return [lax.all_gather(pieces, "ctx", axis=1, tiled=True, axis_index_groups=groups)]

    depth = out_weight.shape[0]
    cut = depth // 6
    near_count = max(G // 2, 1) * T
    near, far = shifts[:near_count], shifts[near_count:]
    arrived = {shift: spread(shift) for shift in near}
    if far:
        held = [blocks[shift] for shift in far]
        arrived[near[1]], held = lax.optimization_barrier((arrived[near[1]], held))
        blocks.update(zip(far, held))
    gathered = []
    for at in range(0, near_count, T):
        own = [arrived[shift][:2] for shift in near[at : at + T]]
        gathered.append(across(jnp.concatenate(own, axis=1)))
    gathered[0], gathered[-1][0], weight = lax.optimization_barrier(
        (gathered[0], gathered[-1][0], out_weight)
    )
    weights = [fetch(weight, 0, cut)]
    if far:
        last, weights[0] = lax.optimization_barrier(([spread(shift) for shift in far], weights[0]))
        arrived.update(zip(far, last))
        for at in range(0, len(far), T):
            gathered.append(across(join(last[at : at + T])))
        gathered[-1][0], weight = lax.optimization_barrier((gathered[-1][0], weight))
    weights.append(fetch(weight, cut, depth - cut))
    others = [arrived[dg, dt] for dg in range(G) for dt in range(1, T)]
    kept = [arrived[dg, 0] for dg in range(G)]
    gathered, others, kept, weights = lax.optimization_barrier((gathered, others, kept, weights))
    half = max(len(gathered) // 2, 1)
    halves = [gathered[at : at + half] for at in range(0, len(gathered), half)]
    kvs = [kv for pieces in halves for kv in exchange(sum(pieces, []))]

    def give_back(attended):
        parts = {0: attended[0]}
        for dg in sorted(range(1, G), key=lambda dg: -min(dg, G - dg)):
            parts[dg] = plan.move(attended[dg], -dg)
        return [parts[dg] for dg in range(G)]

    others = attend(plan, others, kvs, "attend_others")
    kept, others[0] = lax.optimization_barrier((kept, others[0]))
    kept = attend(plan, kept, kvs, "attend_own")
    parts = give_back(others)
    parts, kept = lax.optimization_barrier((parts, kept))
    flops = 2 * (T - 1) * rows * weight.shape[0] * weight.shape[1]
    sent = project(plan, parts, weights, flops, "project_others")
    kept, sent = lax.optimization_barrier((kept, sent))
    received = [
        plan.move(sent[(dt - 1) * rows : dt * rows], 0, -dt) for dt in range(1, T)
    ]
    kept = project(plan, give_back(kept), weights, 0, "project_own")
    return add_up(kept, received)


def solution(mesh):
    spec = P(AXES, None)
    return jax.shard_map(
        local,
        mesh=mesh,
        in_specs=(spec, spec, spec, P("tp", None)),
        out_specs=spec,
        check_vma=False,
    )
```

```python
import functools
import math

import jax
import jax.numpy as jnp
from jax import lax
from jax.experimental import pallas as pl
from jax.experimental.pallas import tpu as pltpu
from jax.sharding import PartitionSpec as P

HD = 128
AXES = ("ctx", "tp")
MIB = 1024 * 1024
F32 = jnp.float32
BF16 = jnp.bfloat16


class Plan:
    def __init__(self, head_count):
        self.C = lax.axis_size("ctx")
        self.T = lax.axis_size("tp")
        self.G = math.gcd(head_count // self.T, self.C)
        self.R = self.C // self.G
        self.heads = head_count // (self.T * self.G)
        self.cols = self.heads * HD
        self.where = jnp.reshape(lax.axis_index(AXES), (1,)).astype(jnp.int32)

    def flat(self, g, r, t):
        return (g % self.G * self.R + r) * self.T + t % self.T

    def move(self, x, dg=0, dt=0, r_map=lambda r: r):
        pairs = [
            (self.flat(g, r, t), self.flat(g + dg, r_map(r), t + dt))
            for g in range(self.G)
            for r in range(self.R)
            for t in range(self.T)
        ]
        return lax.ppermute(x, AXES, pairs)


def pack_kernel(plan, shifts, where_ref, *refs):
    in_refs, outs, (held, in_sem, out_sem) = refs[:3], refs[3:-3], refs[-3:]
    G, R, T, cols = plan.G, plan.R, plan.T, plan.cols
    g, t = where_ref[0] // (R * T), lax.rem(where_ref[0], T)
    inward, outward = [], []
    for index, (dg, dt) in enumerate(shifts):
        start = (lax.rem(t + dt, T) * G + lax.rem(g + dg, G)) * cols
        columns = pl.ds(pl.multiple_of(start, HD), cols)
        for slot, in_ref in enumerate(in_refs):
            inward.append(
                pltpu.make_async_copy(
                    in_ref.at[:, columns], held.at[index, slot], in_sem.at[index, slot]
                )
            )
            inward[-1].start()
    for index, out_ref in enumerate(outs):
        for copy in inward[3 * index : 3 * index + 3]:
            copy.wait()
        outward.append(pltpu.make_async_copy(held.at[index], out_ref, out_sem.at[index]))
        outward[-1].start()
    for copy in outward:
        copy.wait()


def pack(plan, shifts, k, v, q):
    count = len(shifts)
    block = (3, q.shape[0], plan.cols)
    outs = pl.pallas_call(
        functools.partial(pack_kernel, plan, shifts),
        out_shape=[jax.ShapeDtypeStruct(block, BF16)] * count,
        in_specs=[pl.BlockSpec(memory_space=pltpu.SMEM)] + [pl.BlockSpec(memory_space=pl.ANY)] * 3,
        out_specs=[pl.BlockSpec(memory_space=pl.ANY)] * count,
        scratch_shapes=[
            pltpu.VMEM((count, *block), BF16),
            pltpu.SemaphoreType.DMA((count, 3)),
            pltpu.SemaphoreType.DMA((count,)),
        ],
        compiler_params=pltpu.CompilerParams(vmem_limit_bytes=60 * MIB),
        name="pack",
    )(plan.where, k, v, q)
    return dict(zip(shifts, outs))


def join_kernel(slots, *refs):
    outs = refs[len(slots) :]
    places = [0, 0]
    for in_ref, (slot, index) in zip(refs, slots):
        rows = pl.ds(places[slot], in_ref.shape[1])
        out_ref, at = (outs[0], slot) if len(outs) == 1 else (outs[slot], 0)
        out_ref[at, rows, :] = in_ref[index]
        places[slot] += in_ref.shape[1]


def join(pieces, split=False):
    slots, arrays = [], []
    for piece in pieces:
        pair = piece if isinstance(piece, tuple) else (piece, piece)
        for slot, array in enumerate(pair):
            slots.append((slot, slot if array is piece else 0))
            arrays.append(array)
    rows = sum(array.shape[1] for array in arrays) // 2
    shape = jax.ShapeDtypeStruct((1 if split else 2, rows, arrays[0].shape[2]), BF16)
    vmem = pl.BlockSpec(memory_space=pltpu.VMEM)
    outs = pl.pallas_call(
        functools.partial(join_kernel, slots),
        out_shape=[shape] * (1 + split),
        in_specs=[vmem] * len(arrays),
        out_specs=[vmem] * (1 + split),
        compiler_params=pltpu.CompilerParams(vmem_limit_bytes=20 * MIB),
        cost_estimate=pl.CostEstimate(flops=0, bytes_accessed=0, transcendentals=0),
        name="join",
    )(*arrays)
    return tuple(outs) if split else outs[0]


def fetch_kernel(first, w_ref, out_ref, sem):
    depth = out_ref.shape[0] // sem.shape[0]
    copies = []
    for index in range(sem.shape[0]):
        copies.append(
            pltpu.make_async_copy(
                w_ref.at[pl.ds(first + index * depth, depth), :],
                out_ref.at[pl.ds(index * depth, depth), :],
                sem.at[index],
            )
        )
        copies[-1].start()
    for copy in copies:
        copy.wait()


def fetch(w, first, count):
    return pl.pallas_call(
        functools.partial(fetch_kernel, first),
        out_shape=jax.ShapeDtypeStruct((count, w.shape[1]), w.dtype),
        in_specs=[pl.BlockSpec(memory_space=pl.ANY)],
        out_specs=pl.BlockSpec(memory_space=pltpu.VMEM),
        scratch_shapes=[pltpu.SemaphoreType.DMA((2,))],
        compiler_params=pltpu.CompilerParams(vmem_limit_bytes=38 * MIB),
        cost_estimate=pl.CostEstimate(
            flops=0, bytes_accessed=4 * count * w.shape[1], transcendentals=0
        ),
        name="fetch_weight",
    )(w)


def attend_kernel(q_count, kv_count, heads, tile_blocks, *refs):
    q_refs, kv_refs = refs[:q_count], refs[q_count : q_count + kv_count]
    out_refs, scores, values = refs[q_count + kv_count : -2], refs[-2], refs[-1]
    values[:, HD:] = jnp.ones((values.shape[0], HD), BF16)
    scale = math.log2(math.e) / math.sqrt(HD)
    rows = q_refs[0].shape[1]
    per_out = q_count // len(out_refs)
    for head in range(heads):
        cols = slice(head * HD, (head + 1) * HD)
        key = 0
        for kv_ref in kv_refs:
            values[key : key + kv_ref.shape[1], :HD] = kv_ref[1, :, cols]
            key += kv_ref.shape[1]
        for at in range(0, q_count, tile_blocks):
            q = jnp.concatenate(
                [ref[ref.shape[0] - 1, :, cols] for ref in q_refs[at : at + tile_blocks]], axis=0
            )
            peak = None
            key = 0
            for kv_ref in kv_refs:
                keys = kv_ref.shape[1]
                part = lax.dot_general(
                    q, kv_ref[0, :, cols], (((1,), (1,)), ((), ())), preferred_element_type=F32
                )
                scores[head % 2, :, pl.ds(key, keys)] = part
                top = jnp.max(part, axis=-1, keepdims=True)
                peak = top if peak is None else jnp.maximum(peak, top)
                key += keys
            peak = peak * scale
            sums = None
            for key in range(0, values.shape[0], 512):
                keys = slice(key, min(key + 512, values.shape[0]))
                probs = jnp.exp2(scores[head % 2, :, keys] * scale - peak).astype(BF16)
                part = jnp.dot(probs, values[keys, :], preferred_element_type=F32)
                sums = part if sums is None else sums + part
            attended = (sums[:, :HD] / sums[:, HD:]).astype(BF16)
            for index in range(at, at + tile_blocks):
                place = slice(index % per_out * rows, (index % per_out + 1) * rows)
                block = attended[(index - at) * rows : (index - at + 1) * rows]
                out_refs[index // per_out][place, cols] = block


def attend(plan, queries, kvs, name):
    rows = queries[0].shape[1]
    count = len(queries)
    keys = sum(kv.shape[1] for kv in kvs)
    tile_blocks = math.gcd(count, max(256 // rows, 1))
    vmem = pl.BlockSpec(memory_space=pltpu.VMEM)
    return list(
        pl.pallas_call(
            functools.partial(attend_kernel, count, len(kvs), plan.heads, tile_blocks),
            out_shape=[jax.ShapeDtypeStruct((count // plan.G * rows, plan.cols), BF16)] * plan.G,
            in_specs=[vmem] * (count + len(kvs)),
            out_specs=[vmem] * plan.G,
            scratch_shapes=[
                pltpu.VMEM((2, tile_blocks * rows, keys), F32),
                pltpu.VMEM((keys, 2 * HD), BF16),
            ],
            compiler_params=pltpu.CompilerParams(vmem_limit_bytes=20 * MIB),
            cost_estimate=pl.CostEstimate(
                flops=4 * count * rows * keys * plan.cols,
                bytes_accessed=4 * plan.cols * (count * rows + keys),
                transcendentals=count * rows * keys * plan.heads,
            ),
            name=name,
        )(*queries, *kvs)
    )


def project_kernel(plan, weight_count, first, where_ref, *refs):
    parts, w_refs, (out_ref, mixed) = (
        refs[: plan.G],
        refs[plan.G : plan.G + weight_count],
        refs[plan.G + weight_count :],
    )
    own_g = where_ref[0] // (plan.R * plan.T)
    for dg, part in enumerate(parts):
        place = lax.rem(own_g + dg, plan.G) * plan.cols
        mixed[:, pl.ds(pl.multiple_of(place, HD), plan.cols)] = part[...]
    total = None
    depth = 0
    for w_ref in w_refs:
        share = jnp.dot(
            mixed[:, depth : depth + w_ref.shape[0]],
            w_ref[:, first : first + out_ref.shape[1]],
            preferred_element_type=F32,
        )
        total = share if total is None else total + share
        depth += w_ref.shape[0]
    out_ref[...] = total.astype(BF16)


def project(plan, parts, weights, first, count, flops, name):
    rows = parts[0].shape[0]
    depth = sum(w.shape[0] for w in weights)
    vmem = pl.BlockSpec(memory_space=pltpu.VMEM)
    return pl.pallas_call(
        functools.partial(project_kernel, plan, len(weights), first),
        out_shape=jax.ShapeDtypeStruct((rows, count), BF16),
        in_specs=[pl.BlockSpec(memory_space=pltpu.SMEM)] + [vmem] * (len(parts) + len(weights)),
        out_specs=vmem,
        scratch_shapes=[pltpu.VMEM((rows, depth), BF16)],
        compiler_params=pltpu.CompilerParams(vmem_limit_bytes=20 * MIB),
        cost_estimate=pl.CostEstimate(flops=flops, bytes_accessed=flops // 64, transcendentals=0),
        name=name,
    )(plan.where, *parts, *weights)


def add_kernel(first, continued, kept_ref, *refs):
    pieces = refs[continued:-3]
    out_ref, held, sem = refs[-3:]
    cols = pl.ds(first, held.shape[1])
    total = kept_ref[:, cols].astype(F32)
    for piece in pieces:
        total += piece[...].astype(F32)
    held[...] = total.astype(BF16)
    copy = pltpu.make_async_copy(held, out_ref.at[:, cols], sem)
    copy.start()
    copy.wait()


def add_up(kept, pieces, first, out):
    vmem = pl.BlockSpec(memory_space=pltpu.VMEM)
    hbm = pl.BlockSpec(memory_space=pl.ANY)
    continued = out is not None
    return pl.pallas_call(
        functools.partial(add_kernel, first, continued),
        out_shape=jax.ShapeDtypeStruct(kept.shape, BF16),
        in_specs=[vmem] + [hbm] * continued + [vmem] * len(pieces),
        out_specs=hbm,
        scratch_shapes=[pltpu.VMEM(pieces[0].shape, BF16), pltpu.SemaphoreType.DMA],
        input_output_aliases={1: 0} if continued else {},
        compiler_params=pltpu.CompilerParams(vmem_limit_bytes=20 * MIB),
        cost_estimate=pl.CostEstimate(flops=0, bytes_accessed=0, transcendentals=0),
        name="add_shares",
    )(kept, *([out] * continued), *pieces)


def local(query_vectors, key_vectors, value_vectors, out_weight):
    plan = Plan(query_vectors.shape[1] // HD)
    G, R, T = plan.G, plan.R, plan.T
    rows = query_vectors.shape[0]

    first = [(0, dt) for dt in range(T)]
    straight = [(dg, 0) for dg in range(1, G)]
    crossed = [(dg, dt) for dg in range(1, G) for dt in range(1, T)]
    blocks = pack(
        plan, first + straight + crossed, key_vectors, value_vectors, query_vectors
    )

    def spread(shift):
        return blocks[shift] if shift == (0, 0) else plan.move(blocks[shift], *shift)

    wide = R % 2 == 0 and R <= 8

    def across(own):
        shifts = range(1, R // 2 if wide else 1)
        return [own] + [plan.move(own, r_map=lambda r, s=s: (r + 2 * s) % R) for s in shifts]

    def exchange(pieces):
        pieces = join(pieces)
        if wide:
            return [pieces, plan.move(pieces, r_map=lambda r: r ^ 1)]
        groups = [[g * R + r for r in range(R)] for g in range(G)]
        return [lax.all_gather(pieces, "ctx", axis=1, tiled=True, axis_index_groups=groups)]

    depth = out_weight.shape[0]
    cut = depth // 6
    arrived = {shift: spread(shift) for shift in first + straight}
    gathered = [across(jnp.concatenate([arrived[shift][:2] for shift in first], axis=1))]
    weight, weights = out_weight, []
    if crossed:
        for index, shift in enumerate(crossed):
            before = straight[index % 2 if G > 2 else 0]
            arrived[before], blocks[shift] = lax.optimization_barrier(
                (arrived[before], blocks[shift])
            )
        arrived.update({shift: spread(shift) for shift in crossed})
        own = jnp.concatenate([arrived[shift][:2] for shift in straight], axis=1)
        gathered[0], own, weight = lax.optimization_barrier((gathered[0], own, weight))
        gathered.append(across(own))
        weights.append(fetch(weight, 0, cut))
        last, weights[0] = lax.optimization_barrier(
            ([arrived[shift] for shift in crossed], weights[0])
        )
        arrived.update(zip(crossed, last))
        own, weight = lax.optimization_barrier((join(last, split=True), weight))
        gathered.append(list(zip(*map(across, own))))
        weights.append(fetch(weight, cut, depth - cut))
    else:
        weights.append(fetch(weight, 0, depth))
    others = [arrived[dg, dt] for dg in range(G) for dt in range(1, T)]
    kept = [arrived[dg, 0] for dg in range(G)]
    gathered, others, kept, weights = lax.optimization_barrier((gathered, others, kept, weights))
    halves = [gathered[:2], gathered[2:]] if len(gathered) > 2 else [gathered]
    kvs = [kv for pieces in halves for kv in exchange(sum(pieces, []))]

    def give_back(attended):
        parts = {0: attended[0]}
        for dg in sorted(range(1, G), key=lambda dg: -min(dg, G - dg)):
            parts[dg] = plan.move(attended[dg], -dg)
        return [parts[dg] for dg in range(G)]

    others = attend(plan, others, kvs, "attend_others")
    kept, others[0] = lax.optimization_barrier((kept, others[0]))
    kept = attend(plan, kept, kvs, "attend_own")
    parts = give_back(others)
    parts, kept = lax.optimization_barrier((parts, kept))
    width = out_weight.shape[1]
    edges = [0, width // 5 * 3, width]
    received = []
    for start, end in zip(edges, edges[1:]):
        flops = 2 * (T - 1) * rows * depth * (end - start)
        share = project(plan, parts, weights, start, end - start, flops, "project_others")
        received.append(
            [plan.move(share[(dt - 1) * rows : dt * rows], 0, -dt) for dt in range(1, T)]
        )
        parts, kept, _ = lax.optimization_barrier((parts, kept, share))
    kept = project(plan, give_back(kept), weights, 0, width, 0, "project_own")
    out = None
    for start, pieces in zip(edges, received):
        out = add_up(kept, pieces, start, out)
    return out


def solution(mesh):
    spec = P(AXES, None)
    return jax.shard_map(
        local,
        mesh=mesh,
        in_specs=(spec, spec, spec, P("tp", None)),
        out_specs=spec,
        check_vma=False,
    )
```

```python
import functools
import math

import jax
import jax.numpy as jnp
from jax import lax
from jax.experimental import pallas as pl
from jax.experimental.pallas import tpu as pltpu
from jax.sharding import PartitionSpec as P

HD = 128
AXES = ("ctx", "tp")
MIB = 1024 * 1024
F32 = jnp.float32
BF16 = jnp.bfloat16


class Plan:
    def __init__(self, head_count):
        self.C = lax.axis_size("ctx")
        self.T = lax.axis_size("tp")
        self.G = math.gcd(head_count // self.T, self.C)
        self.R = self.C // self.G
        self.heads = head_count // (self.T * self.G)
        self.cols = self.heads * HD
        self.where = jnp.reshape(lax.axis_index(AXES), (1,)).astype(jnp.int32)

    def flat(self, g, r, t):
        return (g % self.G * self.R + r) * self.T + t % self.T

    def move(self, x, dg=0, dt=0, r_map=lambda r: r):
        pairs = [
            (self.flat(g, r, t), self.flat(g + dg, r_map(r), t + dt))
            for g in range(self.G)
            for r in range(self.R)
            for t in range(self.T)
        ]
        return lax.ppermute(x, AXES, pairs)


def pack_kernel(plan, shifts, where_ref, *refs):
    in_refs, outs, (held, in_sem, out_sem) = refs[:3], refs[3:-3], refs[-3:]
    G, R, T, cols = plan.G, plan.R, plan.T, plan.cols
    g, t = where_ref[0] // (R * T), lax.rem(where_ref[0], T)
    inward, outward = [], []
    for index, (dg, dt) in enumerate(shifts):
        start = (lax.rem(t + dt, T) * G + lax.rem(g + dg, G)) * cols
        columns = pl.ds(pl.multiple_of(start, HD), cols)
        for slot, in_ref in enumerate(in_refs):
            inward.append(
                pltpu.make_async_copy(
                    in_ref.at[:, columns], held.at[index, slot], in_sem.at[index, slot]
                )
            )
            inward[-1].start()
    for index, out_ref in enumerate(outs):
        for copy in inward[3 * index : 3 * index + 3]:
            copy.wait()
        outward.append(pltpu.make_async_copy(held.at[index], out_ref, out_sem.at[index]))
        outward[-1].start()
    for copy in outward:
        copy.wait()


def pack(plan, shifts, k, v, q):
    count = len(shifts)
    block = (3, q.shape[0], plan.cols)
    outs = pl.pallas_call(
        functools.partial(pack_kernel, plan, shifts),
        out_shape=[jax.ShapeDtypeStruct(block, BF16)] * count,
        in_specs=[pl.BlockSpec(memory_space=pltpu.SMEM)] + [pl.BlockSpec(memory_space=pl.ANY)] * 3,
        out_specs=[pl.BlockSpec(memory_space=pl.ANY)] * count,
        scratch_shapes=[
            pltpu.VMEM((count, *block), BF16),
            pltpu.SemaphoreType.DMA((count, 3)),
            pltpu.SemaphoreType.DMA((count,)),
        ],
        compiler_params=pltpu.CompilerParams(vmem_limit_bytes=60 * MIB),
        name="pack",
    )(plan.where, k, v, q)
    return dict(zip(shifts, outs))


def join_kernel(slots, *refs):
    outs = refs[len(slots) :]
    places = [0, 0]
    for in_ref, (slot, index) in zip(refs, slots):
        rows = pl.ds(places[slot], in_ref.shape[1])
        out_ref, at = (outs[0], slot) if len(outs) == 1 else (outs[slot], 0)
        out_ref[at, rows, :] = in_ref[index]
        places[slot] += in_ref.shape[1]


def join(pieces, split=False):
    slots, arrays = [], []
    for piece in pieces:
        pair = piece if isinstance(piece, tuple) else (piece, piece)
        for slot, array in enumerate(pair):
            slots.append((slot, slot if array is piece else 0))
            arrays.append(array)
    rows = sum(array.shape[1] for array in arrays) // 2
    shape = jax.ShapeDtypeStruct((1 if split else 2, rows, arrays[0].shape[2]), BF16)
    vmem = pl.BlockSpec(memory_space=pltpu.VMEM)
    outs = pl.pallas_call(
        functools.partial(join_kernel, slots),
        out_shape=[shape] * (1 + split),
        in_specs=[vmem] * len(arrays),
        out_specs=[vmem] * (1 + split),
        compiler_params=pltpu.CompilerParams(vmem_limit_bytes=20 * MIB),
        cost_estimate=pl.CostEstimate(flops=0, bytes_accessed=0, transcendentals=0),
        name="join",
    )(*arrays)
    return tuple(outs) if split else outs[0]


def fetch_kernel(first, w_ref, out_ref, sem):
    depth = out_ref.shape[0] // sem.shape[0]
    copies = []
    for index in range(sem.shape[0]):
        copies.append(
            pltpu.make_async_copy(
                w_ref.at[pl.ds(first + index * depth, depth), :],
                out_ref.at[pl.ds(index * depth, depth), :],
                sem.at[index],
            )
        )
        copies[-1].start()
    for copy in copies:
        copy.wait()


def fetch(w, first, count):
    return pl.pallas_call(
        functools.partial(fetch_kernel, first),
        out_shape=jax.ShapeDtypeStruct((count, w.shape[1]), w.dtype),
        in_specs=[pl.BlockSpec(memory_space=pl.ANY)],
        out_specs=pl.BlockSpec(memory_space=pltpu.VMEM),
        scratch_shapes=[pltpu.SemaphoreType.DMA((2,))],
        compiler_params=pltpu.CompilerParams(vmem_limit_bytes=38 * MIB),
        cost_estimate=pl.CostEstimate(
            flops=0, bytes_accessed=4 * count * w.shape[1], transcendentals=0
        ),
        name="fetch_weight",
    )(w)


def attend_kernel(q_count, kv_count, heads, tile_blocks, *refs):
    q_refs, kv_refs = refs[:q_count], refs[q_count : q_count + kv_count]
    out_refs, scores = refs[q_count + kv_count : -1], refs[-1]
    scale = math.log2(math.e) / math.sqrt(HD)
    rows = q_refs[0].shape[1]
    per_out = q_count // len(out_refs)
    for head in range(heads):
        cols = slice(head * HD, (head + 1) * HD)
        for at in range(0, q_count, tile_blocks):
            q = jnp.concatenate(
                [ref[ref.shape[0] - 1, :, cols] for ref in q_refs[at : at + tile_blocks]], axis=0
            )
            peak = None
            key = 0
            for kv_ref in kv_refs:
                keys = kv_ref.shape[1]
                part = lax.dot_general(
                    q, kv_ref[0, :, cols], (((1,), (1,)), ((), ())), preferred_element_type=F32
                )
                scores[head % 2, :, pl.ds(key, keys)] = part
                top = jnp.max(part, axis=-1, keepdims=True)
                peak = top if peak is None else jnp.maximum(peak, top)
                key += keys
            peak = peak * scale
            weighted = jnp.zeros((q.shape[0], HD), F32)
            total = jnp.zeros((q.shape[0], 1), F32)
            key = 0
            for kv_ref in kv_refs:
                keys = kv_ref.shape[1]
                probs = jnp.exp2(scores[head % 2, :, pl.ds(key, keys)] * scale - peak).astype(BF16)
                total += jnp.sum(probs.astype(F32), axis=-1, keepdims=True)
                weighted += jnp.dot(probs, kv_ref[1, :, cols], preferred_element_type=F32)
                key += keys
            attended = (weighted / total).astype(BF16)
            for index in range(at, at + tile_blocks):
                place = slice(index % per_out * rows, (index % per_out + 1) * rows)
                block = attended[(index - at) * rows : (index - at + 1) * rows]
                out_refs[index // per_out][place, cols] = block


def attend(plan, queries, kvs, name):
    rows = queries[0].shape[1]
    count = len(queries)
    keys = sum(kv.shape[1] for kv in kvs)
    tile_blocks = math.gcd(count, max(256 // rows, 1))
    vmem = pl.BlockSpec(memory_space=pltpu.VMEM)
    return list(
        pl.pallas_call(
            functools.partial(attend_kernel, count, len(kvs), plan.heads, tile_blocks),
            out_shape=[jax.ShapeDtypeStruct((count // plan.G * rows, plan.cols), BF16)] * plan.G,
            in_specs=[vmem] * (count + len(kvs)),
            out_specs=[vmem] * plan.G,
            scratch_shapes=[pltpu.VMEM((2, tile_blocks * rows, keys), F32)],
            compiler_params=pltpu.CompilerParams(vmem_limit_bytes=20 * MIB),
            cost_estimate=pl.CostEstimate(
                flops=4 * count * rows * keys * plan.cols,
                bytes_accessed=4 * plan.cols * (count * rows + keys),
                transcendentals=count * rows * keys * plan.heads,
            ),
            name=name,
        )(*queries, *kvs)
    )


def project_kernel(plan, weight_count, first, where_ref, *refs):
    parts, w_refs, (out_ref, mixed) = (
        refs[: plan.G],
        refs[plan.G : plan.G + weight_count],
        refs[plan.G + weight_count :],
    )
    own_g = where_ref[0] // (plan.R * plan.T)
    for dg, part in enumerate(parts):
        place = lax.rem(own_g + dg, plan.G) * plan.cols
        mixed[:, pl.ds(pl.multiple_of(place, HD), plan.cols)] = part[...]
    total = None
    depth = 0
    for w_ref in w_refs:
        share = jnp.dot(
            mixed[:, depth : depth + w_ref.shape[0]],
            w_ref[:, first : first + out_ref.shape[1]],
            preferred_element_type=F32,
        )
        total = share if total is None else total + share
        depth += w_ref.shape[0]
    out_ref[...] = total.astype(BF16)


def project(plan, parts, weights, first, count, flops, name):
    rows = parts[0].shape[0]
    depth = sum(w.shape[0] for w in weights)
    vmem = pl.BlockSpec(memory_space=pltpu.VMEM)
    return pl.pallas_call(
        functools.partial(project_kernel, plan, len(weights), first),
        out_shape=jax.ShapeDtypeStruct((rows, count), BF16),
        in_specs=[pl.BlockSpec(memory_space=pltpu.SMEM)] + [vmem] * (len(parts) + len(weights)),
        out_specs=vmem,
        scratch_shapes=[pltpu.VMEM((rows, depth), BF16)],
        compiler_params=pltpu.CompilerParams(vmem_limit_bytes=20 * MIB),
        cost_estimate=pl.CostEstimate(flops=flops, bytes_accessed=flops // 64, transcendentals=0),
        name=name,
    )(plan.where, *parts, *weights)


def add_kernel(first, continued, kept_ref, *refs):
    pieces = refs[continued:-3]
    out_ref, held, sem = refs[-3:]
    cols = pl.ds(first, held.shape[1])
    total = kept_ref[:, cols].astype(F32)
    for piece in pieces:
        total += piece[...].astype(F32)
    held[...] = total.astype(BF16)
    copy = pltpu.make_async_copy(held, out_ref.at[:, cols], sem)
    copy.start()
    copy.wait()


def add_up(kept, pieces, first, out):
    vmem = pl.BlockSpec(memory_space=pltpu.VMEM)
    hbm = pl.BlockSpec(memory_space=pl.ANY)
    continued = out is not None
    return pl.pallas_call(
        functools.partial(add_kernel, first, continued),
        out_shape=jax.ShapeDtypeStruct(kept.shape, BF16),
        in_specs=[vmem] + [hbm] * continued + [vmem] * len(pieces),
        out_specs=hbm,
        scratch_shapes=[pltpu.VMEM(pieces[0].shape, BF16), pltpu.SemaphoreType.DMA],
        input_output_aliases={1: 0} if continued else {},
        compiler_params=pltpu.CompilerParams(vmem_limit_bytes=20 * MIB),
        cost_estimate=pl.CostEstimate(flops=0, bytes_accessed=0, transcendentals=0),
        name="add_shares",
    )(kept, *([out] * continued), *pieces)


def local(query_vectors, key_vectors, value_vectors, out_weight):
    plan = Plan(query_vectors.shape[1] // HD)
    G, R, T = plan.G, plan.R, plan.T
    rows = query_vectors.shape[0]

    first = [(0, dt) for dt in range(T)]
    straight = [(dg, 0) for dg in range(1, G)]
    crossed = [(dg, dt) for dg in range(1, G) for dt in range(1, T)]
    blocks = pack(
        plan, first + straight + crossed, key_vectors, value_vectors, query_vectors
    )

    def spread(shift):
        return blocks[shift] if shift == (0, 0) else plan.move(blocks[shift], *shift)

    wide = R % 2 == 0 and R <= 8

    def across(own):
        shifts = range(1, R // 2 if wide else 1)
        return [own] + [plan.move(own, r_map=lambda r, s=s: (r + 2 * s) % R) for s in shifts]

    def exchange(pieces):
        pieces = join(pieces)
        if wide:
            return [pieces, plan.move(pieces, r_map=lambda r: r ^ 1)]
        groups = [[g * R + r for r in range(R)] for g in range(G)]
        return [lax.all_gather(pieces, "ctx", axis=1, tiled=True, axis_index_groups=groups)]

    depth = out_weight.shape[0]
    cuts = [0, depth // 6, depth // 2, depth]
    arrived = {shift: spread(shift) for shift in first + straight}
    gathered = [across(jnp.concatenate([arrived[shift][:2] for shift in first], axis=1))]
    weight, weights = out_weight, []
    if crossed:
        for index, shift in enumerate(crossed):
            before = straight[index % 2 if G > 2 else 0]
            arrived[before], blocks[shift] = lax.optimization_barrier(
                (arrived[before], blocks[shift])
            )
        arrived.update({shift: spread(shift) for shift in crossed})
        own = jnp.concatenate([arrived[shift][:2] for shift in straight], axis=1)
        gathered[0], own, weight = lax.optimization_barrier((gathered[0], own, weight))
        gathered.append(across(own))
        weights.append(fetch(weight, 0, cuts[1]))
        last, weights[0] = lax.optimization_barrier(
            ([arrived[shift] for shift in crossed], weights[0])
        )
        arrived.update(zip(crossed, last))
        own, weight = lax.optimization_barrier((join(last, split=True), weight))
        gathered.append(list(zip(*map(across, own))))
        weights.append(fetch(weight, cuts[1], cuts[2] - cuts[1]))
    else:
        weights.append(fetch(weight, 0, cuts[2]))
    others = [arrived[dg, dt] for dg in range(G) for dt in range(1, T)]
    kept = [arrived[dg, 0] for dg in range(G)]
    gathered, others, kept, weights, weight = lax.optimization_barrier(
        (gathered, others, kept, weights, weight)
    )
    halves = [gathered[:2], gathered[2:]] if len(gathered) > 2 else [gathered]
    kvs = [kv for pieces in halves for kv in exchange(sum(pieces, []))]

    weights = list(weights) + [fetch(weight, cuts[2], depth - cuts[2])]
    others, weights[-1] = lax.optimization_barrier((others, weights[-1]))

    def give_back(attended):
        parts = {0: attended[0]}
        for dg in sorted(range(1, G), key=lambda dg: -min(dg, G - dg)):
            parts[dg] = plan.move(attended[dg], -dg)
        return [parts[dg] for dg in range(G)]

    others = attend(plan, others, kvs, "attend_others")
    kept, others[0] = lax.optimization_barrier((kept, others[0]))
    kept = attend(plan, kept, kvs, "attend_own")
    parts = give_back(others)
    parts, kept = lax.optimization_barrier((parts, kept))
    width = out_weight.shape[1]
    edges = [0, width // 5 * 3, width]
    received = []
    for start, end in zip(edges, edges[1:]):
        flops = 2 * (T - 1) * rows * depth * (end - start)
        share = project(plan, parts, weights, start, end - start, flops, "project_others")
        received.append(
            [plan.move(share[(dt - 1) * rows : dt * rows], 0, -dt) for dt in range(1, T)]
        )
        parts, kept, _ = lax.optimization_barrier((parts, kept, share))
    kept = project(plan, give_back(kept), weights, 0, width, 0, "project_own")
    out = None
    for start, pieces in zip(edges, received):
        out = add_up(kept, pieces, start, out)
    return out


def solution(mesh):
    spec = P(AXES, None)
    return jax.shard_map(
        local,
        mesh=mesh,
        in_specs=(spec, spec, spec, P("tp", None)),
        out_specs=spec,
        check_vma=False,
    )
```

```python
import functools
import math

import jax
import jax.numpy as jnp
from jax import lax
from jax.experimental import pallas as pl
from jax.experimental.pallas import tpu as pltpu
from jax.sharding import PartitionSpec as P

HD = 128
AXES = ("ctx", "tp")
MIB = 1024 * 1024
F32 = jnp.float32
BF16 = jnp.bfloat16


class Plan:
    def __init__(self, head_count):
        self.C = lax.axis_size("ctx")
        self.T = lax.axis_size("tp")
        self.G = math.gcd(head_count // self.T, self.C)
        self.R = self.C // self.G
        self.heads = head_count // (self.T * self.G)
        self.cols = self.heads * HD
        self.where = jnp.reshape(lax.axis_index(AXES), (1,)).astype(jnp.int32)

    def flat(self, g, r, t):
        return (g % self.G * self.R + r) * self.T + t % self.T

    def move(self, x, dg=0, dt=0, r_map=lambda r: r):
        pairs = [
            (self.flat(g, r, t), self.flat(g + dg, r_map(r), t + dt))
            for g in range(self.G)
            for r in range(self.R)
            for t in range(self.T)
        ]
        return lax.ppermute(x, AXES, pairs)


def pack_kernel(plan, shifts, where_ref, *refs):
    in_refs, outs, (held, in_sem, out_sem) = refs[:3], refs[3:-3], refs[-3:]
    G, R, T, cols = plan.G, plan.R, plan.T, plan.cols
    g, t = where_ref[0] // (R * T), lax.rem(where_ref[0], T)
    inward, outward = [], []
    for index, (dg, dt) in enumerate(shifts):
        start = (lax.rem(t + dt, T) * G + lax.rem(g + dg, G)) * cols
        columns = pl.ds(pl.multiple_of(start, HD), cols)
        for slot, in_ref in enumerate(in_refs):
            inward.append(
                pltpu.make_async_copy(
                    in_ref.at[:, columns], held.at[index, slot], in_sem.at[index, slot]
                )
            )
            inward[-1].start()
    for index, out_ref in enumerate(outs):
        for copy in inward[3 * index : 3 * index + 3]:
            copy.wait()
        outward.append(pltpu.make_async_copy(held.at[index], out_ref, out_sem.at[index]))
        outward[-1].start()
    for copy in outward:
        copy.wait()


def pack(plan, shifts, k, v, q):
    count = len(shifts)
    block = (3, q.shape[0], plan.cols)
    outs = pl.pallas_call(
        functools.partial(pack_kernel, plan, shifts),
        out_shape=[jax.ShapeDtypeStruct(block, BF16)] * count,
        in_specs=[pl.BlockSpec(memory_space=pltpu.SMEM)] + [pl.BlockSpec(memory_space=pl.ANY)] * 3,
        out_specs=[pl.BlockSpec(memory_space=pl.ANY)] * count,
        scratch_shapes=[
            pltpu.VMEM((count, *block), BF16),
            pltpu.SemaphoreType.DMA((count, 3)),
            pltpu.SemaphoreType.DMA((count,)),
        ],
        compiler_params=pltpu.CompilerParams(vmem_limit_bytes=60 * MIB),
        name="pack",
    )(plan.where, k, v, q)
    return dict(zip(shifts, outs))


def join_kernel(slots, *refs):
    outs = refs[len(slots) :]
    places = [0, 0]
    for in_ref, (slot, index) in zip(refs, slots):
        rows = pl.ds(places[slot], in_ref.shape[1])
        out_ref, at = (outs[0], slot) if len(outs) == 1 else (outs[slot], 0)
        out_ref[at, rows, :] = in_ref[index]
        places[slot] += in_ref.shape[1]


def join(pieces, split=False):
    slots, arrays = [], []
    for piece in pieces:
        pair = piece if isinstance(piece, tuple) else (piece, piece)
        for slot, array in enumerate(pair):
            slots.append((slot, slot if array is piece else 0))
            arrays.append(array)
    rows = sum(array.shape[1] for array in arrays) // 2
    shape = jax.ShapeDtypeStruct((1 if split else 2, rows, arrays[0].shape[2]), BF16)
    vmem = pl.BlockSpec(memory_space=pltpu.VMEM)
    outs = pl.pallas_call(
        functools.partial(join_kernel, slots),
        out_shape=[shape] * (1 + split),
        in_specs=[vmem] * len(arrays),
        out_specs=[vmem] * (1 + split),
        compiler_params=pltpu.CompilerParams(vmem_limit_bytes=20 * MIB),
        cost_estimate=pl.CostEstimate(flops=0, bytes_accessed=0, transcendentals=0),
        name="join",
    )(*arrays)
    return tuple(outs) if split else outs[0]


def fetch_kernel(first, w_ref, out_ref, sem):
    depth = out_ref.shape[0] // sem.shape[0]
    copies = []
    for index in range(sem.shape[0]):
        copies.append(
            pltpu.make_async_copy(
                w_ref.at[pl.ds(first + index * depth, depth), :],
                out_ref.at[pl.ds(index * depth, depth), :],
                sem.at[index],
            )
        )
        copies[-1].start()
    for copy in copies:
        copy.wait()


def fetch(w, first, count):
    return pl.pallas_call(
        functools.partial(fetch_kernel, first),
        out_shape=jax.ShapeDtypeStruct((count, w.shape[1]), w.dtype),
        in_specs=[pl.BlockSpec(memory_space=pl.ANY)],
        out_specs=pl.BlockSpec(memory_space=pltpu.VMEM),
        scratch_shapes=[pltpu.SemaphoreType.DMA((2,))],
        compiler_params=pltpu.CompilerParams(vmem_limit_bytes=38 * MIB),
        cost_estimate=pl.CostEstimate(
            flops=0, bytes_accessed=4 * count * w.shape[1], transcendentals=0
        ),
        name="fetch_weight",
    )(w)


def attend_kernel(q_count, kv_count, heads, tile_blocks, *refs):
    q_refs, kv_refs = refs[:q_count], refs[q_count : q_count + kv_count]
    out_refs, scores = refs[q_count + kv_count : -1], refs[-1]
    scale = math.log2(math.e) / math.sqrt(HD)
    rows = q_refs[0].shape[1]
    per_out = q_count // len(out_refs)
    for head in range(heads):
        cols = slice(head * HD, (head + 1) * HD)
        for at in range(0, q_count, tile_blocks):
            q = jnp.concatenate(
                [ref[ref.shape[0] - 1, :, cols] for ref in q_refs[at : at + tile_blocks]], axis=0
            )
            peak = None
            key = 0
            for kv_ref in kv_refs:
                keys = kv_ref.shape[1]
                part = lax.dot_general(
                    q, kv_ref[0, :, cols], (((1,), (1,)), ((), ())), preferred_element_type=F32
                )
                scores[head % 2, :, pl.ds(key, keys)] = part
                top = jnp.max(part, axis=-1, keepdims=True)
                peak = top if peak is None else jnp.maximum(peak, top)
                key += keys
            peak = peak * scale
            weighted = jnp.zeros((q.shape[0], HD), F32)
            total = jnp.zeros((q.shape[0], 1), F32)
            key = 0
            for kv_ref in kv_refs:
                keys = kv_ref.shape[1]
                probs = jnp.exp2(scores[head % 2, :, pl.ds(key, keys)] * scale - peak).astype(BF16)
                total += jnp.sum(probs.astype(F32), axis=-1, keepdims=True)
                weighted += jnp.dot(probs, kv_ref[1, :, cols], preferred_element_type=F32)
                key += keys
            attended = (weighted / total).astype(BF16)
            for index in range(at, at + tile_blocks):
                place = slice(index % per_out * rows, (index % per_out + 1) * rows)
                block = attended[(index - at) * rows : (index - at + 1) * rows]
                out_refs[index // per_out][place, cols] = block


def attend(plan, queries, kvs, name):
    rows = queries[0].shape[1]
    count = len(queries)
    keys = sum(kv.shape[1] for kv in kvs)
    tile_blocks = math.gcd(count, max(256 // rows, 1))
    vmem = pl.BlockSpec(memory_space=pltpu.VMEM)
    return list(
        pl.pallas_call(
            functools.partial(attend_kernel, count, len(kvs), plan.heads, tile_blocks),
            out_shape=[jax.ShapeDtypeStruct((count // plan.G * rows, plan.cols), BF16)] * plan.G,
            in_specs=[vmem] * (count + len(kvs)),
            out_specs=[vmem] * plan.G,
            scratch_shapes=[pltpu.VMEM((2, tile_blocks * rows, keys), F32)],
            compiler_params=pltpu.CompilerParams(vmem_limit_bytes=20 * MIB),
            cost_estimate=pl.CostEstimate(
                flops=4 * count * rows * keys * plan.cols,
                bytes_accessed=4 * plan.cols * (count * rows + keys),
                transcendentals=count * rows * keys * plan.heads,
            ),
            name=name,
        )(*queries, *kvs)
    )


def project_kernel(plan, weight_count, first, where_ref, *refs):
    parts, w_refs, (out_ref, mixed) = (
        refs[: plan.G],
        refs[plan.G : plan.G + weight_count],
        refs[plan.G + weight_count :],
    )
    own_g = where_ref[0] // (plan.R * plan.T)
    for dg, part in enumerate(parts):
        place = lax.rem(own_g + dg, plan.G) * plan.cols
        mixed[:, pl.ds(pl.multiple_of(place, HD), plan.cols)] = part[...]
    total = None
    depth = 0
    for w_ref in w_refs:
        share = jnp.dot(
            mixed[:, depth : depth + w_ref.shape[0]],
            w_ref[:, first : first + out_ref.shape[1]],
            preferred_element_type=F32,
        )
        total = share if total is None else total + share
        depth += w_ref.shape[0]
    out_ref[...] = total.astype(BF16)


def project(plan, parts, weights, first, count, flops, name):
    rows = parts[0].shape[0]
    depth = sum(w.shape[0] for w in weights)
    vmem = pl.BlockSpec(memory_space=pltpu.VMEM)
    return pl.pallas_call(
        functools.partial(project_kernel, plan, len(weights), first),
        out_shape=jax.ShapeDtypeStruct((rows, count), BF16),
        in_specs=[pl.BlockSpec(memory_space=pltpu.SMEM)] + [vmem] * (len(parts) + len(weights)),
        out_specs=vmem,
        scratch_shapes=[pltpu.VMEM((rows, depth), BF16)],
        compiler_params=pltpu.CompilerParams(vmem_limit_bytes=20 * MIB),
        cost_estimate=pl.CostEstimate(flops=flops, bytes_accessed=flops // 64, transcendentals=0),
        name=name,
    )(plan.where, *parts, *weights)


def add_kernel(first, continued, kept_ref, *refs):
    pieces = refs[continued:-3]
    out_ref, held, sem = refs[-3:]
    cols = pl.ds(first, held.shape[1])
    total = kept_ref[:, cols].astype(F32)
    for piece in pieces:
        total += piece[...].astype(F32)
    held[...] = total.astype(BF16)
    copy = pltpu.make_async_copy(held, out_ref.at[:, cols], sem)
    copy.start()
    copy.wait()


def add_up(kept, pieces, first, out):
    vmem = pl.BlockSpec(memory_space=pltpu.VMEM)
    hbm = pl.BlockSpec(memory_space=pl.ANY)
    continued = out is not None
    return pl.pallas_call(
        functools.partial(add_kernel, first, continued),
        out_shape=jax.ShapeDtypeStruct(kept.shape, BF16),
        in_specs=[vmem] + [hbm] * continued + [vmem] * len(pieces),
        out_specs=hbm,
        scratch_shapes=[pltpu.VMEM(pieces[0].shape, BF16), pltpu.SemaphoreType.DMA],
        input_output_aliases={1: 0} if continued else {},
        compiler_params=pltpu.CompilerParams(vmem_limit_bytes=20 * MIB),
        cost_estimate=pl.CostEstimate(flops=0, bytes_accessed=0, transcendentals=0),
        name="add_shares",
    )(kept, *([out] * continued), *pieces)


def local(query_vectors, key_vectors, value_vectors, out_weight):
    plan = Plan(query_vectors.shape[1] // HD)
    G, R, T = plan.G, plan.R, plan.T
    rows = query_vectors.shape[0]

    first = [(0, dt) for dt in range(T)]
    straight = [(dg, 0) for dg in range(1, G)]
    crossed = [(dg, dt) for dg in range(1, G) for dt in range(1, T)]
    blocks = pack(
        plan, first + straight + crossed, key_vectors, value_vectors, query_vectors
    )

    def spread(shift):
        return blocks[shift] if shift == (0, 0) else plan.move(blocks[shift], *shift)

    wide = R % 2 == 0 and R <= 8

    def across(own):
        shifts = range(1, R // 2 if wide else 1)
        return [own] + [plan.move(own, r_map=lambda r, s=s: (r + 2 * s) % R) for s in shifts]

    def exchange(pieces):
        pieces = join(pieces)
        if wide:
            return [pieces, plan.move(pieces, r_map=lambda r: r ^ 1)]
        groups = [[g * R + r for r in range(R)] for g in range(G)]
        return [lax.all_gather(pieces, "ctx", axis=1, tiled=True, axis_index_groups=groups)]

    depth = out_weight.shape[0]
    cuts = [0, depth // 6, depth // 2, depth]
    arrived = {shift: spread(shift) for shift in first + straight}
    gathered = [across(jnp.concatenate([arrived[shift][:2] for shift in first], axis=1))]
    weight, weights = out_weight, []
    if crossed:
        for index, shift in enumerate(crossed):
            before = (first[-1:] + straight)[index]
            arrived[before], blocks[shift] = lax.optimization_barrier(
                (arrived[before], blocks[shift])
            )
        arrived.update({shift: spread(shift) for shift in crossed})
        own = jnp.concatenate([arrived[shift][:2] for shift in straight], axis=1)
        gathered[0], own, weight = lax.optimization_barrier((gathered[0], own, weight))
        gathered.append(across(own))
        weights.append(fetch(weight, 0, cuts[1]))
        last, weights[0] = lax.optimization_barrier(
            ([arrived[shift] for shift in crossed], weights[0])
        )
        arrived.update(zip(crossed, last))
        own, weight = lax.optimization_barrier((join(last, split=True), weight))
        gathered.append(list(zip(*map(across, own))))
        weights.append(fetch(weight, cuts[1], cuts[2] - cuts[1]))
    else:
        weights.append(fetch(weight, 0, cuts[2]))
    others = [arrived[dg, dt] for dg in range(G) for dt in range(1, T)]
    kept = [arrived[dg, 0] for dg in range(G)]
    gathered, others, kept, weights, weight = lax.optimization_barrier(
        (gathered, others, kept, weights, weight)
    )
    halves = [gathered[:2], gathered[2:]] if len(gathered) > 2 else [gathered]
    kvs = [kv for pieces in halves for kv in exchange(sum(pieces, []))]

    weights = list(weights) + [fetch(weight, cuts[2], depth - cuts[2])]
    others, weights[-1] = lax.optimization_barrier((others, weights[-1]))

    def give_back(attended):
        parts = {0: attended[0]}
        for dg in sorted(range(1, G), key=lambda dg: -min(dg, G - dg)):
            parts[dg] = plan.move(attended[dg], -dg)
        return [parts[dg] for dg in range(G)]

    others = attend(plan, others, kvs, "attend_others")
    kept, others[0] = lax.optimization_barrier((kept, others[0]))
    kept = attend(plan, kept, kvs, "attend_own")
    parts = give_back(others)
    parts, kept = lax.optimization_barrier((parts, kept))
    width = out_weight.shape[1]
    edges = [0, width // 5 * 3, width]
    received = []
    for start, end in zip(edges, edges[1:]):
        flops = 2 * (T - 1) * rows * depth * (end - start)
        share = project(plan, parts, weights, start, end - start, flops, "project_others")
        received.append(
            [plan.move(share[(dt - 1) * rows : dt * rows], 0, -dt) for dt in range(1, T)]
        )
        parts, kept, _ = lax.optimization_barrier((parts, kept, share))
    kept = project(plan, give_back(kept), weights, 0, width, 0, "project_own")
    out = None
    for start, pieces in zip(edges, received):
        out = add_up(kept, pieces, start, out)
    return out


def solution(mesh):
    spec = P(AXES, None)
    return jax.shard_map(
        local,
        mesh=mesh,
        in_specs=(spec, spec, spec, P("tp", None)),
        out_specs=spec,
        check_vma=False,
    )
```

```python
import functools
import math

import jax
import jax.numpy as jnp
from jax import lax
from jax.experimental import pallas as pl
from jax.experimental.pallas import tpu as pltpu
from jax.sharding import PartitionSpec as P

HD = 128
AXES = ("ctx", "tp")
MIB = 1024 * 1024
F32 = jnp.float32
BF16 = jnp.bfloat16


class Plan:
    def __init__(self, head_count):
        self.C = lax.axis_size("ctx")
        self.T = lax.axis_size("tp")
        self.G = math.gcd(head_count // self.T, self.C)
        self.R = self.C // self.G
        self.heads = head_count // (self.T * self.G)
        self.cols = self.heads * HD
        self.where = jnp.reshape(lax.axis_index(AXES), (1,)).astype(jnp.int32)

    def flat(self, g, r, t):
        return (g % self.G * self.R + r) * self.T + t % self.T

    def move(self, x, dg=0, dt=0, r_map=lambda r: r):
        pairs = [
            (self.flat(g, r, t), self.flat(g + dg, r_map(r), t + dt))
            for g in range(self.G)
            for r in range(self.R)
            for t in range(self.T)
        ]
        return lax.ppermute(x, AXES, pairs)


def pack_kernel(plan, pieces, where_ref, k_ref, v_ref, q_ref, *refs):
    outs, held, in_sem, out_sem = refs[:-3], *refs[-3:]
    G, R, T, cols = plan.G, plan.R, plan.T, plan.cols
    g, t = where_ref[0] // (R * T), lax.rem(where_ref[0], T)
    in_refs = (k_ref, v_ref, q_ref)
    groups = []
    place = 0
    for (dg, dt), slots in pieces:
        start = (lax.rem(t + dt, T) * G + lax.rem(g + dg, G)) * cols
        columns = pl.ds(pl.multiple_of(start, HD), cols)
        groups.append([])
        for slot in slots:
            copy = pltpu.make_async_copy(
                in_refs[slot].at[:, columns], held.at[place], in_sem.at[place]
            )
            copy.start()
            groups[-1].append(copy)
            place += 1
    outward = []
    place = 0
    for group, out_ref in zip(groups, outs):
        for copy in group:
            copy.wait()
        source = held.at[pl.ds(place, len(group))]
        outward.append(pltpu.make_async_copy(source, out_ref, out_sem.at[len(outward)]))
        outward[-1].start()
        place += len(group)
    for copy in outward:
        copy.wait()


def pack(plan, pieces, k, v, q):
    rows = q.shape[0]
    total = sum(len(slots) for shift, slots in pieces)
    outs = pl.pallas_call(
        functools.partial(pack_kernel, plan, pieces),
        out_shape=[
            jax.ShapeDtypeStruct((len(slots), rows, plan.cols), BF16) for shift, slots in pieces
        ],
        in_specs=[pl.BlockSpec(memory_space=pltpu.SMEM)] + [pl.BlockSpec(memory_space=pl.ANY)] * 3,
        out_specs=[pl.BlockSpec(memory_space=pl.ANY)] * len(pieces),
        scratch_shapes=[
            pltpu.VMEM((total, rows, plan.cols), BF16),
            pltpu.SemaphoreType.DMA((total,)),
            pltpu.SemaphoreType.DMA((len(pieces),)),
        ],
        compiler_params=pltpu.CompilerParams(vmem_limit_bytes=60 * MIB),
        name="pack",
    )(plan.where, k, v, q)
    return dict(zip(pieces, outs))


def join_kernel(slots, *refs):
    outs = refs[len(slots) :]
    places = [0, 0]
    for in_ref, (slot, index) in zip(refs, slots):
        rows = pl.ds(places[slot], in_ref.shape[1])
        out_ref, at = (outs[0], slot) if len(outs) == 1 else (outs[slot], 0)
        out_ref[at, rows, :] = in_ref[index]
        places[slot] += in_ref.shape[1]


def join(pieces, split=False):
    slots, arrays = [], []
    for piece in pieces:
        pair = piece if isinstance(piece, tuple) else (piece, piece)
        for slot, array in enumerate(pair):
            slots.append((slot, slot if array is piece else 0))
            arrays.append(array)
    rows = sum(array.shape[1] for array in arrays) // 2
    shape = jax.ShapeDtypeStruct((1 if split else 2, rows, arrays[0].shape[2]), BF16)
    vmem = pl.BlockSpec(memory_space=pltpu.VMEM)
    outs = pl.pallas_call(
        functools.partial(join_kernel, slots),
        out_shape=[shape] * (1 + split),
        in_specs=[vmem] * len(arrays),
        out_specs=[vmem] * (1 + split),
        compiler_params=pltpu.CompilerParams(vmem_limit_bytes=20 * MIB),
        cost_estimate=pl.CostEstimate(flops=0, bytes_accessed=0, transcendentals=0),
        name="join",
    )(*arrays)
    return tuple(outs) if split else outs[0]


def fetch_kernel(first, w_ref, out_ref, sem):
    depth = out_ref.shape[0] // sem.shape[0]
    copies = []
    for index in range(sem.shape[0]):
        copies.append(
            pltpu.make_async_copy(
                w_ref.at[pl.ds(first + index * depth, depth), :],
                out_ref.at[pl.ds(index * depth, depth), :],
                sem.at[index],
            )
        )
        copies[-1].start()
    for copy in copies:
        copy.wait()


def fetch(w, first, count):
    return pl.pallas_call(
        functools.partial(fetch_kernel, first),
        out_shape=jax.ShapeDtypeStruct((count, w.shape[1]), w.dtype),
        in_specs=[pl.BlockSpec(memory_space=pl.ANY)],
        out_specs=pl.BlockSpec(memory_space=pltpu.VMEM),
        scratch_shapes=[pltpu.SemaphoreType.DMA((2,))],
        compiler_params=pltpu.CompilerParams(vmem_limit_bytes=38 * MIB),
        cost_estimate=pl.CostEstimate(
            flops=0, bytes_accessed=4 * count * w.shape[1], transcendentals=0
        ),
        name="fetch_weight",
    )(w)


def attend_kernel(q_count, kv_count, heads, tile_blocks, *refs):
    q_refs, kv_refs = refs[:q_count], refs[q_count : q_count + kv_count]
    out_refs, scores = refs[q_count + kv_count : -1], refs[-1]
    scale = math.log2(math.e) / math.sqrt(HD)
    rows = q_refs[0].shape[1]
    per_out = q_count // len(out_refs)
    for head in range(heads):
        cols = slice(head * HD, (head + 1) * HD)
        for at in range(0, q_count, tile_blocks):
            q = jnp.concatenate(
                [ref[ref.shape[0] - 1, :, cols] for ref in q_refs[at : at + tile_blocks]], axis=0
            )
            peak = None
            key = 0
            for kv_ref in kv_refs:
                keys = kv_ref.shape[1]
                part = lax.dot_general(
                    q, kv_ref[0, :, cols], (((1,), (1,)), ((), ())), preferred_element_type=F32
                )
                scores[head % 2, :, pl.ds(key, keys)] = part
                top = jnp.max(part, axis=-1, keepdims=True)
                peak = top if peak is None else jnp.maximum(peak, top)
                key += keys
            peak = peak * scale
            weighted = jnp.zeros((q.shape[0], HD), F32)
            total = jnp.zeros((q.shape[0], 1), F32)
            key = 0
            for kv_ref in kv_refs:
                keys = kv_ref.shape[1]
                probs = jnp.exp2(scores[head % 2, :, pl.ds(key, keys)] * scale - peak).astype(BF16)
                total += jnp.sum(probs.astype(F32), axis=-1, keepdims=True)
                weighted += jnp.dot(probs, kv_ref[1, :, cols], preferred_element_type=F32)
                key += keys
            attended = (weighted / total).astype(BF16)
            for index in range(at, at + tile_blocks):
                place = slice(index % per_out * rows, (index % per_out + 1) * rows)
                block = attended[(index - at) * rows : (index - at + 1) * rows]
                out_refs[index // per_out][place, cols] = block


def attend(plan, queries, kvs, name):
    rows = queries[0].shape[1]
    count = len(queries)
    keys = sum(kv.shape[1] for kv in kvs)
    tile_blocks = math.gcd(count, max(256 // rows, 1))
    vmem = pl.BlockSpec(memory_space=pltpu.VMEM)
    return list(
        pl.pallas_call(
            functools.partial(attend_kernel, count, len(kvs), plan.heads, tile_blocks),
            out_shape=[jax.ShapeDtypeStruct((count // plan.G * rows, plan.cols), BF16)] * plan.G,
            in_specs=[vmem] * (count + len(kvs)),
            out_specs=[vmem] * plan.G,
            scratch_shapes=[pltpu.VMEM((2, tile_blocks * rows, keys), F32)],
            compiler_params=pltpu.CompilerParams(vmem_limit_bytes=20 * MIB),
            cost_estimate=pl.CostEstimate(
                flops=4 * count * rows * keys * plan.cols,
                bytes_accessed=4 * plan.cols * (count * rows + keys),
                transcendentals=count * rows * keys * plan.heads,
            ),
            name=name,
        )(*queries, *kvs)
    )


def project_kernel(plan, weight_count, first, where_ref, *refs):
    parts, w_refs, (out_ref, mixed) = (
        refs[: plan.G],
        refs[plan.G : plan.G + weight_count],
        refs[plan.G + weight_count :],
    )
    own_g = where_ref[0] // (plan.R * plan.T)
    for dg, part in enumerate(parts):
        place = lax.rem(own_g + dg, plan.G) * plan.cols
        mixed[:, pl.ds(pl.multiple_of(place, HD), plan.cols)] = part[...]
    total = None
    depth = 0
    for w_ref in w_refs:
        share = jnp.dot(
            mixed[:, depth : depth + w_ref.shape[0]],
            w_ref[:, first : first + out_ref.shape[1]],
            preferred_element_type=F32,
        )
        total = share if total is None else total + share
        depth += w_ref.shape[0]
    out_ref[...] = total.astype(BF16)


def project(plan, parts, weights, first, count, flops, name):
    rows = parts[0].shape[0]
    depth = sum(w.shape[0] for w in weights)
    vmem = pl.BlockSpec(memory_space=pltpu.VMEM)
    return pl.pallas_call(
        functools.partial(project_kernel, plan, len(weights), first),
        out_shape=jax.ShapeDtypeStruct((rows, count), BF16),
        in_specs=[pl.BlockSpec(memory_space=pltpu.SMEM)] + [vmem] * (len(parts) + len(weights)),
        out_specs=vmem,
        scratch_shapes=[pltpu.VMEM((rows, depth), BF16)],
        compiler_params=pltpu.CompilerParams(vmem_limit_bytes=20 * MIB),
        cost_estimate=pl.CostEstimate(flops=flops, bytes_accessed=flops // 64, transcendentals=0),
        name=name,
    )(plan.where, *parts, *weights)


def add_kernel(first, continued, kept_ref, *refs):
    pieces = refs[continued:-3]
    out_ref, held, sem = refs[-3:]
    cols = pl.ds(first, held.shape[1])
    total = kept_ref[:, cols].astype(F32)
    for piece in pieces:
        total += piece[...].astype(F32)
    held[...] = total.astype(BF16)
    copy = pltpu.make_async_copy(held, out_ref.at[:, cols], sem)
    copy.start()
    copy.wait()


def add_up(kept, pieces, first, out):
    vmem = pl.BlockSpec(memory_space=pltpu.VMEM)
    hbm = pl.BlockSpec(memory_space=pl.ANY)
    continued = out is not None
    return pl.pallas_call(
        functools.partial(add_kernel, first, continued),
        out_shape=jax.ShapeDtypeStruct(kept.shape, BF16),
        in_specs=[vmem] + [hbm] * continued + [vmem] * len(pieces),
        out_specs=hbm,
        scratch_shapes=[pltpu.VMEM(pieces[0].shape, BF16), pltpu.SemaphoreType.DMA],
        input_output_aliases={1: 0} if continued else {},
        compiler_params=pltpu.CompilerParams(vmem_limit_bytes=20 * MIB),
        cost_estimate=pl.CostEstimate(flops=0, bytes_accessed=0, transcendentals=0),
        name="add_shares",
    )(kept, *([out] * continued), *pieces)


def local(query_vectors, key_vectors, value_vectors, out_weight):
    plan = Plan(query_vectors.shape[1] // HD)
    G, R, T = plan.G, plan.R, plan.T
    rows = query_vectors.shape[0]

    first = [(0, dt) for dt in range(T)]
    straight = [(dg, 0) for dg in range(1, G)]
    crossed = [(dg, dt) for dg in range(1, G) for dt in range(1, T)]
    whole, pair = (0, 1, 2), (0, 1)
    pieces = [(shift, whole) for shift in first] + [(shift, pair) for shift in straight]
    pieces += [(shift, whole) for shift in crossed] + [(shift, (2,)) for shift in straight]
    packed = pack(plan, pieces, key_vectors, value_vectors, query_vectors)
    blocks = {shift: packed[shift, slots] for shift, slots in pieces if len(slots) > 1}
    late = {shift: packed[shift, (2,)] for shift in straight}

    def spread(shift):
        return blocks[shift] if shift == (0, 0) else plan.move(blocks[shift], *shift)

    wide = R % 2 == 0 and R <= 8

    def across(own):
        shifts = range(1, R // 2 if wide else 1)
        return [own] + [plan.move(own, r_map=lambda r, s=s: (r + 2 * s) % R) for s in shifts]

    def exchange(pieces):
        pieces = join(pieces)
        if wide:
            return [pieces, plan.move(pieces, r_map=lambda r: r ^ 1)]
        groups = [[g * R + r for r in range(R)] for g in range(G)]
        return [lax.all_gather(pieces, "ctx", axis=1, tiled=True, axis_index_groups=groups)]

    depth = out_weight.shape[0]
    cuts = [0, depth // 6, depth // 2, depth]
    arrived = {shift: spread(shift) for shift in first + straight}
    gathered = [across(jnp.concatenate([arrived[shift][:2] for shift in first], axis=1))]
    weight, weights = out_weight, []
    if crossed:
        for index, shift in enumerate(crossed):
            before = first[-1] if index == 0 else straight[0]
            arrived[before], blocks[shift] = lax.optimization_barrier(
                (arrived[before], blocks[shift])
            )
        arrived.update({shift: spread(shift) for shift in crossed})
        own = jnp.concatenate([arrived[shift][:2] for shift in straight], axis=1)
        gathered[0], own, weight = lax.optimization_barrier((gathered[0], own, weight))
        gathered.append(across(own))
        weights.append(fetch(weight, 0, cuts[1]))
        last, weights[0] = lax.optimization_barrier(
            ([arrived[shift] for shift in crossed], weights[0])
        )
        arrived.update(zip(crossed, last))
        own, weight, late = lax.optimization_barrier((join(last, split=True), weight, late))
        blocks.update(late)
        arrived.update({shift: spread(shift) for shift in straight})
        gathered.append(list(zip(*map(across, own))))
        weights.append(fetch(weight, cuts[1], cuts[2] - cuts[1]))
    else:
        weights.append(fetch(weight, 0, cuts[2]))
    others = [arrived[dg, dt] for dg in range(G) for dt in range(1, T)]
    kept = [arrived[dg, 0] for dg in range(G)]
    gathered, others, kept, weights, weight = lax.optimization_barrier(
        (gathered, others, kept, weights, weight)
    )
    halves = [gathered[:2], gathered[2:]] if len(gathered) > 2 else [gathered]
    kvs = [kv for pieces in halves for kv in exchange(sum(pieces, []))]

    weights = list(weights) + [fetch(weight, cuts[2], depth - cuts[2])]
    others, weights[-1] = lax.optimization_barrier((others, weights[-1]))

    def give_back(attended):
        parts = {0: attended[0]}
        for dg in sorted(range(1, G), key=lambda dg: -min(dg, G - dg)):
            parts[dg] = plan.move(attended[dg], -dg)
        return [parts[dg] for dg in range(G)]

    others = attend(plan, others, kvs, "attend_others")
    kept, others[0] = lax.optimization_barrier((kept, others[0]))
    kept = attend(plan, kept, kvs, "attend_own")
    parts = give_back(others)
    parts, kept = lax.optimization_barrier((parts, kept))
    width = out_weight.shape[1]
    edges = [0, width // 5 * 3, width]
    received = []
    for start, end in zip(edges, edges[1:]):
        flops = 2 * (T - 1) * rows * depth * (end - start)
        share = project(plan, parts, weights, start, end - start, flops, "project_others")
        received.append(
            [plan.move(share[(dt - 1) * rows : dt * rows], 0, -dt) for dt in range(1, T)]
        )
        parts, kept, _ = lax.optimization_barrier((parts, kept, share))
    kept = project(plan, give_back(kept), weights, 0, width, 0, "project_own")
    out = None
    for start, pieces in zip(edges, received):
        out = add_up(kept, pieces, start, out)
    return out


def solution(mesh):
    spec = P(AXES, None)
    return jax.shard_map(
        local,
        mesh=mesh,
        in_specs=(spec, spec, spec, P("tp", None)),
        out_specs=spec,
        check_vma=False,
    )
```

```python
import functools
import math

import jax
import jax.numpy as jnp
from jax import lax
from jax.experimental import pallas as pl
from jax.experimental.pallas import tpu as pltpu
from jax.sharding import PartitionSpec as P

HD = 128
AXES = ("ctx", "tp")
MIB = 1024 * 1024
F32 = jnp.float32
BF16 = jnp.bfloat16


class Plan:
    def __init__(self, head_count):
        self.C = lax.axis_size("ctx")
        self.T = lax.axis_size("tp")
        self.G = math.gcd(head_count // self.T, self.C)
        self.R = self.C // self.G
        self.heads = head_count // (self.T * self.G)
        self.cols = self.heads * HD
        self.where = jnp.reshape(lax.axis_index(AXES), (1,)).astype(jnp.int32)

    def flat(self, g, r, t):
        return (g % self.G * self.R + r) * self.T + t % self.T

    def move(self, x, dg=0, dt=0, r_map=lambda r: r):
        pairs = [
            (self.flat(g, r, t), self.flat(g + dg, r_map(r), t + dt))
            for g in range(self.G)
            for r in range(self.R)
            for t in range(self.T)
        ]
        return lax.ppermute(x, AXES, pairs)


def pack_kernel(plan, pieces, where_ref, k_ref, v_ref, q_ref, *refs):
    outs, held, in_sem, out_sem = refs[:-3], *refs[-3:]
    G, R, T, cols = plan.G, plan.R, plan.T, plan.cols
    g, t = where_ref[0] // (R * T), lax.rem(where_ref[0], T)
    in_refs = (k_ref, v_ref, q_ref)
    groups = []
    place = 0
    for (dg, dt), slots in pieces:
        start = (lax.rem(t + dt, T) * G + lax.rem(g + dg, G)) * cols
        columns = pl.ds(pl.multiple_of(start, HD), cols)
        groups.append([])
        for slot in slots:
            copy = pltpu.make_async_copy(
                in_refs[slot].at[:, columns], held.at[place], in_sem.at[place]
            )
            copy.start()
            groups[-1].append(copy)
            place += 1
    outward = []
    place = 0
    for group, out_ref in zip(groups, outs):
        for copy in group:
            copy.wait()
        source = held.at[pl.ds(place, len(group))]
        outward.append(pltpu.make_async_copy(source, out_ref, out_sem.at[len(outward)]))
        outward[-1].start()
        place += len(group)
    for copy in outward:
        copy.wait()


def pack(plan, pieces, k, v, q):
    rows = q.shape[0]
    total = sum(len(slots) for shift, slots in pieces)
    outs = pl.pallas_call(
        functools.partial(pack_kernel, plan, pieces),
        out_shape=[
            jax.ShapeDtypeStruct((len(slots), rows, plan.cols), BF16) for shift, slots in pieces
        ],
        in_specs=[pl.BlockSpec(memory_space=pltpu.SMEM)] + [pl.BlockSpec(memory_space=pl.ANY)] * 3,
        out_specs=[pl.BlockSpec(memory_space=pl.ANY)] * len(pieces),
        scratch_shapes=[
            pltpu.VMEM((total, rows, plan.cols), BF16),
            pltpu.SemaphoreType.DMA((total,)),
            pltpu.SemaphoreType.DMA((len(pieces),)),
        ],
        compiler_params=pltpu.CompilerParams(vmem_limit_bytes=60 * MIB),
        name="pack",
    )(plan.where, k, v, q)
    return dict(zip(pieces, outs))


def join_kernel(slots, *refs):
    outs = refs[len(slots) :]
    places = [0, 0]
    for in_ref, (slot, index) in zip(refs, slots):
        rows = pl.ds(places[slot], in_ref.shape[1])
        out_ref, at = (outs[0], slot) if len(outs) == 1 else (outs[slot], 0)
        out_ref[at, rows, :] = in_ref[index]
        places[slot] += in_ref.shape[1]


def join(pieces, split=False):
    slots, arrays = [], []
    for piece in pieces:
        pair = piece if isinstance(piece, tuple) else (piece, piece)
        for slot, array in enumerate(pair):
            slots.append((slot, slot if array is piece else 0))
            arrays.append(array)
    rows = sum(array.shape[1] for array in arrays) // 2
    shape = jax.ShapeDtypeStruct((1 if split else 2, rows, arrays[0].shape[2]), BF16)
    vmem = pl.BlockSpec(memory_space=pltpu.VMEM)
    outs = pl.pallas_call(
        functools.partial(join_kernel, slots),
        out_shape=[shape] * (1 + split),
        in_specs=[vmem] * len(arrays),
        out_specs=[vmem] * (1 + split),
        compiler_params=pltpu.CompilerParams(vmem_limit_bytes=20 * MIB),
        cost_estimate=pl.CostEstimate(flops=0, bytes_accessed=0, transcendentals=0),
        name="join",
    )(*arrays)
    return tuple(outs) if split else outs[0]


def fetch_kernel(first, w_ref, out_ref, sem):
    depth = out_ref.shape[0] // sem.shape[0]
    copies = []
    for index in range(sem.shape[0]):
        copies.append(
            pltpu.make_async_copy(
                w_ref.at[pl.ds(first + index * depth, depth), :],
                out_ref.at[pl.ds(index * depth, depth), :],
                sem.at[index],
            )
        )
        copies[-1].start()
    for copy in copies:
        copy.wait()


def fetch(w, first, count):
    return pl.pallas_call(
        functools.partial(fetch_kernel, first),
        out_shape=jax.ShapeDtypeStruct((count, w.shape[1]), w.dtype),
        in_specs=[pl.BlockSpec(memory_space=pl.ANY)],
        out_specs=pl.BlockSpec(memory_space=pltpu.VMEM),
        scratch_shapes=[pltpu.SemaphoreType.DMA((2,))],
        compiler_params=pltpu.CompilerParams(vmem_limit_bytes=38 * MIB),
        cost_estimate=pl.CostEstimate(
            flops=0, bytes_accessed=4 * count * w.shape[1], transcendentals=0
        ),
        name="fetch_weight",
    )(w)


def attend_kernel(q_count, kv_count, heads, tile_blocks, *refs):
    q_refs, kv_refs = refs[:q_count], refs[q_count : q_count + kv_count]
    out_refs, scores = refs[q_count + kv_count : -1], refs[-1]
    scale = math.log2(math.e) / math.sqrt(HD)
    rows = q_refs[0].shape[1]
    per_out = q_count // len(out_refs)
    for head in range(heads):
        cols = slice(head * HD, (head + 1) * HD)
        for at in range(0, q_count, tile_blocks):
            q = jnp.concatenate(
                [ref[ref.shape[0] - 1, :, cols] for ref in q_refs[at : at + tile_blocks]], axis=0
            )
            peak = None
            key = 0
            for kv_ref in kv_refs:
                keys = kv_ref.shape[1]
                part = lax.dot_general(
                    q, kv_ref[0, :, cols], (((1,), (1,)), ((), ())), preferred_element_type=F32
                )
                scores[head % 2, :, pl.ds(key, keys)] = part
                top = jnp.max(part, axis=-1, keepdims=True)
                peak = top if peak is None else jnp.maximum(peak, top)
                key += keys
            peak = peak * scale
            weighted = jnp.zeros((q.shape[0], HD), F32)
            total = jnp.zeros((q.shape[0], 1), F32)
            key = 0
            for kv_ref in kv_refs:
                keys = kv_ref.shape[1]
                probs = jnp.exp2(scores[head % 2, :, pl.ds(key, keys)] * scale - peak).astype(BF16)
                total += jnp.sum(probs.astype(F32), axis=-1, keepdims=True)
                weighted += jnp.dot(probs, kv_ref[1, :, cols], preferred_element_type=F32)
                key += keys
            attended = (weighted / total).astype(BF16)
            for index in range(at, at + tile_blocks):
                place = slice(index % per_out * rows, (index % per_out + 1) * rows)
                block = attended[(index - at) * rows : (index - at + 1) * rows]
                out_refs[index // per_out][place, cols] = block


def attend(plan, queries, kvs, name):
    rows = queries[0].shape[1]
    count = len(queries)
    keys = sum(kv.shape[1] for kv in kvs)
    tile_blocks = math.gcd(count, max(256 // rows, 1))
    vmem = pl.BlockSpec(memory_space=pltpu.VMEM)
    return list(
        pl.pallas_call(
            functools.partial(attend_kernel, count, len(kvs), plan.heads, tile_blocks),
            out_shape=[jax.ShapeDtypeStruct((count // plan.G * rows, plan.cols), BF16)] * plan.G,
            in_specs=[vmem] * (count + len(kvs)),
            out_specs=[vmem] * plan.G,
            scratch_shapes=[pltpu.VMEM((2, tile_blocks * rows, keys), F32)],
            compiler_params=pltpu.CompilerParams(vmem_limit_bytes=20 * MIB),
            cost_estimate=pl.CostEstimate(
                flops=4 * count * rows * keys * plan.cols,
                bytes_accessed=4 * plan.cols * (count * rows + keys),
                transcendentals=count * rows * keys * plan.heads,
            ),
            name=name,
        )(*queries, *kvs)
    )


def project_kernel(plan, weight_count, first, where_ref, *refs):
    parts, w_refs, (out_ref, mixed) = (
        refs[: plan.G],
        refs[plan.G : plan.G + weight_count],
        refs[plan.G + weight_count :],
    )
    own_g = where_ref[0] // (plan.R * plan.T)
    for dg, part in enumerate(parts):
        place = lax.rem(own_g + dg, plan.G) * plan.cols
        mixed[:, pl.ds(pl.multiple_of(place, HD), plan.cols)] = part[...]
    total = None
    depth = 0
    for w_ref in w_refs:
        share = jnp.dot(
            mixed[:, depth : depth + w_ref.shape[0]],
            w_ref[:, first : first + out_ref.shape[1]],
            preferred_element_type=F32,
        )
        total = share if total is None else total + share
        depth += w_ref.shape[0]
    out_ref[...] = total.astype(BF16)


def project(plan, parts, weights, first, count, flops, name):
    rows = parts[0].shape[0]
    depth = sum(w.shape[0] for w in weights)
    vmem = pl.BlockSpec(memory_space=pltpu.VMEM)
    return pl.pallas_call(
        functools.partial(project_kernel, plan, len(weights), first),
        out_shape=jax.ShapeDtypeStruct((rows, count), BF16),
        in_specs=[pl.BlockSpec(memory_space=pltpu.SMEM)] + [vmem] * (len(parts) + len(weights)),
        out_specs=vmem,
        scratch_shapes=[pltpu.VMEM((rows, depth), BF16)],
        compiler_params=pltpu.CompilerParams(vmem_limit_bytes=20 * MIB),
        cost_estimate=pl.CostEstimate(flops=flops, bytes_accessed=flops // 64, transcendentals=0),
        name=name,
    )(plan.where, *parts, *weights)


def add_kernel(first, continued, kept_ref, *refs):
    pieces = refs[continued:-3]
    out_ref, held, sem = refs[-3:]
    cols = pl.ds(first, held.shape[1])
    total = kept_ref[:, cols].astype(F32)
    for piece in pieces:
        total += piece[...].astype(F32)
    held[...] = total.astype(BF16)
    copy = pltpu.make_async_copy(held, out_ref.at[:, cols], sem)
    copy.start()
    copy.wait()


def add_up(kept, pieces, first, out):
    vmem = pl.BlockSpec(memory_space=pltpu.VMEM)
    hbm = pl.BlockSpec(memory_space=pl.ANY)
    continued = out is not None
    return pl.pallas_call(
        functools.partial(add_kernel, first, continued),
        out_shape=jax.ShapeDtypeStruct(kept.shape, BF16),
        in_specs=[vmem] + [hbm] * continued + [vmem] * len(pieces),
        out_specs=hbm,
        scratch_shapes=[pltpu.VMEM(pieces[0].shape, BF16), pltpu.SemaphoreType.DMA],
        input_output_aliases={1: 0} if continued else {},
        compiler_params=pltpu.CompilerParams(vmem_limit_bytes=20 * MIB),
        cost_estimate=pl.CostEstimate(flops=0, bytes_accessed=0, transcendentals=0),
        name="add_shares",
    )(kept, *([out] * continued), *pieces)


def local(query_vectors, key_vectors, value_vectors, out_weight):
    plan = Plan(query_vectors.shape[1] // HD)
    G, R, T = plan.G, plan.R, plan.T
    rows = query_vectors.shape[0]

    first = [(0, dt) for dt in range(T)]
    straight = [(dg, 0) for dg in range(1, G)]
    crossed = [(dg, dt) for dg in range(1, G) for dt in range(1, T)]
    whole, pair = (0, 1, 2), (0, 1)
    pieces = [(shift, whole) for shift in first] + [(shift, pair) for shift in straight]
    pieces += [(shift, whole) for shift in crossed] + [(shift, (2,)) for shift in straight]
    packed = pack(plan, pieces, key_vectors, value_vectors, query_vectors)
    blocks = {shift: packed[shift, slots] for shift, slots in pieces if len(slots) > 1}
    late = {shift: packed[shift, (2,)] for shift in straight}

    def spread(shift):
        return blocks[shift] if shift == (0, 0) else plan.move(blocks[shift], *shift)

    wide = R % 2 == 0 and R <= 8

    def across(own):
        shifts = range(1, R // 2 if wide else 1)
        return [own] + [plan.move(own, r_map=lambda r, s=s: (r + 2 * s) % R) for s in shifts]

    def exchange(pieces):
        pieces = join(pieces)
        if wide:
            return [pieces, plan.move(pieces, r_map=lambda r: r ^ 1)]
        groups = [[g * R + r for r in range(R)] for g in range(G)]
        return [lax.all_gather(pieces, "ctx", axis=1, tiled=True, axis_index_groups=groups)]

    depth = out_weight.shape[0]
    cuts = [0, depth // 6, depth // 2, depth]
    arrived = {shift: spread(shift) for shift in first + straight}
    gathered = [across(jnp.concatenate([arrived[shift][:2] for shift in first], axis=1))]
    weight, weights = out_weight, []
    if crossed:
        for index, shift in enumerate(crossed):
            before = first[-1] if index == 0 else straight[0]
            arrived[before], blocks[shift] = lax.optimization_barrier(
                (arrived[before], blocks[shift])
            )
        arrived.update({shift: spread(shift) for shift in crossed})
        own = jnp.concatenate([arrived[shift][:2] for shift in straight], axis=1)
        gathered[0], own, weight = lax.optimization_barrier((gathered[0], own, weight))
        gathered.append(across(own))
        weights.append(fetch(weight, 0, cuts[1]))
        last, weights[0] = lax.optimization_barrier(
            ([arrived[shift] for shift in crossed], weights[0])
        )
        arrived.update(zip(crossed, last))
        own, weight, late = lax.optimization_barrier((join(last, split=True), weight, late))
        blocks.update(late)
        arrived.update({shift: spread(shift) for shift in straight})
        gathered.append(list(zip(*map(across, own))))
    else:
        weights.append(fetch(weight, 0, cuts[2]))
    others = [arrived[dg, dt] for dg in range(G) for dt in range(1, T)]
    kept = [arrived[dg, 0] for dg in range(G)]
    gathered, others, kept, weights, weight = lax.optimization_barrier(
        (gathered, others, kept, weights, weight)
    )
    halves = [gathered[:2], gathered[2:]] if len(gathered) > 2 else [gathered]
    kvs = [kv for pieces in halves for kv in exchange(sum(pieces, []))]

    weights = list(weights) + [fetch(weight, cuts[2], depth - cuts[2])]
    others, weights[-1] = lax.optimization_barrier((others, weights[-1]))

    def give_back(attended):
        parts = {0: attended[0]}
        for dg in sorted(range(1, G), key=lambda dg: -min(dg, G - dg)):
            parts[dg] = plan.move(attended[dg], -dg)
        return [parts[dg] for dg in range(G)]

    others = attend(plan, others, kvs, "attend_others")
    kept, others[0], weight = lax.optimization_barrier((kept, others[0], weight))
    if crossed:
        weights.insert(1, fetch(weight, cuts[1], cuts[2] - cuts[1]))
    kept = attend(plan, kept, kvs, "attend_own")
    parts = give_back(others)
    parts, kept, weights = lax.optimization_barrier((parts, kept, weights))
    width = out_weight.shape[1]
    edges = [0, width // 5 * 3, width]
    received = []
    for start, end in zip(edges, edges[1:]):
        flops = 2 * (T - 1) * rows * depth * (end - start)
        share = project(plan, parts, weights, start, end - start, flops, "project_others")
        received.append(
            [plan.move(share[(dt - 1) * rows : dt * rows], 0, -dt) for dt in range(1, T)]
        )
        parts, kept, _ = lax.optimization_barrier((parts, kept, share))
    kept = project(plan, give_back(kept), weights, 0, width, 0, "project_own")
    out = None
    for start, pieces in zip(edges, received):
        out = add_up(kept, pieces, start, out)
    return out


def solution(mesh):
    spec = P(AXES, None)
    return jax.shard_map(
        local,
        mesh=mesh,
        in_specs=(spec, spec, spec, P("tp", None)),
        out_specs=spec,
        check_vma=False,
    )
```

```python
import functools
import math

import jax
import jax.numpy as jnp
from jax import lax
from jax.experimental import pallas as pl
from jax.experimental.pallas import tpu as pltpu
from jax.sharding import PartitionSpec as P

HD = 128
AXES = ("ctx", "tp")
MIB = 1024 * 1024
F32 = jnp.float32
BF16 = jnp.bfloat16


class Plan:
    def __init__(self, head_count):
        self.C = lax.axis_size("ctx")
        self.T = lax.axis_size("tp")
        self.G = math.gcd(head_count // self.T, self.C)
        self.R = self.C // self.G
        self.heads = head_count // (self.T * self.G)
        self.cols = self.heads * HD
        self.where = jnp.reshape(lax.axis_index(AXES), (1,)).astype(jnp.int32)

    def flat(self, g, r, t):
        return (g % self.G * self.R + r) * self.T + t % self.T

    def move(self, x, dg=0, dt=0, r_map=lambda r: r):
        pairs = [
            (self.flat(g, r, t), self.flat(g + dg, r_map(r), t + dt))
            for g in range(self.G)
            for r in range(self.R)
            for t in range(self.T)
        ]
        return lax.ppermute(x, AXES, pairs)


def pack_kernel(plan, shifts, where_ref, *refs):
    in_refs, outs, (held, in_sem, out_sem) = refs[:3], refs[3:-3], refs[-3:]
    G, R, T, cols = plan.G, plan.R, plan.T, plan.cols
    g, t = where_ref[0] // (R * T), lax.rem(where_ref[0], T)
    inward, outward = [], []
    for index, (dg, dt) in enumerate(shifts):
        start = (lax.rem(t + dt, T) * G + lax.rem(g + dg, G)) * cols
        columns = pl.ds(pl.multiple_of(start, HD), cols)
        for slot, in_ref in enumerate(in_refs):
            inward.append(
                pltpu.make_async_copy(
                    in_ref.at[:, columns], held.at[index, slot], in_sem.at[index, slot]
                )
            )
            inward[-1].start()
    for index, out_ref in enumerate(outs):
        for copy in inward[3 * index : 3 * index + 3]:
            copy.wait()
        outward.append(pltpu.make_async_copy(held.at[index], out_ref, out_sem.at[index]))
        outward[-1].start()
    for copy in outward:
        copy.wait()


def pack(plan, shifts, k, v, q):
    count = len(shifts)
    block = (3, q.shape[0], plan.cols)
    outs = pl.pallas_call(
        functools.partial(pack_kernel, plan, shifts),
        out_shape=[jax.ShapeDtypeStruct(block, BF16)] * count,
        in_specs=[pl.BlockSpec(memory_space=pltpu.SMEM)] + [pl.BlockSpec(memory_space=pl.ANY)] * 3,
        out_specs=[pl.BlockSpec(memory_space=pl.ANY)] * count,
        scratch_shapes=[
            pltpu.VMEM((count, *block), BF16),
            pltpu.SemaphoreType.DMA((count, 3)),
            pltpu.SemaphoreType.DMA((count,)),
        ],
        compiler_params=pltpu.CompilerParams(vmem_limit_bytes=60 * MIB),
        name="pack",
    )(plan.where, k, v, q)
    return dict(zip(shifts, outs))


def join_kernel(slots, *refs):
    outs = refs[len(slots) :]
    places = [0, 0]
    for in_ref, (slot, index) in zip(refs, slots):
        rows = pl.ds(places[slot], in_ref.shape[1])
        out_ref, at = (outs[0], slot) if len(outs) == 1 else (outs[slot], 0)
        out_ref[at, rows, :] = in_ref[index]
        places[slot] += in_ref.shape[1]


def join(pieces, split=False):
    slots, arrays = [], []
    for piece in pieces:
        pair = piece if isinstance(piece, tuple) else (piece, piece)
        for slot, array in enumerate(pair):
            slots.append((slot, slot if array is piece else 0))
            arrays.append(array)
    rows = sum(array.shape[1] for array in arrays) // 2
    shape = jax.ShapeDtypeStruct((1 if split else 2, rows, arrays[0].shape[2]), BF16)
    vmem = pl.BlockSpec(memory_space=pltpu.VMEM)
    outs = pl.pallas_call(
        functools.partial(join_kernel, slots),
        out_shape=[shape] * (1 + split),
        in_specs=[vmem] * len(arrays),
        out_specs=[vmem] * (1 + split),
        compiler_params=pltpu.CompilerParams(vmem_limit_bytes=20 * MIB),
        cost_estimate=pl.CostEstimate(flops=0, bytes_accessed=0, transcendentals=0),
        name="join",
    )(*arrays)
    return tuple(outs) if split else outs[0]


def fetch_kernel(first, w_ref, out_ref, sem):
    depth = out_ref.shape[0] // sem.shape[0]
    copies = []
    for index in range(sem.shape[0]):
        copies.append(
            pltpu.make_async_copy(
                w_ref.at[pl.ds(first + index * depth, depth), :],
                out_ref.at[pl.ds(index * depth, depth), :],
                sem.at[index],
            )
        )
        copies[-1].start()
    for copy in copies:
        copy.wait()


def fetch(w, first, count):
    return pl.pallas_call(
        functools.partial(fetch_kernel, first),
        out_shape=jax.ShapeDtypeStruct((count, w.shape[1]), w.dtype),
        in_specs=[pl.BlockSpec(memory_space=pl.ANY)],
        out_specs=pl.BlockSpec(memory_space=pltpu.VMEM),
        scratch_shapes=[pltpu.SemaphoreType.DMA((2,))],
        compiler_params=pltpu.CompilerParams(vmem_limit_bytes=38 * MIB),
        cost_estimate=pl.CostEstimate(
            flops=0, bytes_accessed=4 * count * w.shape[1], transcendentals=0
        ),
        name="fetch_weight",
    )(w)


def attend_kernel(q_count, kv_count, heads, tile_blocks, *refs):
    q_refs, kv_refs = refs[:q_count], refs[q_count : q_count + kv_count]
    out_refs, scores = refs[q_count + kv_count : -1], refs[-1]
    scale = math.log2(math.e) / math.sqrt(HD)
    rows = q_refs[0].shape[1]
    per_out = q_count // len(out_refs)
    for head in range(heads):
        cols = slice(head * HD, (head + 1) * HD)
        for at in range(0, q_count, tile_blocks):
            q = jnp.concatenate(
                [ref[ref.shape[0] - 1, :, cols] for ref in q_refs[at : at + tile_blocks]], axis=0
            )
            peak = None
            key = 0
            for kv_ref in kv_refs:
                keys = kv_ref.shape[1]
                part = lax.dot_general(
                    q, kv_ref[0, :, cols], (((1,), (1,)), ((), ())), preferred_element_type=F32
                )
                scores[head % 2, :, pl.ds(key, keys)] = part
                top = jnp.max(part, axis=-1, keepdims=True)
                peak = top if peak is None else jnp.maximum(peak, top)
                key += keys
            peak = peak * scale
            weighted = jnp.zeros((q.shape[0], HD), F32)
            total = jnp.zeros((q.shape[0], 1), F32)
            key = 0
            for kv_ref in kv_refs:
                keys = kv_ref.shape[1]
                probs = jnp.exp2(scores[head % 2, :, pl.ds(key, keys)] * scale - peak).astype(BF16)
                total += jnp.sum(probs.astype(F32), axis=-1, keepdims=True)
                weighted += jnp.dot(probs, kv_ref[1, :, cols], preferred_element_type=F32)
                key += keys
            attended = (weighted / total).astype(BF16)
            for index in range(at, at + tile_blocks):
                place = slice(index % per_out * rows, (index % per_out + 1) * rows)
                block = attended[(index - at) * rows : (index - at + 1) * rows]
                out_refs[index // per_out][place, cols] = block


def attend(plan, queries, kvs, name):
    rows = queries[0].shape[1]
    count = len(queries)
    keys = sum(kv.shape[1] for kv in kvs)
    tile_blocks = math.gcd(count, max(256 // rows, 1))
    vmem = pl.BlockSpec(memory_space=pltpu.VMEM)
    return list(
        pl.pallas_call(
            functools.partial(attend_kernel, count, len(kvs), plan.heads, tile_blocks),
            out_shape=[jax.ShapeDtypeStruct((count // plan.G * rows, plan.cols), BF16)] * plan.G,
            in_specs=[vmem] * (count + len(kvs)),
            out_specs=[vmem] * plan.G,
            scratch_shapes=[pltpu.VMEM((2, tile_blocks * rows, keys), F32)],
            compiler_params=pltpu.CompilerParams(vmem_limit_bytes=20 * MIB),
            cost_estimate=pl.CostEstimate(
                flops=4 * count * rows * keys * plan.cols,
                bytes_accessed=4 * plan.cols * (count * rows + keys),
                transcendentals=count * rows * keys * plan.heads,
            ),
            name=name,
        )(*queries, *kvs)
    )


def project_kernel(plan, weight_count, first, where_ref, *refs):
    parts, w_refs, (out_ref, mixed) = (
        refs[: plan.G],
        refs[plan.G : plan.G + weight_count],
        refs[plan.G + weight_count :],
    )
    own_g = where_ref[0] // (plan.R * plan.T)
    for dg, part in enumerate(parts):
        place = lax.rem(own_g + dg, plan.G) * plan.cols
        mixed[:, pl.ds(pl.multiple_of(place, HD), plan.cols)] = part[...]
    total = None
    depth = 0
    for w_ref in w_refs:
        share = jnp.dot(
            mixed[:, depth : depth + w_ref.shape[0]],
            w_ref[:, first : first + out_ref.shape[1]],
            preferred_element_type=F32,
        )
        total = share if total is None else total + share
        depth += w_ref.shape[0]
    out_ref[...] = total.astype(BF16)


def project(plan, parts, weights, first, count, flops, name):
    rows = parts[0].shape[0]
    depth = sum(w.shape[0] for w in weights)
    vmem = pl.BlockSpec(memory_space=pltpu.VMEM)
    return pl.pallas_call(
        functools.partial(project_kernel, plan, len(weights), first),
        out_shape=jax.ShapeDtypeStruct((rows, count), BF16),
        in_specs=[pl.BlockSpec(memory_space=pltpu.SMEM)] + [vmem] * (len(parts) + len(weights)),
        out_specs=vmem,
        scratch_shapes=[pltpu.VMEM((rows, depth), BF16)],
        compiler_params=pltpu.CompilerParams(vmem_limit_bytes=20 * MIB),
        cost_estimate=pl.CostEstimate(flops=flops, bytes_accessed=flops // 64, transcendentals=0),
        name=name,
    )(plan.where, *parts, *weights)


def add_kernel(first, continued, kept_ref, *refs):
    pieces = refs[continued:-3]
    out_ref, held, sem = refs[-3:]
    cols = pl.ds(first, held.shape[1])
    total = kept_ref[:, cols].astype(F32)
    for piece in pieces:
        total += piece[...].astype(F32)
    held[...] = total.astype(BF16)
    copy = pltpu.make_async_copy(held, out_ref.at[:, cols], sem)
    copy.start()
    copy.wait()


def add_up(kept, pieces, first, out):
    vmem = pl.BlockSpec(memory_space=pltpu.VMEM)
    hbm = pl.BlockSpec(memory_space=pl.ANY)
    continued = out is not None
    return pl.pallas_call(
        functools.partial(add_kernel, first, continued),
        out_shape=jax.ShapeDtypeStruct(kept.shape, BF16),
        in_specs=[vmem] + [hbm] * continued + [vmem] * len(pieces),
        out_specs=hbm,
        scratch_shapes=[pltpu.VMEM(pieces[0].shape, BF16), pltpu.SemaphoreType.DMA],
        input_output_aliases={1: 0} if continued else {},
        compiler_params=pltpu.CompilerParams(vmem_limit_bytes=20 * MIB),
        cost_estimate=pl.CostEstimate(flops=0, bytes_accessed=0, transcendentals=0),
        name="add_shares",
    )(kept, *([out] * continued), *pieces)


def local(query_vectors, key_vectors, value_vectors, out_weight):
    plan = Plan(query_vectors.shape[1] // HD)
    G, R, T = plan.G, plan.R, plan.T
    rows = query_vectors.shape[0]

    first = [(0, dt) for dt in range(T)]
    straight = [(dg, 0) for dg in range(1, G)]
    crossed = [(dg, dt) for dg in range(1, G) for dt in range(1, T)]
    blocks = pack(
        plan, first + straight + crossed, key_vectors, value_vectors, query_vectors
    )

    def spread(shift):
        return blocks[shift] if shift == (0, 0) else plan.move(blocks[shift], *shift)

    wide = R % 2 == 0 and R <= 8

    def across(own):
        shifts = range(1, R // 2 if wide else 1)
        return [own] + [plan.move(own, r_map=lambda r, s=s: (r + 2 * s) % R) for s in shifts]

    def exchange(pieces):
        pieces = join(pieces)
        if wide:
            return [pieces, plan.move(pieces, r_map=lambda r: r ^ 1)]
        groups = [[g * R + r for r in range(R)] for g in range(G)]
        return [lax.all_gather(pieces, "ctx", axis=1, tiled=True, axis_index_groups=groups)]

    depth = out_weight.shape[0]
    cuts = [0, depth // 6, depth // 6 * 4, depth]
    arrived = {shift: spread(shift) for shift in first + straight}
    gathered = [across(jnp.concatenate([arrived[shift][:2] for shift in first], axis=1))]
    weight, weights = out_weight, []
    if crossed:
        for index, shift in enumerate(crossed):
            before = straight[index % 2 if G > 2 else 0]
            arrived[before], blocks[shift] = lax.optimization_barrier(
                (arrived[before], blocks[shift])
            )
        arrived.update({shift: spread(shift) for shift in crossed})
        own = jnp.concatenate([arrived[shift][:2] for shift in straight], axis=1)
        gathered[0], own, weight = lax.optimization_barrier((gathered[0], own, weight))
        gathered.append(across(own))
        weights.append(fetch(weight, 0, cuts[1]))
        last, weights[0] = lax.optimization_barrier(
            ([arrived[shift] for shift in crossed], weights[0])
        )
        arrived.update(zip(crossed, last))
        own, weight = lax.optimization_barrier((join(last, split=True), weight))
        gathered.append(list(zip(*map(across, own))))
        weights.append(fetch(weight, cuts[1], cuts[2] - cuts[1]))
    else:
        weights.append(fetch(weight, 0, cuts[2]))
    others = [arrived[dg, dt] for dg in range(G) for dt in range(1, T)]
    kept = [arrived[dg, 0] for dg in range(G)]
    gathered, others, kept, weights, weight = lax.optimization_barrier(
        (gathered, others, kept, weights, weight)
    )
    halves = [gathered[:2], gathered[2:]] if len(gathered) > 2 else [gathered]
    kvs = [kv for pieces in halves for kv in exchange(sum(pieces, []))]

    weights = list(weights) + [fetch(weight, cuts[2], depth - cuts[2])]
    others, weights[-1] = lax.optimization_barrier((others, weights[-1]))

    def give_back(attended):
        parts = {0: attended[0]}
        for dg in sorted(range(1, G), key=lambda dg: -min(dg, G - dg)):
            parts[dg] = plan.move(attended[dg], -dg)
        return [parts[dg] for dg in range(G)]

    others = attend(plan, others, kvs, "attend_others")
    kept, others[0] = lax.optimization_barrier((kept, others[0]))
    kept = attend(plan, kept, kvs, "attend_own")
    parts = give_back(others)
    parts, kept = lax.optimization_barrier((parts, kept))
    width = out_weight.shape[1]
    edges = [0, width // 5 * 3, width]
    received = []
    for start, end in zip(edges, edges[1:]):
        flops = 2 * (T - 1) * rows * depth * (end - start)
        share = project(plan, parts, weights, start, end - start, flops, "project_others")
        received.append(
            [plan.move(share[(dt - 1) * rows : dt * rows], 0, -dt) for dt in range(1, T)]
        )
        parts, kept, _ = lax.optimization_barrier((parts, kept, share))
    kept = project(plan, give_back(kept), weights, 0, width, 0, "project_own")
    out = None
    for start, pieces in zip(edges, received):
        out = add_up(kept, pieces, start, out)
    return out


def solution(mesh):
    spec = P(AXES, None)
    return jax.shard_map(
        local,
        mesh=mesh,
        in_specs=(spec, spec, spec, P("tp", None)),
        out_specs=spec,
        check_vma=False,
    )
```
